32 devices in a mesh: dp: 2 (over x), fsdp: 16 (over z, y, core).
Axes of the slice: x: 2, y: 2, z: 4, core: 2. Of those that a mesh axis runs over, the one named last changes fastest.
Arguments:
- tokens: bfloat16 [81920, 512], P(('dp', 'fsdp')), may hold values from -6 to 6
- positions: bfloat16 [64, 512], P(None, 'fsdp'), may hold values from -4 to 4
- norm_one_gain: bfloat16 [512], P('fsdp'), may hold values from 0.5 to 1.5
- norm_one_bias: bfloat16 [512], P('fsdp'), may hold values from -1 to 1
- qkv_weight: bfloat16 [512, 1536], P('fsdp'), may hold values from -0.25 to 0.25
- out_weight: bfloat16 [512, 512], P('fsdp'), may hold values from -0.75 to 0.75
- norm_two_gain: bfloat16 [512], P('fsdp'), may hold values from 0.5 to 1.5
- norm_two_bias: bfloat16 [512], P('fsdp'), may hold values from -1 to 1
- up_weight: bfloat16 [512, 2048], P('fsdp'), may hold values from -0.25 to 0.25
- up_bias: bfloat16 [2048], P('fsdp'), may hold values from -1.5 to 1.5
- down_weight: bfloat16 [2048, 512], P('fsdp'), may hold values from -0.25 to 0.25
- down_bias: bfloat16 [512], P('fsdp'), may hold values from -1.5 to 1.5
- final_gain: bfloat16 [512], P('fsdp'), may hold values from 0.5 to 1.5
- final_bias: bfloat16 [512], P('fsdp'), may hold values from -1 to 1
- actor_weight: bfloat16 [512, 18], P('fsdp'), may hold values from -0.5 to 0.5
- actor_bias: bfloat16 [18], replicated, may hold values from -4 to 4
- actions: int32 [81920], P(('dp', 'fsdp')), may hold values from 0 to 17, as said below
- action_masks: int32 [81920, 18], P(('dp', 'fsdp')), may hold values from 0 to 1
- game_ids: int32 [1280], P(('dp', 'fsdp')), may hold values from 0 to 25
- returns: float32 [81920], P(('dp', 'fsdp')), may hold values from -8 to 8
- values: float32 [81920], P(('dp', 'fsdp')), may hold values from -6 to 6
- running: float32 [2, 26], replicated, may hold values from -2 to 5, as said below
- percentiles: float32 [2, 26], replicated, may hold values from -2 to 5, as said below
Outputs:
- actor_loss: float32 [], replicated
- statistics: float32 [2, 26], replicated
- tokens_grad: float32 [81920, 512], P(('dp', 'fsdp'))
- positions_grad: float32 [64, 512], P(None, 'fsdp')
- norm_one_gain_grad: float32 [512], P('fsdp')
- norm_one_bias_grad: float32 [512], P('fsdp')
- qkv_weight_grad: float32 [512, 1536], P('fsdp')
- out_weight_grad: float32 [512, 512], P('fsdp')
- norm_two_gain_grad: float32 [512], P('fsdp')
- norm_two_bias_grad: float32 [512], P('fsdp')
- up_weight_grad: float32 [512, 2048], P('fsdp')
- up_bias_grad: float32 [2048], P('fsdp')
- down_weight_grad: float32 [2048, 512], P('fsdp')
- down_bias_grad: float32 [512], P('fsdp')
- final_gain_grad: float32 [512], P('fsdp')
- final_bias_grad: float32 [512], P('fsdp')
- actor_weight_grad: float32 [512, 18], P('fsdp')
- actor_bias_grad: float32 [18], replicated
The draws below stay inside these ranges and needn't reach their ends.
Inputs may be any that keep to these rules, and one draw needn't show every extreme that they name: `actions`: each frame's taken action is allowed by its mask, and slot 0 is allowed in every frame. `running`: row 1 exceeds row 0 in every game. `percentiles`: row 1 exceeds row 0 in every game.
All inputs are finite; a program needn't handle non-finite values.
Results may differ from the reference program's by a relative error of at most 0.014.
Values may be sent and summed in bfloat16 or wider, within the bound.
A program may use at most 192 MiB of HBM per device.

```python
import math
import jax
import jax.numpy as jnp
from jax import lax

D = 512
HEADS = 8
HEAD = 64
FF = 2048
ACTIONS = 18
GAMES = 26
LENGTH = 64
GROUP = 128
SEQS = 1280
TOKENS = 81920


def choose_actions(key):
    picked = jax.random.randint(jax.random.fold_in(key, 11), (TOKENS,), 0, ACTIONS)
    coin_draws = jax.random.randint(jax.random.fold_in(key, 12), (TOKENS, ACTIONS), 0, 5)
    slot_ids = lax.broadcasted_iota(jnp.int32, (TOKENS, ACTIONS), 1)
    allowed = (coin_draws < 3) | (slot_ids == picked[:, None]) | (slot_ids == 0)
    return (picked.astype(jnp.int32), allowed.astype(jnp.int32))


def draw_actions(key, part):
    return choose_actions(key)[0]


def draw_action_masks(key, part):
    return choose_actions(key)[1]


def return_bounds(key):
    lower_end = jax.random.uniform(jax.random.fold_in(key, 1), (GAMES,), jnp.float32, -2.0, 1.0)
    width_log = jax.random.uniform(jax.random.fold_in(key, 2), (GAMES,), jnp.float32, math.log(0.3), math.log(4.0))
    return jnp.stack([lower_end, lower_end + jnp.exp(width_log)])


def draw_running(key, part):
    key = jax.random.fold_in(key, 3)
    return return_bounds(key)


def draw_percentiles(key, part):
    key = jax.random.fold_in(key, 4)
    return return_bounds(key)


def plant(array, stream_key, least, largest):
    dims = array.shape
    spot = [jax.random.randint(jax.random.fold_in(stream_key, axis), (), 0, dims[axis]) for axis in range(len(dims))]
    array = array.at[tuple(spot)].set(least)
    longest = dims.index(max(dims))
    spot[longest] = (spot[longest] + 1) % dims[longest]
    return array.at[tuple(spot)].set(largest)


def block_scale(key, dims, split, least, top_value):
    def one(dim, blocks):
        steps = jax.random.uniform(jax.random.fold_in(jax.random.fold_in(key, 6), dim), (blocks,), jnp.float32, least / len(split), top_value / len(split))
        return jnp.repeat(jnp.exp(steps), dims[dim] // blocks).reshape((-1,) + (1,) * (len(dims) - dim - 1))

    loudness = one(*split[0])
    for cut in split[1:]:
        loudness = loudness * one(*cut)
    return loudness


def scatter_about(rng, dims, deviation, most, cuts=(), kind=jnp.bfloat16):
    level = block_scale(rng, dims, cuts, -0.22, 0.18) if cuts else 1.0
    drawn = jax.random.normal(rng, dims, jnp.float32) * deviation * level
    return jnp.minimum(jnp.maximum(drawn, -most), most).astype(kind)


def setup_inputs(seed: int = 0) -> dict:
    keys = jax.random.split(jax.random.key(seed), 24)
    tokens = scatter_about(keys[0], (TOKENS, D), 1.0, 6.0, ((0, 32),))
    positions = scatter_about(keys[1], (LENGTH, D), 0.5, 4.0, ((1, 16),))
    norm_one_gain = jnp.clip(1.0 + 0.1 * jax.random.normal(keys[2], (D,), jnp.float32), 0.5, 1.5).astype(jnp.bfloat16)
    norm_one_bias = scatter_about(keys[3], (D,), 0.2, 1.0, ((0, 16),))
    qkv_weight = scatter_about(keys[4], (D, 3 * D), D ** -0.5, 0.25, ((0, 16),))
    out_weight = scatter_about(keys[5], (D, D), (D // 8) ** -0.5, 0.75, ((0, 16),))
    norm_two_gain = jnp.clip(1.0 + 0.1 * jax.random.normal(keys[6], (D,), jnp.float32), 0.5, 1.5).astype(jnp.bfloat16)
    norm_two_bias = scatter_about(keys[7], (D,), 0.2, 1.0, ((0, 16),))
    up_weight = scatter_about(keys[8], (D, FF), D ** -0.5, 0.25, ((0, 16),))
    up_bias = scatter_about(keys[9], (FF,), 0.3, 1.5, ((0, 16),))
    down_weight = scatter_about(keys[10], (FF, D), (FF // 4) ** -0.5, 0.25, ((0, 16),))
    down_bias = scatter_about(keys[11], (D,), 0.3, 1.5, ((0, 16),))
    final_gain = jnp.clip(1.0 + 0.1 * jax.random.normal(keys[12], (D,), jnp.float32), 0.5, 1.5).astype(jnp.bfloat16)
    final_bias = scatter_about(keys[13], (D,), 0.2, 1.0, ((0, 16),))
    actor_weight = scatter_about(keys[14], (D, ACTIONS), (D // 4) ** -0.5, 0.5, ((0, 16),))
    actor_bias = scatter_about(keys[15], (ACTIONS,), 1.0, 4.0)
    actions = draw_actions(jax.random.fold_in(keys[23], 71), 0)
    action_masks = draw_action_masks(jax.random.fold_in(keys[23], 71), 0)
    game_ids = plant(jax.random.randint(keys[18], (SEQS,), 0, GAMES), jax.random.fold_in(keys[18], 1), 0, GAMES - 1).astype(jnp.int32)
    returns = scatter_about(keys[19], (TOKENS,), 1.5, 8.0, ((0, 32),), jnp.float32)
    values = scatter_about(keys[20], (TOKENS,), 1.0, 6.0, ((0, 32),), jnp.float32)
    running = draw_running(jax.random.fold_in(keys[23], 71), 0)
    percentiles = draw_percentiles(jax.random.fold_in(keys[23], 71), 0)
    return dict(tokens=tokens, positions=positions, norm_one_gain=norm_one_gain, norm_one_bias=norm_one_bias, qkv_weight=qkv_weight, out_weight=out_weight, norm_two_gain=norm_two_gain, norm_two_bias=norm_two_bias, up_weight=up_weight, up_bias=up_bias, down_weight=down_weight, down_bias=down_bias, final_gain=final_gain, final_bias=final_bias, actor_weight=actor_weight, actor_bias=actor_bias, actions=actions, action_masks=action_masks, game_ids=game_ids, returns=returns, values=values, running=running, percentiles=percentiles)


MASKED = -1e+30
EPSILON = 1e-05
DECAY_RATE = 0.9
ENTROPY_WEIGHT = 0.1

@jax.custom_vjp
def low(v):
    return lax.optimization_barrier(v.astype(jnp.bfloat16)).astype(jnp.float32)

@jax.custom_vjp
def low_back(v):
    return v

def low_keep(v):
    return (low(v), None)

def low_pass(kept, grad):
    return (grad,)

def back_keep(v):
    return (v, None)

def back_low(kept, grad):
    return (low(grad),)
low.defvjp(low_keep, low_pass)
low_back.defvjp(back_keep, back_low)

def matmul(left, right):
    return jnp.dot(left, right, precision=lax.Precision.HIGHEST, preferred_element_type=jnp.float32)

def layer_norm(values, gain, offset):
    centred = values - lax.optimization_barrier(jnp.mean(values, -1, keepdims=True))
    spread = lax.optimization_barrier(jnp.mean(centred * centred, -1, keepdims=True))
    return centred * lax.rsqrt(spread + EPSILON) * gain + offset

def policy_loss(logits, action_masks, actions, advantage):
    allowed = action_masks > 0
    held = jnp.where(allowed, logits, MASKED)
    highest = lax.optimization_barrier(jnp.max(held, -1, keepdims=True))
    shifted = held - highest
    summed = lax.optimization_barrier(jnp.sum(jnp.exp(shifted), -1, keepdims=True))
    log_probs = shifted - jnp.log(summed)
    probabilities = jnp.exp(log_probs)
    entropy = -lax.optimization_barrier(jnp.sum(jnp.where(allowed, probabilities * log_probs, 0.0), -1))
    slot_ids = lax.broadcasted_iota(jnp.int32, held.shape, 1)
    chosen = lax.optimization_barrier(jnp.sum(jnp.where(slot_ids == actions[:, None], log_probs, 0.0), -1))
    return jnp.sum(-advantage * chosen - ENTROPY_WEIGHT * entropy)

def group_mask():
    row_ids = lax.broadcasted_iota(jnp.int32, (GROUP, GROUP), 0)
    col_ids = lax.broadcasted_iota(jnp.int32, (GROUP, GROUP), 1)
    return (row_ids // LENGTH == col_ids // LENGTH) & (col_ids <= row_ids)

def span_loss(params, inputs, actions, action_masks, advantage):
    positions, gain_one, bias_one, qkv_weight, out_weight, gain_two, bias_two, up_weight, up_bias, down_weight, down_bias, gain_last, bias_last, actor_weight, actor_bias = params
    row_count = inputs.shape[0]
    start_rows = (inputs.reshape(row_count // LENGTH, LENGTH, D) + positions).reshape(row_count, D)
    mixed_rows = low_back(low(matmul(low(layer_norm(start_rows, gain_one, bias_one)), qkv_weight)))
    shaped = mixed_rows.reshape(row_count // GROUP, GROUP, 3, HEADS, HEAD)
    query_rows = shaped[:, :, 0]
    key_rows = shaped[:, :, 1]
    value_rows = shaped[:, :, 2]
    scores = jnp.einsum('gqhd,gkhd->ghqk', query_rows, key_rows, precision=lax.Precision.HIGHEST) * HEAD ** (-0.5)
    scores = jnp.where(group_mask(), low_back(scores), MASKED)
    highest = lax.optimization_barrier(jnp.max(scores, -1, keepdims=True))
    weights = jnp.exp(scores - highest)
    weights = weights / lax.optimization_barrier(jnp.sum(weights, -1, keepdims=True))
    attended = jnp.einsum('ghqk,gkhd->gqhd', low(weights), value_rows, precision=lax.Precision.HIGHEST)
    attended = low_back(low(attended)).reshape(row_count, D)
    middle = start_rows + low_back(matmul(attended, out_weight))
    hidden_in = low_back(matmul(low(layer_norm(middle, gain_two, bias_two)), up_weight) + up_bias)
    active_rows = low(jax.nn.gelu(hidden_in, approximate=False))
    final_rows = middle + low_back(matmul(active_rows, down_weight)) + down_bias
    logits = low_back(matmul(low(layer_norm(final_rows, gain_last, bias_last)), actor_weight) + actor_bias)
    return policy_loss(logits, action_masks, actions, advantage)

def reference(tokens, positions, norm_one_gain, norm_one_bias, qkv_weight, out_weight, norm_two_gain, norm_two_bias, up_weight, up_bias, down_weight, down_bias, final_gain, final_bias, actor_weight, actor_bias, actions, action_masks, game_ids, returns, values, running, percentiles):
    fresh_stats = DECAY_RATE * running + (1.0 - DECAY_RATE) * percentiles
    spread = jnp.maximum(1.0, fresh_stats[1] - fresh_stats[0])
    advantage = (returns - values) / jnp.repeat(spread[game_ids], LENGTH)
    params = tuple((weight.astype(jnp.float32) for weight in (positions, norm_one_gain, norm_one_bias, qkv_weight, out_weight, norm_two_gain, norm_two_bias, up_weight, up_bias, down_weight, down_bias, final_gain, final_bias, actor_weight, actor_bias)))
    block_rows = math.gcd(TOKENS, 4096)
    block_count = TOKENS // block_rows
    inputs = tokens.astype(jnp.float32).reshape(block_count, block_rows, D)
    side_data = (actions.reshape(block_count, block_rows), action_masks.reshape(block_count, block_rows, ACTIONS), advantage.reshape(block_count, block_rows))
    checked = jax.checkpoint(span_loss)

    def forward(inputs, params):

        def advance(running_total, pieces):
            return (running_total + checked(params, pieces[0], pieces[1], pieces[2], pieces[3]), None)
        loss_total, unused = lax.scan(advance, jnp.zeros((), jnp.float32), (inputs,) + side_data)
        return loss_total / TOKENS
    actor_loss, pullback = jax.vjp(forward, inputs, params)
    input_grad, grads = pullback(jnp.ones((), jnp.float32) * SEQS)
    return (actor_loss, fresh_stats, input_grad.reshape(TOKENS, D)) + tuple(grads)
```

```python
import functools
import math
import math

import jax
import jax.numpy as jnp
from jax import lax
from jax.experimental import pallas as pl
from jax.experimental.pallas import tpu as pltpu
from jax.sharding import PartitionSpec as P

HEADS = 8
HEAD = 64
LENGTH = 64
QUAD = 4
WIDE = QUAD * HEAD
MASKED = -1e30
EPSILON = 1e-05
DECAY_RATE = 0.9
ENTROPY_WEIGHT = 0.1
SLOTS = 32
VMEM_BYTES = 63 * 1024 * 1024
BF16 = jnp.bfloat16
F32 = jnp.float32

G1, B1, G2, B2, DB, GL, BL = range(7)
MESH = pl.DeviceIdType.MESH


def dot(left, right, left_dim, right_dim):
    return lax.dot_general(
        left, right, (((left_dim,), (right_dim,)), ((), ())), preferred_element_type=F32
    )


def mean_last(values):
    return jnp.sum(values, -1, keepdims=True) * (1.0 / values.shape[-1])


def normalise(values):
    centred = values - mean_last(values)
    scale = lax.rsqrt(mean_last(centred * centred) + EPSILON)
    return centred * scale, scale


def norm_back(unit, scale, gain, upstream):
    inner = upstream * gain
    return scale * (inner - mean_last(inner) - unit * mean_last(inner * unit))


def fold_rows(values):
    rows, width = values.shape
    return jnp.sum(values.reshape(rows // 8, 8, width), 0)


def gelu_pair(values):
    half = jnp.exp2(values * values * (-0.5 * 1.4426950408889634))
    span = 1.0 + jnp.abs(values) * (0.3275911 * 0.7071067811865476)
    guess = pl.reciprocal(span, approx=True)
    t = guess * (2.0 - span * guess)
    poly = t * (
        0.5 * 0.254829592
        + t
        * (
            0.5 * -0.284496736
            + t * (0.5 * 1.421413741 + t * (0.5 * -1.453152027 + t * (0.5 * 1.061405429)))
        )
    )
    tail = poly * half
    cdf = jnp.where(values < 0.0, tail, 1.0 - tail)
    density = half * 0.3989422804014327
    return values * cdf, cdf + values * density


def pair_masks():
    lane = lax.broadcasted_iota(jnp.int32, (LENGTH, 2 * HEAD), 1)
    first = jnp.where(lane < HEAD, 1.0, 0.0)
    return first.astype(BF16), (1.0 - first).astype(BF16)


def spread_heads(rows, masks):
    zero = jnp.zeros((LENGTH, 2 * HEAD), BF16)
    left, right = rows[:, : 2 * HEAD], rows[:, 2 * HEAD :]
    blocks = [jnp.concatenate([left * mask, zero], 1) for mask in masks]
    blocks += [jnp.concatenate([zero, right * mask], 1) for mask in masks]
    return jnp.concatenate(blocks, 0)


def gather_heads(blocks):
    lane = lax.broadcasted_iota(jnp.int32, (LENGTH, 2 * HEAD), 1)
    pairs = []
    for pair in range(QUAD // 2):
        lanes = slice(pair * 2 * HEAD, (pair + 1) * 2 * HEAD)
        low = 2 * pair * HEAD
        first, second = blocks[low : low + HEAD, lanes], blocks[low + HEAD : low + 2 * HEAD, lanes]
        pairs.append(jnp.where(lane < HEAD, first, second))
    return jnp.concatenate(pairs, 1)


def causal_bias():
    key = lax.broadcasted_iota(jnp.int32, (LENGTH, WIDE), 0)
    query = lax.rem(lax.broadcasted_iota(jnp.int32, (LENGTH, WIDE), 1), HEAD)
    return jnp.where(key <= query, 0.0, MASKED)


LOG2E = 1.4426950408889634
SCORE_SCALE = HEAD ** (-0.5) * LOG2E


def chains(r, i):
    width = r.tokens.shape[1]
    found = []
    for s in range(4):
        row = pl.multiple_of((4 * i + s) * LENGTH, LENGTH)
        for half in range(width // WIDE):
            at = half * WIDE
            columns = [slice(k * width + at, k * width + at + WIDE) for k in range(3)]
            found.append((4 * i + s, pl.ds(row, LENGTH), columns))
    return found


def attend_group(r, i):
    masks, bias = pair_masks(), r.causal[...]
    group = chains(r, i)
    scores = [
        dot(r.qkv[rows, k], spread_heads(r.qkv[rows, q], masks), 1, 1)
        for _, rows, (q, k, _) in group
    ]
    probs = []
    for (seq, _, (q, _, _)), score in zip(group, scores, strict=True):
        score = score * SCORE_SCALE + bias
        highest = jnp.max(score, 0, keepdims=True)
        weights = jnp.exp2(score - highest)
        summed = jnp.sum(weights, 0, keepdims=True)
        probs.append((weights * (1.0 / summed)).astype(BF16))
        r.totals[pl.ds(seq, 1), q] = highest + jnp.log(summed) * LOG2E
    blocks = [
        dot(prob, r.qkv[rows, v], 0, 0) for (_, rows, (_, _, v)), prob in zip(group, probs, strict=True)
    ]
    for (_, rows, (q, _, _)), block in zip(group, blocks, strict=True):
        r.attended[rows, q] = gather_heads(block).astype(BF16)


def attend_back_group(r, i):
    masks, bias = pair_masks(), r.causal[...]
    done = []
    for half in range(2):
        group = chains(r, i)[half::2]
        queries = [spread_heads(r.qkv[rows, q], masks) for _, rows, (q, _, _) in group]
        aboves = [spread_heads(r.attended[rows, q], masks) for _, rows, (q, _, _) in group]
        scores = [
            dot(r.qkv[rows, k], query, 1, 1)
            for (_, rows, (_, k, _)), query in zip(group, queries, strict=True)
        ]
        prob_grads = [
            dot(r.qkv[rows, v], above, 1, 1)
            for (_, rows, (_, _, v)), above in zip(group, aboves, strict=True)
        ]
        probs, score_grads = [], []
        for (seq, _, (q, _, _)), score, pull in zip(group, scores, prob_grads, strict=True):
            prob = jnp.exp2(score * SCORE_SCALE + bias - r.totals[pl.ds(seq, 1), q])
            row_terms = jnp.sum(pull * prob, 0, keepdims=True)
            score_grads.append((prob * (pull - row_terms)).astype(BF16))
            probs.append(prob.astype(BF16))
        value_grads = [dot(prob, above, 1, 0) for prob, above in zip(probs, aboves, strict=True)]
        key_grads = [dot(grad, query, 1, 0) for grad, query in zip(score_grads, queries, strict=True)]
        query_grads = [
            dot(grad, r.qkv[rows, k], 0, 0)
            for (_, rows, (_, k, _)), grad in zip(group, score_grads, strict=True)
        ]
        for (_, rows, (q, k, v)), dq, dk, dv in zip(
            group, query_grads, key_grads, value_grads, strict=True
        ):
            done.append((rows, q, (gather_heads(dq) * HEAD ** (-0.5)).astype(BF16)))
            done.append((rows, k, (dk * HEAD ** (-0.5)).astype(BF16)))
            done.append((rows, v, dv.astype(BF16)))
    for rows, columns, grad in done:
        r.qkv[rows, columns] = grad


def policy(logits, masks, actions, advantage, scale):
    allowed = masks > 0
    held = jnp.where(allowed, logits, MASKED)
    shifted = held - jnp.max(held, 0, keepdims=True)
    weights = jnp.exp(shifted)
    summed = jnp.sum(weights, 0, keepdims=True)
    log_probs = shifted - jnp.log(summed)
    probs = weights * (1.0 / summed)
    plogp = jnp.where(allowed, probs * log_probs, 0.0)
    entropy = -jnp.sum(plogp, 0, keepdims=True)
    slot = lax.broadcasted_iota(jnp.int32, logits.shape, 0)
    taken = slot == actions
    chosen = jnp.sum(jnp.where(taken, log_probs, 0.0), 0, keepdims=True)
    loss = -advantage * chosen - ENTROPY_WEIGHT * entropy
    pull = advantage * (probs - jnp.where(taken, 1.0, 0.0)) + ENTROPY_WEIGHT * (
        plogp + probs * entropy
    )
    return loss, jnp.where(allowed, pull * scale, 0.0)


STRIP = 32
THIN = 16
LARGE = 1 << 20


class Names:
    def __init__(self, names, refs):
        self.table = dict(zip(names, refs, strict=True))

    def __getattr__(self, name):
        return self.table[name]


SPLIT = (4, 2, 2)
PACK_ROWS = 48
PACK_GRAD_ROWS = 40
POSITION_AT, SMALL_AT, BIAS_AT, LOSS_AT = 0, 64, 96, 97


def merged(block):
    return block.reshape(-1, block.shape[-1])


def start_rows(r, row, at):
    frame = at % LENGTH
    start = r.tokens[pl.ds(pl.multiple_of(row + at, STRIP), STRIP), :].astype(F32)
    return start + r.positions[frame : frame + STRIP, :]


def norm_pass(r):
    count = r.tokens.shape[0]
    rows = 4 * LENGTH

    def body(i, carry):
        row = pl.multiple_of(i * rows, rows)
        for at in range(0, rows, STRIP):
            unit, _ = normalise(start_rows(r, row, at))
            normed = unit * r.small[G1 : G1 + 1, :] + r.small[B1 : B1 + 1, :]
            r.attended[pl.ds(pl.multiple_of(row + at, STRIP), STRIP), :] = normed.astype(BF16)
        r.normed_t[:, pl.ds(row, rows)] = r.attended[pl.ds(row, rows), :].T
        return carry

    lax.fori_loop(0, count // rows, body, 0)


def front(r, pump):
    count, width = r.tokens.shape
    rows = 4 * LENGTH

    def body(i, carry):
        pump(i)
        row = pl.multiple_of(i * rows, rows)
        normed = r.attended[pl.ds(row, rows), :]
        for at in range(0, 3 * width, width):
            r.qkv[pl.ds(row, rows), at : at + width] = dot(
                normed, merged(r.w_qkv[:, :, :, :, at : at + width]), 1, 0
            ).astype(BF16)
        attend_group(r, i)
        return carry

    lax.fori_loop(0, count // rows, body, 0)


def add_grad(ref, index, values):
    ref[index] += values.reshape(ref[index].shape)


def add_columns(ref, values):
    count = ref.shape[-1]
    for k in range(values.shape[1] // count):
        ref[k // 2, k % 2] += values[:, k * count : (k + 1) * count]


def clear(r):
    for ref in (r.g_out, r.g_up, r.g_down):

        def body(z, carry, ref=ref):
            ref[z] = jnp.zeros(ref.shape[1:], F32)
            return carry

        lax.fori_loop(0, ref.shape[0], body, 0)
    for ref in (r.g_actor, r.g_small, r.g_up_bias, r.g_positions, r.head_sums):
        ref[...] = jnp.zeros_like(ref)


def frame_values(r):
    r.causal[...] = causal_bias()
    fresh = DECAY_RATE * r.running[...] + (1.0 - DECAY_RATE) * r.percentiles[...]
    spread = jnp.maximum(1.0, fresh[1:2, :] - fresh[0:1, :])
    seqs = r.game_ids.shape[0]
    game = r.game_ids[...].reshape(seqs, 1)
    slot = lax.broadcasted_iota(jnp.int32, (seqs, spread.shape[1]), 1)
    column = jnp.sum(jnp.where(slot == game, spread, 0.0), 1, keepdims=True)
    count = 8 * LENGTH
    owner = lax.broadcasted_iota(jnp.int32, (8, count), 0)
    frame = lax.broadcasted_iota(jnp.int32, (8, count), 1)
    for k in range(seqs // 8):
        here = slice(k * count, (k + 1) * count)
        near = jnp.where(frame // LENGTH == owner, column[8 * k : 8 * k + 8], 0.0)
        wide = jnp.sum(near, 0, keepdims=True)
        r.advantage[:, here] = (r.returns[here] - r.values[here]).reshape(1, count) / wide
        r.action_row[:, here] = r.actions[here].reshape(1, count)


class Tile:
    def __init__(self, r, side):
        def pick(name):
            return r.table[name, side]

        self.active, self.slope = pick("active"), pick("slope")
        self.two_t, self.unit, self.last = pick("two_t"), pick("unit"), pick("last")
        self.scale = pick("scale")


def middle_part(r, scale):
    count, width = r.tokens.shape
    rows = r.low.shape[0]
    shards = r.w_up.shape[0]
    chunk = r.w_up.shape[-1] // shards
    slots = r.masks.shape[0]
    out_weight = r.w_out
    head_bias = jnp.concatenate(
        [r.actor_bias[...].astype(F32).reshape(slots, 1), jnp.zeros((SLOTS - slots, 1), F32)], 0
    )
    everything = slice(None)
    strips = [slice(at, at + STRIP) for at in range(0, rows, STRIP)]

    def gain(k):
        return r.small[k : k + 1, :]

    def tile_rows(i):
        return pl.ds(pl.multiple_of(i * rows, rows), rows)

    def project(i):
        return dot(r.attended[tile_rows(i), :], merged(out_weight[...]), 1, 0)

    def before(i, t, projected):
        row = pl.multiple_of(i * rows, rows)
        for strip in strips:
            mid = start_rows(r, row, strip.start) + projected[strip]
            unit, spread = normalise(mid)
            r.two_low[strip, :] = (unit * gain(G2) + gain(B2)).astype(BF16)
            t.unit[strip, :] = unit
            t.scale[strip, :] = spread
            t.last[strip, :] = mid + gain(DB)
        t.two_t[...] = r.two_low[...].T

    def columns(j):
        return pl.ds(pl.multiple_of(j * chunk, chunk), chunk)

    def up_weight(j):
        return merged(r.w_up[:, :, :, :, columns(j)])

    def activate(j, t, hidden):
        cols = columns(j)
        bias = r.up_bias[:, cols]
        for at in range(0, rows, THIN):
            value, derivative = gelu_pair(hidden[at : at + THIN] + bias)
            t.active[at : at + THIN, cols] = value.astype(BF16)
            t.slope[at : at + THIN, cols] = derivative.astype(BF16)

    def forward_only(j, t):
        activate(j, t, dot(r.two_low[...], up_weight(j), 1, 0))
        t.last[...] += dot(t.active[:, columns(j)], merged(r.w_down[j]), 1, 0)

    def both_ways(j, here, there):
        cols = columns(j)
        if there is not None:
            hidden = dot(r.two_low[...], up_weight(j), 1, 0)
        hidden_grad = dot(r.low[...], merged(r.w_down[j]), 1, 1)
        add_columns(r.g_down.at[j], dot(r.low_t[...], here.active[:, cols], 1, 0))
        total = r.g_up_bias[:, cols]
        for at in range(0, rows, THIN):
            strip = slice(at, at + THIN)
            part = (hidden_grad[strip] * here.slope[strip, cols].astype(F32)).astype(BF16)
            r.hidden_grad[strip, :] = part
            total += fold_rows(part.astype(F32))
        r.g_up_bias[:, cols] = total
        r.two_in[...] += dot(r.hidden_grad[...], up_weight(j), 1, 1)
        add_grad(
            r.g_up,
            (everything, everything, everything, everything, cols),
            dot(here.two_t[...], r.hidden_grad[...], 1, 0),
        )
        if there is not None:
            activate(j, there, hidden)
            there.last[...] += dot(there.active[:, cols], merged(r.w_down[j]), 1, 0)

    def last_norm(i, t):
        for strip in strips:
            unit, spread = normalise(t.last[strip, :])
            r.low[strip, :] = (unit * gain(GL) + gain(BL)).astype(BF16)
            t.last[strip, :] = unit
            r.scale_last[strip, :] = spread
        return dot(r.actor[...], r.low[...], 1, 1) + head_bias

    def head(i, logits):
        here = tile_rows(i)
        masks = jnp.concatenate(
            [r.masks[:, here], jnp.zeros((SLOTS - slots, rows), jnp.int32)], 0
        )
        loss, pull = policy(logits, masks, r.action_row[:, here], r.advantage[:, here], scale)
        logit_grad = pull.astype(BF16)
        last_in = dot(logit_grad, r.actor[...], 0, 0)
        r.g_actor[...] += dot(logit_grad, r.low[...], 1, 0)
        wide_grad = logit_grad.astype(F32)
        fold = r.head_sums[0:SLOTS, :]
        for at in range(0, rows, 128):
            fold += wide_grad[:, at : at + 128]
        r.head_sums[0:SLOTS, :] = fold
        fold = r.head_sums[SLOTS : SLOTS + 1, :]
        for at in range(0, rows, 128):
            fold += loss[:, at : at + 128]
        r.head_sums[SLOTS : SLOTS + 1, :] = fold
        return last_in

    def last_norm_back(t, last_in):
        sums = [r.g_small[k] for k in (GL, BL, DB)]
        for strip in strips:
            above, unit = last_in[strip], t.last[strip, :]
            grad = norm_back(unit, r.scale_last[strip, :], gain(GL), above)
            sums[0] += fold_rows(above * unit)
            sums[1] += fold_rows(above)
            sums[2] += fold_rows(grad)
            t.last[strip, :] = grad
            r.low[strip, :] = grad.astype(BF16)
        for k, total in zip((GL, BL, DB), sums, strict=True):
            r.g_small[k] = total
        r.low_t[...] = r.low[...].T
        r.two_in[...] = jnp.zeros((rows, width), F32)

    def two_norm_back(i, t):
        row = pl.multiple_of(i * rows, rows)
        sums = [r.g_small[k] for k in (G2, B2)]
        for strip in strips:
            above, unit = r.two_in[strip, :], t.unit[strip, :]
            sums[0] += fold_rows(above * unit)
            sums[1] += fold_rows(above)
            grad = t.last[strip, :] + norm_back(unit, t.scale[strip, :], gain(G2), above)
            r.middle_grad[pl.ds(pl.multiple_of(row + strip.start, STRIP), STRIP), :] = grad
            r.middle_low[strip, :] = grad.astype(BF16)
        for k, total in zip((G2, B2), sums, strict=True):
            r.g_small[k] = total

    def out_back(i):
        here = tile_rows(i)
        add_grad(r.g_out, ..., dot(r.attended[here, :], r.middle_low[...], 0, 0))
        r.attended[here, :] = dot(r.middle_low[...], merged(out_weight[...]), 1, 1).astype(BF16)

    sides = [Tile(r, 0), Tile(r, 1)]
    tiles = count // rows

    def chunks(step):
        def body(j, carry):
            step(j)
            return carry

        lax.fori_loop(0, shards, body, 0)

    def step(i, side, first=False, last=False):
        here, there = sides[side], sides[1 - side]
        projected = None if last else project(i + 1)
        logits = last_norm(i, here)
        if not first:
            two_norm_back(i - 1, there)
        last_in = head(i, logits)
        if not last:
            before(i + 1, there, projected)
        last_norm_back(here, last_in)
        if not first:
            out_back(i - 1)
        chunks(lambda j: both_ways(j, here, None if last else there))

    before(0, sides[0], project(0))
    chunks(lambda j: forward_only(j, sides[0]))
    step(0, 0, first=True)

    def pair(p, carry):
        step(2 * p + 1, 1)
        step(2 * p + 2, 0)
        return carry

    lax.fori_loop(0, (tiles - 2) // 2, pair, 0)
    step(tiles - 1, 1, last=True)
    two_norm_back(tiles - 1, sides[1])
    out_back(tiles - 1)


def attend_back(r, pump):
    count = r.tokens.shape[0]
    rows = 4 * LENGTH

    def body(i, carry):
        pump(i)
        attend_back_group(r, i)
        return carry

    lax.fori_loop(0, count // rows, body, 0)


def qkv_weight_grad(r, third):
    width = r.tokens.shape[1]
    step = width // 2
    for at in range(third * width, (third + 1) * width, step):
        values = dot(r.normed_t[...], r.qkv[:, at : at + step], 1, 0)
        r.g_qkv[:, :, :, :, at : at + step] = values.reshape(r.g_qkv.shape[:4] + (step,))


def start_back(r, pump, tile_done):
    count = r.tokens.shape[0]
    rows = 4 * LENGTH
    gain = r.small[G1 : G1 + 1, :]

    def body(i, carry):
        pump(i)
        row = pl.multiple_of(i * rows, rows)
        one_in = dot(r.qkv[pl.ds(row, rows), :], merged(r.w_qkv[...]), 1, 1)
        sums = [r.g_small[k] for k in (G1, B1)]
        for at in range(0, rows, STRIP):
            there = pl.ds(pl.multiple_of(row + at, STRIP), STRIP)
            unit, scale = normalise(start_rows(r, row, at))
            above = one_in[at : at + STRIP]
            sums[0] += fold_rows(above * unit)
            sums[1] += fold_rows(above)
            grad = r.middle_grad[there, :] + norm_back(unit, scale, gain, above)
            r.middle_grad[there, :] = grad
            frame = at % LENGTH
            r.g_positions[frame : frame + STRIP, :] += grad
        for k, total in zip((G1, B1), sums, strict=True):
            r.g_small[k] = total
        tile_done(i)
        return carry

    lax.fori_loop(0, count // rows, body, 0)


def pack_shards(r):
    part = r.positions_in.shape[0]
    slots = r.masks.shape[0]
    rows = [
        ref[...].astype(F32).reshape(1, part)
        for ref in (r.gain1, r.bias1, r.gain2, r.bias2, r.bias_down, r.gain3, r.bias3)
    ]
    rows += [r.actor_in[...].astype(F32), jnp.zeros((32 - 7 - slots, part), F32)]
    features = jnp.concatenate(
        [r.positions_in[...].astype(F32), jnp.concatenate(rows, 0).T, jnp.zeros((part, 32), F32)], 1
    )
    bias = r.up_bias_in[...].astype(F32).reshape(1, 128)
    packed = jnp.concatenate([features, bias, jnp.zeros((PACK_ROWS - part - 1, 128), F32)], 0)
    r.pack_own[...] = packed.astype(BF16)


def unpack_shards(r):
    slots = r.masks.shape[0]
    blocks = r.pack[...].astype(F32).reshape(-1, PACK_ROWS, 128)
    part = r.positions_in.shape[0]
    features = merged(blocks[:, :part, :]).T
    r.positions[...] = features[POSITION_AT : POSITION_AT + LENGTH]
    small = features[SMALL_AT : SMALL_AT + 32]
    r.small[...] = small[0:8]
    width = small.shape[1]
    r.actor[...] = jnp.concatenate(
        [small[7 : 7 + slots], jnp.zeros((SLOTS - slots, width), F32)], 0
    ).astype(BF16)
    r.up_bias[...] = jnp.concatenate(
        [blocks[f, part : part + 1, :] for f in range(blocks.shape[0])], 1
    )


def small_rows(r):
    slots = r.masks.shape[0]
    rows = [jnp.sum(r.g_small[k], 0, keepdims=True) for k in range(7)]
    return jnp.concatenate(
        rows + [r.g_actor[0:slots, :], jnp.zeros((32 - 7 - slots, rows[0].shape[1]), F32)], 0
    )


def pack_grads(r):
    width = r.tokens.shape[1]
    part = r.positions_in.shape[0]
    features = jnp.concatenate(
        [r.g_positions[...], small_rows(r), jnp.zeros((128 - SMALL_AT - 32, width), F32)], 0
    ).T
    sums = jnp.sum(r.head_sums[0 : SLOTS + 8, :], 1, keepdims=True)
    lane = lax.broadcasted_iota(jnp.int32, (part, 128), 1)
    bias = jnp.sum(r.g_up_bias[...], 0, keepdims=True)
    shape = r.g_pack.shape
    for f in range(width // part):
        block = features[f * part : (f + 1) * part]
        block = jnp.where(lane == BIAS_AT, sums[0:SLOTS], block)
        block = jnp.where(lane == LOSS_AT, sums[SLOTS : SLOTS + 1], block)
        owner = (f // 4, f // 2 % 2, f % 2)
        rows = [block, bias[:, f * 128 : (f + 1) * 128], jnp.zeros((shape[3] - part - 1, 128), F32)]
        r.g_pack[owner] = jnp.concatenate(rows, 0)


GATHERS = 9
REDUCES = (
    (128, 512, BF16),
    (2048, 32, BF16),
    (512, 32, BF16),
    (512, 32, BF16),
    (512, 32, BF16),
    (512, 32, BF16),
    (128, PACK_GRAD_ROWS, F32),
)


class Place:
    def __init__(self):
        self.x = lax.axis_index("dp")
        f = lax.axis_index("fsdp")
        self.z, self.y, self.c = f // 4, f // 2 % 2, f % 2

    def at(self, x=None, z=None, y=None, c=None):
        pick = lambda new, old: old if new is None else new
        f = pick(z, self.z) * 4 + pick(y, self.y) * 2 + pick(c, self.c)
        return (pick(x, self.x), f)

    def z_partner(self, k):
        return (self.z + 1 - 2 * (self.z % 2), (self.z + 2) % 4, 3 - self.z)[k]

    def partners(self):
        return [self.at(z=self.z_partner(k)) for k in range(3)] + [
            self.at(y=1 - self.y),
            self.at(c=1 - self.c),
            self.at(x=1 - self.x),
        ]


class Gather:
    def __init__(self, r, place, index, full, own, at, count):
        cols = slice(at, at + count)
        self.full, self.own, self.cols, self.place = full, own, cols, place
        p = place

        def copy(src, dst, k, device):
            return pltpu.make_async_remote_copy(
                src_ref=src,
                dst_ref=dst,
                send_sem=r.gather_send.at[index, k],
                recv_sem=r.gather_recv.at[index, k],
                device_id=device,
                device_id_type=MESH,
            )

        mine = full.at[p.z, p.y, p.c, :, cols]
        self.z = [copy(own.at[:, cols], mine, k, p.at(z=p.z_partner(k))) for k in range(3)]
        line = full.at[:, p.y, p.c, :, cols]
        self.y = copy(line, line, 3, p.at(y=1 - p.y))
        plane = full.at[:, :, p.c, :, cols]
        self.c = copy(plane, plane, 4, p.at(c=1 - p.c))

    def start_z(self):
        for copy in self.z:
            copy.start()
        p = self.place
        self.full[p.z, p.y, p.c, :, self.cols] = self.own[:, self.cols]

    def start_y(self):
        for copy in self.z:
            copy.wait_recv()
        self.y.start()

    def start_c(self):
        self.y.wait_recv()
        self.c.start()

    def ready(self):
        self.c.wait_recv()

    def close(self):
        for copy in self.z + [self.y, self.c]:
            copy.wait_send()


class Reduce:
    def __init__(self, r, place, index, grad, at=0):
        count, _, kind = REDUCES[index]
        self.grad, self.cols, self.place, self.kind = grad, slice(at, at + count), place, kind
        p = place
        self.buffers = [r.table[index, part] for part in range(len(REDUCE_LEADS))]
        sc, rc, ry, rz, rx = self.buffers
        self.sy, self.sz, self.sx = sc.at[:, 0], [sc.at[k, 1] for k in range(3)], sc.at[3, 1]

        def copy(src, dst, k, device):
            return pltpu.make_async_remote_copy(
                src_ref=src,
                dst_ref=dst,
                send_sem=r.reduce_send.at[index, k],
                recv_sem=r.reduce_recv.at[index, k],
                device_id=device,
                device_id_type=MESH,
            )

        self.c = copy(sc, rc, 0, p.at(c=1 - p.c))
        self.y = copy(self.sy, ry, 1, p.at(y=1 - p.y))
        self.z = [copy(self.sz[k], rz.at[k], 2 + k, p.at(z=p.z_partner(k))) for k in range(3)]
        self.x = copy(self.sx, rx, 5, p.at(x=1 - p.x))

    def start_c(self):
        sc, p = self.buffers[0], self.place

        def body(z, carry):
            sc[z] = self.grad[z, :, 1 - p.c, :, self.cols].astype(self.kind)
            return carry

        lax.fori_loop(0, 4, body, 0)
        self.c.start()

    def start_y(self):
        rc, sy = self.buffers[1], self.sy
        p = self.place
        self.c.wait()

        def body(z, carry):
            away = self.grad[z, 1 - p.y, p.c, :, self.cols] + rc[z, 1 - p.y].astype(F32)
            sy[z] = away.astype(self.kind)
            self.grad[z, p.y, p.c, :, self.cols] += rc[z, p.y].astype(F32)
            return carry

        lax.fori_loop(0, 4, body, 0)
        self.y.start()

    def start_z(self):
        ry, sz = self.buffers[2], self.sz
        p = self.place
        self.y.wait_recv()
        for k in (2, 1, 0):
            owner = p.z_partner(k)
            away = self.grad[owner, p.y, p.c, :, self.cols] + ry[owner].astype(F32)
            sz[k][...] = away.astype(self.kind)
            self.z[k].start()
        self.grad[p.z, p.y, p.c, :, self.cols] += ry[p.z].astype(F32)

    def start_x(self):
        rz, sx = self.buffers[3], self.sx
        p = self.place
        for copy in self.z:
            copy.wait_recv()
        near = self.grad[p.z, p.y, p.c, :, self.cols] + rz[0].astype(F32)
        sx[...] = (near + (rz[1].astype(F32) + rz[2].astype(F32))).astype(self.kind)
        self.x.start()

    def finish(self, out):
        sx, rx = self.sx, self.buffers[4]
        self.x.wait_recv()
        out[:, self.cols] = sx[...].astype(F32) + rx[...].astype(F32)

    def close(self):
        for copy in self.z + [self.y, self.x]:
            copy.wait_send()


REDUCE_LEADS = ((4, 2), (4, 2), (4,), (3,), ())


def layer_scratch(row_count, width, hidden_width, shards):
    tile = 256
    seqs = row_count // LENGTH
    pairs = dict(
        active=((tile, hidden_width), BF16),
        slope=((tile, hidden_width), BF16),
        two_t=((width, tile), BF16),
        unit=((tile, width), F32),
        last=((tile, width), F32),
        scale=((tile, 1), F32),
    )
    both = {(name, side): item for name, item in pairs.items() for side in range(2)}
    return both | dict(
        tokens=((row_count, width), BF16),
        middle_grad=((row_count, width), F32),
        normed_t=((width, row_count), BF16),
        qkv=((row_count, 3 * width), BF16),
        attended=((row_count, width), BF16),
        totals=((seqs, width), F32),
        causal=((LENGTH, WIDE), F32),
        advantage=((1, row_count), F32),
        action_row=((1, row_count), jnp.int32),
        two_low=((tile, width), BF16),
        low=((tile, width), BF16),
        low_t=((width, tile), BF16),
        middle_low=((tile, width), BF16),
        hidden_grad=((tile, hidden_width // 4), BF16),
        two_in=((tile, width), F32),
        scale_last=((tile, 1), F32),
        local_sem=pltpu.SemaphoreType.DMA((2,)),
    )


def grad_shapes(width, hidden_width, shards):
    split = SPLIT
    part, hidden_part = width // shards, hidden_width // shards
    return dict(
        g_qkv=(split + (part, 3 * width), F32),
        g_out=(split + (part, width), F32),
        g_up=(split + (part, hidden_width), F32),
        g_down=(split + (width, hidden_part), F32),
        g_actor=((SLOTS, width), F32),
        g_small=((7, 8, width), F32),
        g_up_bias=((8, hidden_width), F32),
        g_positions=((LENGTH, width), F32),
        head_sums=((SLOTS + 8, 128), F32),
    )


def at_step(i, table):
    for step, actions in table.items():

        @pl.when(i == step)
        def _(actions=actions):
            for action in actions:
                action()


def spread_kernel(names, scale, *refs):
    r = Names(names, refs)
    place = Place()
    load = pltpu.make_async_copy(r.tokens_in, r.tokens, r.local_sem.at[0])
    load.start()
    partners = place.partners()
    barrier = pltpu.get_barrier_semaphore()
    for device in partners:
        pl.semaphore_signal(barrier, inc=1, device_id=device, device_id_type=MESH)
    pack_shards(r)
    pl.semaphore_wait(barrier, len(partners))
    width, hidden_width = r.w_out.shape[-1], r.w_up.shape[-1]
    plan = [(r.pack, r.pack_own, 0, 128)]
    plan += [(r.w_qkv, r.qkv_in, k * width, width) for k in range(3)]
    plan += [(r.w_out, r.out_in, 0, width)]
    plan += [(r.w_up, r.up_in, k * hidden_width // 2, hidden_width // 2) for k in range(2)]
    plan += [(r.w_down, r.down_in, k * width // 2, width // 2) for k in range(2)]
    gathers = [Gather(r, place, k, *item) for k, item in enumerate(plan)]
    pack, q, k, v, out, up0, up1, down0, down1 = gathers
    pack.start_z()
    q.start_z()
    k.start_z()
    v.start_z()
    pack.start_y()
    q.start_y()
    pack.start_c()
    clear(r)
    frame_values(r)
    pack.ready()
    unpack_shards(r)
    k.start_y()
    q.start_c()
    load.wait()
    out.start_z()
    up0.start_z()
    norm_pass(r)
    v.start_y()
    k.start_c()
    up1.start_z()
    down0.start_z()
    down1.start_z()
    v.start_c()
    for group in (q, k, v):
        group.ready()

    front(
        r,
        lambda i: at_step(
            i,
            {
                1: [out.start_y],
                2: [out.start_c],
                3: [up0.start_y],
                5: [up1.start_y, up0.start_c],
                7: [down0.start_y, up1.start_c],
                9: [down1.start_y, down0.start_c],
            },
        ),
    )
    down1.start_c()
    for group in (out, up0, up1, down0, down1):
        group.ready()
    middle_part(r, scale)

    plan = [(r.g_down,), (r.g_up,), (r.g_out,)]
    plan += [(r.g_qkv, k * width) for k in range(3)] + [(r.g_pack,)]
    reduces = [Reduce(r, place, k, *item) for k, item in enumerate(plan)]
    down, up, out, q, k, v, pack = reduces
    down.start_c()
    up.start_c()
    out.start_c()
    attend_back(
        r,
        lambda i: at_step(
            i,
            {
                1: [down.start_y],
                2: [up.start_y],
                3: [out.start_y],
                5: [down.start_z],
                8: [up.start_z, down.start_x],
                9: [out.start_z],
            },
        ),
    )
    for third, group in enumerate((q, k, v)):
        qkv_weight_grad(r, third)
        group.start_c()
        if third:
            (q, k)[third - 1].start_y()
    v.start_y()
    up.start_x()
    out.start_x()

    def stored(i):
        rows = pl.ds(pl.multiple_of(i * 4 * LENGTH, 4 * LENGTH), 4 * LENGTH)
        return pltpu.make_async_copy(
            r.middle_grad.at[rows, :], r.tokens_grad.at[rows, :], r.store_sem.at[i]
        )

    start_back(
        r,
        lambda i: at_step(
            i, {2: [q.start_z], 4: [k.start_z], 6: [v.start_z, q.start_x], 8: [k.start_x]}
        ),
        lambda i: stored(i).start(),
    )
    pack_grads(r)
    pack.start_c()
    v.start_x()
    pack.start_y()
    down.finish(r.down_out)
    up.finish(r.up_out)
    out.finish(r.out_out)
    pack.start_z()
    for group in (q, k, v):
        group.finish(r.qkv_out)
    pack.start_x()
    for i in range(r.middle_grad.shape[0] // (4 * LENGTH)):
        stored(i).wait()
    for group in gathers + reduces:
        group.close()
    pack.finish(r.pack_out)


def finish_kernel(names, count, *refs):
    r = Names(names, refs)
    step = 4 * LENGTH
    parts = [pl.ds(at, step) for at in range(0, r.tokens.shape[0], step)]
    loads = [
        pltpu.make_async_copy(r.tokens.at[part, :], r.held.at[part, :], r.load_sem.at[k])
        for k, part in enumerate(parts)
    ]
    stores = [
        pltpu.make_async_copy(r.held.at[part, :], r.o_tokens.at[part, :], r.store_sem.at[k])
        for k, part in enumerate(parts)
    ]
    for load in loads:
        load.start()
    r.o_qkv[...] = r.qkv[...]
    r.o_out[...] = r.out[...]
    r.o_up[...] = r.up[...]
    r.o_down[...] = r.down[...].T
    r.o_stats[...] = DECAY_RATE * r.running[...] + (1.0 - DECAY_RATE) * r.percentiles[...]
    part, positions = r.o_positions.shape
    slots = r.o_actor.shape[0]
    features = r.pack[0:part, :]
    r.o_positions[...] = features[:, POSITION_AT : POSITION_AT + positions]
    turned = features.T
    vectors = (r.gain1, r.bias1, r.gain2, r.bias2, r.bias_down, r.gain3, r.bias3)
    for k, ref in enumerate(vectors):
        ref[...] = turned[SMALL_AT + k : SMALL_AT + k + 1, :].reshape(part)
    r.o_actor[...] = turned[SMALL_AT + 7 : SMALL_AT + 7 + slots, :]
    r.o_actor_bias[...] = turned[BIAS_AT : BIAS_AT + 1, :].reshape(part)[0:slots]
    r.o_loss[...] = features[0:1, LOSS_AT : LOSS_AT + 1] * (1.0 / count)
    r.o_up_bias[...] = r.pack[part : part + 1, :].reshape(128)
    for load, store in zip(loads, stores, strict=True):
        load.wait()
        store.start()
    for store in stores:
        store.wait()


def local_kernel(names, scale, *refs):
    r = Names(names, refs)
    load = pltpu.make_async_copy(r.tokens_in, r.tokens, r.local_sem.at[0])
    load.start()
    clear(r)
    frame_values(r)
    load.wait()
    norm_pass(r)
    front(r, lambda i: None)
    middle_part(r, scale)
    attend_back(r, lambda i: None)
    for third in range(3):
        qkv_weight_grad(r, third)
    start_back(r, lambda i: None, lambda i: None)
    store = pltpu.make_async_copy(r.middle_grad, r.tokens_grad, r.local_sem.at[1])
    store.start()
    store.wait()


def run(kernel, constant, ins, outs, scratch, flops=0, side_effects=False, collective=None):
    vmem = pl.BlockSpec(memory_space=pltpu.VMEM)
    anywhere = pl.BlockSpec(memory_space=pl.ANY)
    in_specs = [anywhere if array.size > LARGE else vmem for array in ins.values()]
    out_specs = [anywhere if math.prod(shape) > LARGE else vmem for shape, _ in outs.values()]
    return pl.pallas_call(
        functools.partial(kernel, (*ins, *outs, *scratch), constant),
        out_shape=[jax.ShapeDtypeStruct(shape, kind) for shape, kind in outs.values()],
        in_specs=in_specs,
        out_specs=out_specs,
        scratch_shapes=[
            item if not isinstance(item, tuple) else pltpu.VMEM(item[0], item[1])
            for item in scratch.values()
        ],
        compiler_params=pltpu.CompilerParams(
            vmem_limit_bytes=VMEM_BYTES, has_side_effects=side_effects, collective_id=collective
        ),
        cost_estimate=pl.CostEstimate(flops=flops, bytes_accessed=1 << 24, transcendentals=0),
    )(*ins.values())


def on_device(
    tokens,
    positions,
    norm_one_gain,
    norm_one_bias,
    qkv_weight,
    out_weight,
    norm_two_gain,
    norm_two_bias,
    up_weight,
    up_bias,
    down_weight,
    down_bias,
    final_gain,
    final_bias,
    actor_weight,
    actor_bias,
    actions,
    action_masks,
    game_ids,
    returns,
    values,
    running,
    percentiles,
):
    row_count, width = tokens.shape
    seq_count = row_count // LENGTH
    hidden_width = up_weight.shape[1]
    slots = actor_weight.shape[1]
    fsdp = lax.axis_size("fsdp")
    device_count = lax.axis_size("dp") * fsdp
    token_total = row_count * device_count
    scale = float(seq_count * device_count) / token_total
    flops = 6 * row_count * width * (4 * width + 2 * hidden_width)
    part, hidden_part = width // fsdp, hidden_width // fsdp

    vectors = dict(
        gain1=norm_one_gain,
        bias1=norm_one_bias,
        gain2=norm_two_gain,
        bias2=norm_two_bias,
        bias_down=down_bias,
        gain3=final_gain,
        bias3=final_bias,
    )
    stats = dict(running=running, percentiles=percentiles)
    frames = stats | dict(
        tokens_in=tokens,
        actor_bias=actor_bias,
        actions=actions,
        masks=action_masks.T,
        game_ids=game_ids,
        returns=returns,
        values=values,
    )
    scratch = layer_scratch(row_count, width, hidden_width, 16)
    grads = grad_shapes(width, hidden_width, 16)
    weight_shapes = dict(
        w_qkv=(SPLIT + (width // 16, 3 * width), BF16),
        w_out=(SPLIT + (width // 16, width), BF16),
        w_up=(SPLIT + (width // 16, hidden_width), BF16),
        w_down=(SPLIT + (hidden_width // 16, width), BF16),
    )

    if fsdp == 16 and lax.axis_size("dp") == 2:
        ins = frames | vectors
        ins |= dict(qkv_in=qkv_weight, out_in=out_weight, up_in=up_weight, down_in=down_weight)
        ins |= dict(up_bias_in=up_bias, positions_in=positions.T, actor_in=actor_weight.T)
        shard_grads = dict(
            qkv_out=((part, 3 * width), F32),
            out_out=((part, width), F32),
            up_out=((part, hidden_width), F32),
            down_out=((width, hidden_part), F32),
        )
        outs = dict(
            tokens_grad=((row_count, width), F32), pack_out=((PACK_GRAD_ROWS, 128), F32)
        )
        scratch |= grads | weight_shapes
        scratch |= dict(
            pack=(SPLIT + (PACK_ROWS, 128), BF16),
            pack_own=((PACK_ROWS, 128), BF16),
            g_pack=(SPLIT + (PACK_GRAD_ROWS, 128), F32),
            positions=((LENGTH, width), F32),
            small=((8, width), F32),
            actor=((SLOTS, width), BF16),
            up_bias=((1, hidden_width), F32),
            gather_send=pltpu.SemaphoreType.DMA((GATHERS, 5)),
            gather_recv=pltpu.SemaphoreType.DMA((GATHERS, 5)),
            reduce_send=pltpu.SemaphoreType.DMA((len(REDUCES), 6)),
            reduce_recv=pltpu.SemaphoreType.DMA((len(REDUCES), 6)),
            store_sem=pltpu.SemaphoreType.DMA((row_count // (4 * LENGTH),)),
        )
        for index, (count, rows, kind) in enumerate(REDUCES):
            for item, lead in enumerate(REDUCE_LEADS):
                scratch[index, item] = (lead + (rows, count), kind)
        tokens_grad, pack, qkv_g, out_g, up_g, down_g = run(
            spread_kernel, scale, ins, outs | shard_grads, scratch, flops, True, 0
        )
        vector = ((part,), F32)
        final = dict(
            o_loss=((1, 1), F32),
            o_stats=(running.shape, F32),
            o_positions=((part, LENGTH), F32),
            o_qkv=shard_grads["qkv_out"],
            o_out=shard_grads["out_out"],
            o_up=shard_grads["up_out"],
            o_down=((hidden_part, width), F32),
            o_up_bias=((hidden_part,), F32),
            o_actor=((slots, part), F32),
            o_actor_bias=((slots,), F32),
            o_tokens=((row_count, width), F32),
        )
        copies = pltpu.SemaphoreType.DMA((row_count // (4 * LENGTH),))
        done = run(
            finish_kernel,
            token_total,
            stats
            | dict(pack=pack, qkv=qkv_g, out=out_g, up=up_g, down=down_g, tokens=tokens_grad),
            final | dict.fromkeys(vectors, vector),
            dict(held=((row_count, width), F32), load_sem=copies, store_sem=copies),
        )
        loss, new_stats, pos_g, qkv_g, out_g, up_g, down_g = done[:7]
        up_bias_g, actor_g, actor_bias_g, tokens_grad = done[7:11]
        gain1, bias1, gain2, bias2, bias_down, gain3, bias3 = done[11:]
        return (
            loss.reshape(()),
            new_stats,
            tokens_grad,
            pos_g.T,
            gain1,
            bias1,
            qkv_g,
            out_g,
            gain2,
            bias2,
            up_g,
            up_bias_g,
            down_g,
            bias_down,
            gain3,
            bias3,
            actor_g.T,
            actor_bias_g,
        )

    def gather(array, axis):
        return lax.all_gather(array, "fsdp", axis=axis, tiled=True)

    packed = gather(
        jnp.concatenate([jnp.stack(list(vectors.values())), actor_weight.T, positions], 0), 1
    )
    fulls = [gather(weight, 0) for weight in (qkv_weight, out_weight, up_weight, down_weight)]
    ins = frames | {
        name: full.reshape(weight_shapes[name][0])
        for name, full in zip(weight_shapes, fulls, strict=True)
    }
    ins |= dict(
        positions=packed[7 + slots :].astype(F32),
        small=jnp.pad(packed[0:7].astype(F32), ((0, 1), (0, 0))),
        actor=jnp.pad(packed[7 : 7 + slots], ((0, SLOTS - slots), (0, 0))),
        up_bias=gather(up_bias, 0).astype(F32).reshape(1, hidden_width),
    )
    outs = dict(tokens_grad=((row_count, width), F32)) | grads
    tokens_grad, *sums = run(local_kernel, scale, ins, outs, scratch, flops)
    sums = Names(grads, sums)

    def scatter(array, axis):
        piece = lax.psum_scatter(array, "fsdp", scatter_dimension=axis, tiled=True)
        return lax.psum(piece.astype(BF16), "dp").astype(F32)

    down_sum = jnp.swapaxes(sums.g_down, 3, 4)
    qkv_part, out_part, up_part, down_part = (
        scatter(merged(grad), 0) for grad in (sums.g_qkv, sums.g_out, sums.g_up, down_sum)
    )
    rows = [jnp.sum(sums.g_small, 1), sums.g_actor[:slots], sums.g_positions]
    side = scatter(jnp.concatenate(rows, 0), 1)
    up_bias_part = scatter(jnp.sum(sums.g_up_bias, 0), 0)
    head_total = lax.psum(jnp.sum(sums.head_sums[: SLOTS + 1], 1), ("dp", "fsdp"))
    return (
        head_total[SLOTS] / token_total,
        DECAY_RATE * running + (1.0 - DECAY_RATE) * percentiles,
        tokens_grad,
        side[7 + slots :],
        side[G1],
        side[B1],
        qkv_part,
        out_part,
        side[G2],
        side[B2],
        up_part,
        up_bias_part,
        down_part,
        side[DB],
        side[GL],
        side[BL],
        side[7 : 7 + slots].T,
        head_total[:slots],
    )


def solution(mesh):
    rows, cols, both = P(("dp", "fsdp"), None), P(None, "fsdp"), P(("dp", "fsdp"))
    weight, vector, whole = P("fsdp", None), P("fsdp"), P()
    in_specs = (rows, cols, vector, vector, weight, weight, vector, vector, weight, vector)
    in_specs += (weight, vector, vector, vector, weight, whole, both, rows, both, both, both)
    in_specs += (whole, whole)
    out_specs = (whole, whole, rows, cols, vector, vector, weight, weight, vector, vector)
    out_specs += (weight, vector, weight, vector, vector, vector, weight, whole)
    return jax.shard_map(
        on_device, mesh=mesh, in_specs=in_specs, out_specs=out_specs, check_vma=False
    )
```

```python
import functools
import math
import math

import jax
import jax.numpy as jnp
from jax import lax
from jax.experimental import pallas as pl
from jax.experimental.pallas import tpu as pltpu
from jax.sharding import PartitionSpec as P

HEADS = 8
HEAD = 64
LENGTH = 64
QUAD = 4
WIDE = QUAD * HEAD
MASKED = -1e30
EPSILON = 1e-05
DECAY_RATE = 0.9
ENTROPY_WEIGHT = 0.1
SLOTS = 32
VMEM_BYTES = 63 * 1024 * 1024
BF16 = jnp.bfloat16
F32 = jnp.float32

G1, B1, G2, B2, DB, GL, BL = range(7)
MESH = pl.DeviceIdType.MESH


def dot(left, right, left_dim, right_dim):
    return lax.dot_general(
        left, right, (((left_dim,), (right_dim,)), ((), ())), preferred_element_type=F32
    )


def mean_last(values):
    return jnp.sum(values, -1, keepdims=True) * (1.0 / values.shape[-1])


def normalise(values):
    centred = values - mean_last(values)
    scale = lax.rsqrt(mean_last(centred * centred) + EPSILON)
    return centred * scale, scale


def norm_back(unit, scale, gain, upstream):
    inner = upstream * gain
    return scale * (inner - mean_last(inner) - unit * mean_last(inner * unit))


def fold_rows(values):
    rows, width = values.shape
    return jnp.sum(values.reshape(rows // 8, 8, width), 0)


def gelu_pair(values):
    half = jnp.exp2(values * values * (-0.5 * 1.4426950408889634))
    span = 1.0 + jnp.abs(values) * (0.3275911 * 0.7071067811865476)
    guess = pl.reciprocal(span, approx=True)
    t = guess * (2.0 - span * guess)
    poly = t * (
        0.5 * 0.254829592
        + t
        * (
            0.5 * -0.284496736
            + t * (0.5 * 1.421413741 + t * (0.5 * -1.453152027 + t * (0.5 * 1.061405429)))
        )
    )
    tail = poly * half
    cdf = jnp.where(values < 0.0, tail, 1.0 - tail)
    density = half * 0.3989422804014327
    return values * cdf, cdf + values * density


def pair_masks():
    lane = lax.broadcasted_iota(jnp.int32, (LENGTH, 2 * HEAD), 1)
    first = jnp.where(lane < HEAD, 1.0, 0.0)
    return first.astype(BF16), (1.0 - first).astype(BF16)


def spread_heads(rows, masks):
    zero = jnp.zeros((LENGTH, 2 * HEAD), BF16)
    left, right = rows[:, : 2 * HEAD], rows[:, 2 * HEAD :]
    blocks = [jnp.concatenate([left * mask, zero], 1) for mask in masks]
    blocks += [jnp.concatenate([zero, right * mask], 1) for mask in masks]
    return jnp.concatenate(blocks, 0)


def gather_heads(blocks):
    lane = lax.broadcasted_iota(jnp.int32, (LENGTH, 2 * HEAD), 1)
    pairs = []
    for pair in range(QUAD // 2):
        lanes = slice(pair * 2 * HEAD, (pair + 1) * 2 * HEAD)
        low = 2 * pair * HEAD
        first, second = blocks[low : low + HEAD, lanes], blocks[low + HEAD : low + 2 * HEAD, lanes]
        pairs.append(jnp.where(lane < HEAD, first, second))
    return jnp.concatenate(pairs, 1)


def causal_bias():
    key = lax.broadcasted_iota(jnp.int32, (LENGTH, WIDE), 0)
    query = lax.rem(lax.broadcasted_iota(jnp.int32, (LENGTH, WIDE), 1), HEAD)
    return jnp.where(key <= query, 0.0, MASKED)


LOG2E = 1.4426950408889634
SCORE_SCALE = HEAD ** (-0.5) * LOG2E


def chains(r, i):
    width = r.tokens.shape[1]
    found = []
    for s in range(4):
        row = pl.multiple_of((4 * i + s) * LENGTH, LENGTH)
        for half in range(width // WIDE):
            at = half * WIDE
            columns = [slice(k * width + at, k * width + at + WIDE) for k in range(3)]
            found.append((4 * i + s, pl.ds(row, LENGTH), columns))
    return found


def attend_group(r, i):
    masks, bias = pair_masks(), r.causal[...]
    group = chains(r, i)
    scores = [
        dot(r.qkv[rows, k], spread_heads(r.qkv[rows, q], masks), 1, 1)
        for _, rows, (q, k, _) in group
    ]
    probs = []
    for (seq, _, (q, _, _)), score in zip(group, scores, strict=True):
        score = score * SCORE_SCALE + bias
        highest = jnp.max(score, 0, keepdims=True)
        weights = jnp.exp2(score - highest)
        summed = jnp.sum(weights, 0, keepdims=True)
        probs.append((weights * (1.0 / summed)).astype(BF16))
        r.totals[pl.ds(seq, 1), q] = highest + jnp.log(summed) * LOG2E
    blocks = [
        dot(prob, r.qkv[rows, v], 0, 0) for (_, rows, (_, _, v)), prob in zip(group, probs, strict=True)
    ]
    for (_, rows, (q, _, _)), block in zip(group, blocks, strict=True):
        r.attended[rows, q] = gather_heads(block).astype(BF16)


def attend_back_group(r, i):
    masks, bias = pair_masks(), r.causal[...]
    done = []
    for half in range(2):
        group = chains(r, i)[half::2]
        queries = [spread_heads(r.qkv[rows, q], masks) for _, rows, (q, _, _) in group]
        aboves = [spread_heads(r.attended[rows, q], masks) for _, rows, (q, _, _) in group]
        scores = [
            dot(r.qkv[rows, k], query, 1, 1)
            for (_, rows, (_, k, _)), query in zip(group, queries, strict=True)
        ]
        prob_grads = [
            dot(r.qkv[rows, v], above, 1, 1)
            for (_, rows, (_, _, v)), above in zip(group, aboves, strict=True)
        ]
        probs, score_grads = [], []
        for (seq, _, (q, _, _)), score, pull in zip(group, scores, prob_grads, strict=True):
            prob = jnp.exp2(score * SCORE_SCALE + bias - r.totals[pl.ds(seq, 1), q])
            row_terms = jnp.sum(pull * prob, 0, keepdims=True)
            score_grads.append((prob * (pull - row_terms)).astype(BF16))
            probs.append(prob.astype(BF16))
        value_grads = [dot(prob, above, 1, 0) for prob, above in zip(probs, aboves, strict=True)]
        key_grads = [dot(grad, query, 1, 0) for grad, query in zip(score_grads, queries, strict=True)]
        query_grads = [
            dot(grad, r.qkv[rows, k], 0, 0)
            for (_, rows, (_, k, _)), grad in zip(group, score_grads, strict=True)
        ]
        for (_, rows, (q, k, v)), dq, dk, dv in zip(
            group, query_grads, key_grads, value_grads, strict=True
        ):
            done.append((rows, q, (gather_heads(dq) * HEAD ** (-0.5)).astype(BF16)))
            done.append((rows, k, (dk * HEAD ** (-0.5)).astype(BF16)))
            done.append((rows, v, dv.astype(BF16)))
    for rows, columns, grad in done:
        r.qkv[rows, columns] = grad


def policy(logits, masks, actions, advantage, scale):
    allowed = masks > 0
    held = jnp.where(allowed, logits, MASKED)
    shifted = held - jnp.max(held, 0, keepdims=True)
    weights = jnp.exp(shifted)
    summed = jnp.sum(weights, 0, keepdims=True)
    log_probs = shifted - jnp.log(summed)
    probs = weights * (1.0 / summed)
    plogp = jnp.where(allowed, probs * log_probs, 0.0)
    entropy = -jnp.sum(plogp, 0, keepdims=True)
    slot = lax.broadcasted_iota(jnp.int32, logits.shape, 0)
    taken = slot == actions
    chosen = jnp.sum(jnp.where(taken, log_probs, 0.0), 0, keepdims=True)
    loss = -advantage * chosen - ENTROPY_WEIGHT * entropy
    pull = advantage * (probs - jnp.where(taken, 1.0, 0.0)) + ENTROPY_WEIGHT * (
        plogp + probs * entropy
    )
    return loss, jnp.where(allowed, pull * scale, 0.0)


STRIP = 32
THIN = 16
LARGE = 1 << 20


class Names:
    def __init__(self, names, refs):
        self.table = dict(zip(names, refs, strict=True))

    def __getattr__(self, name):
        return self.table[name]


SPLIT = (4, 2, 2)
PACK_ROWS = 48
PACK_GRAD_ROWS = 40
POSITION_AT, SMALL_AT, BIAS_AT, LOSS_AT = 0, 64, 96, 97


def merged(block):
    return block.reshape(-1, block.shape[-1])


def start_rows(r, row, at):
    frame = at % LENGTH
    start = r.tokens[pl.ds(pl.multiple_of(row + at, STRIP), STRIP), :].astype(F32)
    return start + r.positions[frame : frame + STRIP, :]


def norm_pass(r):
    count = r.tokens.shape[0]
    rows = 4 * LENGTH

    def body(i, carry):
        row = pl.multiple_of(i * rows, rows)
        for at in range(0, rows, STRIP):
            unit, _ = normalise(start_rows(r, row, at))
            normed = unit * r.small[G1 : G1 + 1, :] + r.small[B1 : B1 + 1, :]
            r.attended[pl.ds(pl.multiple_of(row + at, STRIP), STRIP), :] = normed.astype(BF16)
        r.normed_t[:, pl.ds(row, rows)] = r.attended[pl.ds(row, rows), :].T
        return carry

    lax.fori_loop(0, count // rows, body, 0)


def front(r, pump):
    count, width = r.tokens.shape
    rows = 4 * LENGTH

    def body(i, carry):
        pump(i)
        row = pl.multiple_of(i * rows, rows)
        normed = r.attended[pl.ds(row, rows), :]
        for at in range(0, 3 * width, width):
            r.qkv[pl.ds(row, rows), at : at + width] = dot(
                normed, merged(r.w_qkv[:, :, :, :, at : at + width]), 1, 0
            ).astype(BF16)
        attend_group(r, i)
        return carry

    lax.fori_loop(0, count // rows, body, 0)


def add_grad(ref, index, values):
    ref[index] += values.reshape(ref[index].shape)


def add_columns(ref, values):
    count = ref.shape[-1]
    for k in range(values.shape[1] // count):
        ref[k // 2, k % 2] += values[:, k * count : (k + 1) * count]


def clear(r):
    for ref in (r.g_out, r.g_up, r.g_down):

        def body(z, carry, ref=ref):
            ref[z] = jnp.zeros(ref.shape[1:], F32)
            return carry

        lax.fori_loop(0, ref.shape[0], body, 0)
    for ref in (r.g_actor, r.g_small, r.g_up_bias, r.g_positions, r.head_sums):
        ref[...] = jnp.zeros_like(ref)


def frame_values(r):
    r.causal[...] = causal_bias()
    fresh = DECAY_RATE * r.running[...] + (1.0 - DECAY_RATE) * r.percentiles[...]
    spread = jnp.maximum(1.0, fresh[1:2, :] - fresh[0:1, :])
    seqs = r.game_ids.shape[0]
    game = r.game_ids[...].reshape(seqs, 1)
    slot = lax.broadcasted_iota(jnp.int32, (seqs, spread.shape[1]), 1)
    column = jnp.sum(jnp.where(slot == game, spread, 0.0), 1, keepdims=True)
    count = 8 * LENGTH
    owner = lax.broadcasted_iota(jnp.int32, (8, count), 0)
    frame = lax.broadcasted_iota(jnp.int32, (8, count), 1)
    for k in range(seqs // 8):
        here = slice(k * count, (k + 1) * count)
        near = jnp.where(frame // LENGTH == owner, column[8 * k : 8 * k + 8], 0.0)
        wide = jnp.sum(near, 0, keepdims=True)
        r.advantage[:, here] = (r.returns[here] - r.values[here]).reshape(1, count) / wide
        r.action_row[:, here] = r.actions[here].reshape(1, count)


class Tile:
    def __init__(self, r, side):
        def pick(name):
            return r.table[name, side]

        self.active, self.slope = pick("active"), pick("slope")
        self.two_t, self.unit, self.last = pick("two_t"), pick("unit"), pick("last")
        self.scale = pick("scale")


def middle_part(r, scale, arrive):
    count, width = r.tokens.shape
    rows = r.low.shape[0]
    shards = r.w_up.shape[0]
    chunk = r.w_up.shape[-1] // shards
    slots = r.masks.shape[0]
    out_weight = r.w_out
    head_bias = jnp.concatenate(
        [r.actor_bias[...].astype(F32).reshape(slots, 1), jnp.zeros((SLOTS - slots, 1), F32)], 0
    )
    everything = slice(None)
    strips = [slice(at, at + STRIP) for at in range(0, rows, STRIP)]

    def gain(k):
        return r.small[k : k + 1, :]

    def tile_rows(i):
        return pl.ds(pl.multiple_of(i * rows, rows), rows)

    def project(i):
        return dot(r.attended[tile_rows(i), :], merged(out_weight[...]), 1, 0)

    def before(i, t, projected):
        row = pl.multiple_of(i * rows, rows)
        for strip in strips:
            mid = start_rows(r, row, strip.start) + projected[strip]
            unit, spread = normalise(mid)
            r.two_low[strip, :] = (unit * gain(G2) + gain(B2)).astype(BF16)
            t.unit[strip, :] = unit
            t.scale[strip, :] = spread
            t.last[strip, :] = mid + gain(DB)
        t.two_t[...] = r.two_low[...].T

    def columns(j):
        return pl.ds(pl.multiple_of(j * chunk, chunk), chunk)

    def up_weight(j):
        return merged(r.w_up[:, :, :, :, columns(j)])

    def activate(j, t, hidden):
        cols = columns(j)
        bias = r.up_bias[:, cols]
        for at in range(0, rows, THIN):
            value, derivative = gelu_pair(hidden[at : at + THIN] + bias)
            t.active[at : at + THIN, cols] = value.astype(BF16)
            t.slope[at : at + THIN, cols] = derivative.astype(BF16)

    def forward_only(j, t):
        activate(j, t, dot(r.two_low[...], up_weight(j), 1, 0))
        t.last[...] += dot(t.active[:, columns(j)], merged(r.w_down[j]), 1, 0)

    def both_ways(j, here, there):
        cols = columns(j)
        if there is not None:
            hidden = dot(r.two_low[...], up_weight(j), 1, 0)
        hidden_grad = dot(r.low[...], merged(r.w_down[j]), 1, 1)
        add_columns(r.g_down.at[j], dot(r.low_t[...], here.active[:, cols], 1, 0))
        total = r.g_up_bias[:, cols]
        for at in range(0, rows, THIN):
            strip = slice(at, at + THIN)
            part = (hidden_grad[strip] * here.slope[strip, cols].astype(F32)).astype(BF16)
            r.hidden_grad[strip, :] = part
            total += fold_rows(part.astype(F32))
        r.g_up_bias[:, cols] = total
        r.two_in[...] += dot(r.hidden_grad[...], up_weight(j), 1, 1)
        add_grad(
            r.g_up,
            (everything, everything, everything, everything, cols),
            dot(here.two_t[...], r.hidden_grad[...], 1, 0),
        )
        if there is not None:
            activate(j, there, hidden)
            there.last[...] += dot(there.active[:, cols], merged(r.w_down[j]), 1, 0)

    def last_norm(i, t):
        for strip in strips:
            unit, spread = normalise(t.last[strip, :])
            r.low[strip, :] = (unit * gain(GL) + gain(BL)).astype(BF16)
            t.last[strip, :] = unit
            r.scale_last[strip, :] = spread
        return dot(r.actor[...], r.low[...], 1, 1) + head_bias

    def head(i, logits):
        here = tile_rows(i)
        masks = jnp.concatenate(
            [r.masks[:, here], jnp.zeros((SLOTS - slots, rows), jnp.int32)], 0
        )
        loss, pull = policy(logits, masks, r.action_row[:, here], r.advantage[:, here], scale)
        logit_grad = pull.astype(BF16)
        last_in = dot(logit_grad, r.actor[...], 0, 0)
        r.g_actor[...] += dot(logit_grad, r.low[...], 1, 0)
        wide_grad = logit_grad.astype(F32)
        fold = r.head_sums[0:SLOTS, :]
        for at in range(0, rows, 128):
            fold += wide_grad[:, at : at + 128]
        r.head_sums[0:SLOTS, :] = fold
        fold = r.head_sums[SLOTS : SLOTS + 1, :]
        for at in range(0, rows, 128):
            fold += loss[:, at : at + 128]
        r.head_sums[SLOTS : SLOTS + 1, :] = fold
        return last_in

    def last_norm_back(t, last_in):
        sums = [r.g_small[k] for k in (GL, BL, DB)]
        for strip in strips:
            above, unit = last_in[strip], t.last[strip, :]
            grad = norm_back(unit, r.scale_last[strip, :], gain(GL), above)
            sums[0] += fold_rows(above * unit)
            sums[1] += fold_rows(above)
            sums[2] += fold_rows(grad)
            t.last[strip, :] = grad
            r.low[strip, :] = grad.astype(BF16)
        for k, total in zip((GL, BL, DB), sums, strict=True):
            r.g_small[k] = total
        r.low_t[...] = r.low[...].T
        r.two_in[...] = jnp.zeros((rows, width), F32)

    def two_norm_back(i, t):
        row = pl.multiple_of(i * rows, rows)
        sums = [r.g_small[k] for k in (G2, B2)]
        for strip in strips:
            above, unit = r.two_in[strip, :], t.unit[strip, :]
            sums[0] += fold_rows(above * unit)
            sums[1] += fold_rows(above)
            grad = t.last[strip, :] + norm_back(unit, t.scale[strip, :], gain(G2), above)
            r.middle_grad[pl.ds(pl.multiple_of(row + strip.start, STRIP), STRIP), :] = grad
            r.middle_low[strip, :] = grad.astype(BF16)
        for k, total in zip((G2, B2), sums, strict=True):
            r.g_small[k] = total

    def out_back(i):
        here = tile_rows(i)
        add_grad(r.g_out, ..., dot(r.attended[here, :], r.middle_low[...], 0, 0))
        r.attended[here, :] = dot(r.middle_low[...], merged(out_weight[...]), 1, 1).astype(BF16)

    sides = [Tile(r, 0), Tile(r, 1)]
    tiles = count // rows

    def chunks(step):
        def body(j, carry):
            step(j)
            return carry

        lax.fori_loop(0, shards, body, 0)

    def step(i, side, first=False, last=False):
        here, there = sides[side], sides[1 - side]
        projected = None if last else project(i + 1)
        logits = last_norm(i, here)
        if not first:
            two_norm_back(i - 1, there)
        last_in = head(i, logits)
        if not last:
            before(i + 1, there, projected)
        last_norm_back(here, last_in)
        if not first:
            out_back(i - 1)
        chunks(lambda j: both_ways(j, here, None if last else there))

    before(0, sides[0], project(0))
    arrive()
    chunks(lambda j: forward_only(j, sides[0]))
    step(0, 0, first=True)

    def pair(p, carry):
        step(2 * p + 1, 1)
        step(2 * p + 2, 0)
        return carry

    lax.fori_loop(0, (tiles - 2) // 2, pair, 0)
    step(tiles - 1, 1, last=True)
    two_norm_back(tiles - 1, sides[1])
    out_back(tiles - 1)


def attend_back(r, pump):
    count = r.tokens.shape[0]
    rows = 4 * LENGTH

    def body(i, carry):
        pump(i)
        attend_back_group(r, i)
        return carry

    lax.fori_loop(0, count // rows, body, 0)


def qkv_weight_grad(r, third):
    width = r.tokens.shape[1]
    step = width // 2
    for at in range(third * width, (third + 1) * width, step):
        values = dot(r.normed_t[...], r.qkv[:, at : at + step], 1, 0)
        r.g_qkv[:, :, :, :, at : at + step] = values.reshape(r.g_qkv.shape[:4] + (step,))


def start_back(r, pump, tile_done):
    count = r.tokens.shape[0]
    rows = 4 * LENGTH
    gain = r.small[G1 : G1 + 1, :]

    def body(i, carry):
        pump(i)
        row = pl.multiple_of(i * rows, rows)
        one_in = dot(r.qkv[pl.ds(row, rows), :], merged(r.w_qkv[...]), 1, 1)
        sums = [r.g_small[k] for k in (G1, B1)]
        for at in range(0, rows, STRIP):
            there = pl.ds(pl.multiple_of(row + at, STRIP), STRIP)
            unit, scale = normalise(start_rows(r, row, at))
            above = one_in[at : at + STRIP]
            sums[0] += fold_rows(above * unit)
            sums[1] += fold_rows(above)
            grad = r.middle_grad[there, :] + norm_back(unit, scale, gain, above)
            r.middle_grad[there, :] = grad
            frame = at % LENGTH
            r.g_positions[frame : frame + STRIP, :] += grad
        for k, total in zip((G1, B1), sums, strict=True):
            r.g_small[k] = total
        tile_done(i)
        return carry

    lax.fori_loop(0, count // rows, body, 0)


def pack_shards(r):
    part = r.positions_in.shape[0]
    slots = r.masks.shape[0]
    rows = [
        ref[...].astype(F32).reshape(1, part)
        for ref in (r.gain1, r.bias1, r.gain2, r.bias2, r.bias_down, r.gain3, r.bias3)
    ]
    rows += [r.actor_in[...].astype(F32), jnp.zeros((32 - 7 - slots, part), F32)]
    features = jnp.concatenate(
        [r.positions_in[...].astype(F32), jnp.concatenate(rows, 0).T, jnp.zeros((part, 32), F32)], 1
    )
    bias = r.up_bias_in[...].astype(F32).reshape(1, 128)
    packed = jnp.concatenate([features, bias, jnp.zeros((PACK_ROWS - part - 1, 128), F32)], 0)
    r.pack_own[...] = packed.astype(BF16)


def unpack_shards(r):
    slots = r.masks.shape[0]
    blocks = r.pack[...].astype(F32).reshape(-1, PACK_ROWS, 128)
    part = r.positions_in.shape[0]
    features = merged(blocks[:, :part, :]).T
    r.positions[...] = features[POSITION_AT : POSITION_AT + LENGTH]
    small = features[SMALL_AT : SMALL_AT + 32]
    r.small[...] = small[0:8]
    width = small.shape[1]
    r.actor[...] = jnp.concatenate(
        [small[7 : 7 + slots], jnp.zeros((SLOTS - slots, width), F32)], 0
    ).astype(BF16)
    r.up_bias[...] = jnp.concatenate(
        [blocks[f, part : part + 1, :] for f in range(blocks.shape[0])], 1
    )


def small_rows(r):
    slots = r.masks.shape[0]
    rows = [jnp.sum(r.g_small[k], 0, keepdims=True) for k in range(7)]
    return jnp.concatenate(
        rows + [r.g_actor[0:slots, :], jnp.zeros((32 - 7 - slots, rows[0].shape[1]), F32)], 0
    )


def pack_grads(r):
    width = r.tokens.shape[1]
    part = r.positions_in.shape[0]
    features = jnp.concatenate(
        [r.g_positions[...], small_rows(r), jnp.zeros((128 - SMALL_AT - 32, width), F32)], 0
    ).T
    sums = jnp.sum(r.head_sums[0 : SLOTS + 8, :], 1, keepdims=True)
    lane = lax.broadcasted_iota(jnp.int32, (part, 128), 1)
    bias = jnp.sum(r.g_up_bias[...], 0, keepdims=True)
    shape = r.g_pack.shape
    for f in range(width // part):
        block = features[f * part : (f + 1) * part]
        block = jnp.where(lane == BIAS_AT, sums[0:SLOTS], block)
        block = jnp.where(lane == LOSS_AT, sums[SLOTS : SLOTS + 1], block)
        owner = (f // 4, f // 2 % 2, f % 2)
        rows = [block, bias[:, f * 128 : (f + 1) * 128], jnp.zeros((shape[3] - part - 1, 128), F32)]
        r.g_pack[owner] = jnp.concatenate(rows, 0)


GATHERS = 9
REDUCES = (
    (128, 512, BF16, False),
    (2048, 32, BF16, True),
    (512, 32, BF16, True),
    (512, 32, BF16, False),
    (512, 32, BF16, False),
    (512, 32, BF16, True),
    (128, PACK_GRAD_ROWS, F32, False),
)


class Place:
    def __init__(self):
        self.x = lax.axis_index("dp")
        f = lax.axis_index("fsdp")
        self.z, self.y, self.c = f // 4, f // 2 % 2, f % 2

    def at(self, x=None, z=None, y=None, c=None):
        pick = lambda new, old: old if new is None else new
        f = pick(z, self.z) * 4 + pick(y, self.y) * 2 + pick(c, self.c)
        return (pick(x, self.x), f)

    def z_partner(self, k):
        return (self.z + 1 - 2 * (self.z % 2), (self.z + 2) % 4, 3 - self.z)[k]

    def partners(self):
        return [self.at(z=self.z_partner(k)) for k in range(3)] + [
            self.at(y=1 - self.y),
            self.at(c=1 - self.c),
            self.at(x=1 - self.x),
        ]


def remote(r_send, r_recv, index):
    def copy(src, dst, k, device):
        return pltpu.make_async_remote_copy(
            src_ref=src,
            dst_ref=dst,
            send_sem=r_send.at[index, k],
            recv_sem=r_recv.at[index, k],
            device_id=device,
            device_id_type=MESH,
        )

    return copy


class Gather:
    def __init__(self, r, place, index, full, own, at, count, halved=False):
        p = place
        copy = remote(r.gather_send, r.gather_recv, index)
        cols = part = slice(at, at + count)
        if halved:
            part = pl.ds(pl.multiple_of(at + p.x * (count // 2), 128), count // 2)
        self.full, self.own, self.part, self.place = full, own, part, place
        mine = full.at[p.z, p.y, p.c, :, part]
        self.z = [copy(own.at[:, part], mine, k, p.at(z=p.z_partner(k))) for k in range(3)]
        line = full.at[:, p.y, p.c, :, part]
        self.y = copy(line, line, 3, p.at(y=1 - p.y))
        plane = full.at[:, :, p.c, :, part]
        self.x = copy(plane, plane, 4, p.at(x=1 - p.x)) if halved else None
        plane = full.at[:, :, p.c, :, cols]
        self.c = copy(plane, plane, 5, p.at(c=1 - p.c))

    def start_z(self):
        for copy in self.z:
            copy.start()
        p = self.place
        self.full[p.z, p.y, p.c, :, self.part] = self.own[:, self.part]

    def start_y(self):
        for copy in self.z:
            copy.wait_recv()
        self.y.start()

    def start_x(self):
        self.y.wait_recv()
        self.x.start()

    def start_c(self):
        (self.y if self.x is None else self.x).wait_recv()
        self.c.start()

    def ready(self):
        self.c.wait_recv()

    def close(self):
        for copy in self.z + [self.y, self.c] + ([] if self.x is None else [self.x]):
            copy.wait_send()


class Reduce:
    def __init__(self, r, place, index, grad, at=0):
        count, _, kind, halved = REDUCES[index]
        self.grad, self.place, self.kind, self.halved = grad, place, kind, halved
        p = place
        copy = remote(r.reduce_send, r.reduce_recv, index)
        self.cols = slice(at, at + count)
        self.buffers = [r.table[index, part] for part in range(len(reduce_leads(halved)))]
        sc, rc, ry, rz, rx = self.buffers[:5]
        keep = count
        self.part = self.cols
        if halved:
            keep = count // 2
            self.part = self.half(at, keep, p.x)
            self.away = self.half(at, keep, 1 - p.x)
            self.local, self.local_away = self.half(0, keep, p.x), self.half(0, keep, 1 - p.x)
            self.sx1 = sc.at[:, :, :, 0:keep]
            self.x1 = copy(self.sx1, self.buffers[5], 6, p.at(x=1 - p.x))
        tail = slice(count - keep, count)
        self.sy = sc.at[:, 0, :, tail]
        self.sz = [sc.at[k, 1, :, tail] for k in range(3)]
        self.sx = sc.at[3, 1, :, tail]
        self.c = copy(sc, rc, 0, p.at(c=1 - p.c))
        self.y = copy(self.sy, ry, 1, p.at(y=1 - p.y))
        self.z = [copy(self.sz[k], rz.at[k], 2 + k, p.at(z=p.z_partner(k))) for k in range(3)]
        self.x = copy(self.sx, rx, 5, p.at(x=1 - p.x))

    @staticmethod
    def half(at, keep, x):
        return pl.ds(pl.multiple_of(at + x * keep, 128), keep)

    def start_c(self):
        sc, p = self.buffers[0], self.place

        def body(z, carry):
            sc[z] = self.grad[z, :, 1 - p.c, :, self.cols].astype(self.kind)
            return carry

        lax.fori_loop(0, 4, body, 0)
        self.c.start()

    def start_x1(self):
        rc, p = self.buffers[1], self.place
        self.c.wait()

        def body(z, carry):
            away = self.grad[z, :, p.c, :, self.away] + rc[z, :, :, self.local_away].astype(F32)
            self.sx1[z] = away.astype(self.kind)
            self.grad[z, :, p.c, :, self.part] += rc[z, :, :, self.local].astype(F32)
            return carry

        lax.fori_loop(0, 4, body, 0)
        self.x1.start()

    def start_y(self):
        p = self.place
        if self.halved:
            held = self.buffers[5]
            self.x1.wait_recv()
        else:
            held = self.buffers[1]
            self.c.wait()

        def body(z, carry):
            away = self.grad[z, 1 - p.y, p.c, :, self.part] + held[z, 1 - p.y].astype(F32)
            self.sy[z] = away.astype(self.kind)
            self.grad[z, p.y, p.c, :, self.part] += held[z, p.y].astype(F32)
            return carry

        lax.fori_loop(0, 4, body, 0)
        self.y.start()

    def start_z(self):
        ry, p = self.buffers[2], self.place
        self.y.wait_recv()
        for k in (2, 1, 0):
            owner = p.z_partner(k)
            away = self.grad[owner, p.y, p.c, :, self.part] + ry[owner].astype(F32)
            self.sz[k][...] = away.astype(self.kind)
            self.z[k].start()
        self.grad[p.z, p.y, p.c, :, self.part] += ry[p.z].astype(F32)

    def start_x(self):
        rz, p = self.buffers[3], self.place
        for copy in self.z:
            copy.wait_recv()
        near = self.grad[p.z, p.y, p.c, :, self.part] + rz[0].astype(F32)
        self.sx[...] = (near + (rz[1].astype(F32) + rz[2].astype(F32))).astype(self.kind)
        self.x.start()

    def finish(self, out):
        rx = self.buffers[4]
        self.x.wait_recv()
        if self.halved:
            out[:, self.part] = self.sx[...].astype(F32)
            out[:, self.away] = rx[...].astype(F32)
        else:
            out[:, self.cols] = self.sx[...].astype(F32) + rx[...].astype(F32)

    def close(self):
        for copy in self.z + [self.y, self.x] + ([self.x1] if self.halved else []):
            copy.wait_send()


def reduce_leads(halved):
    leads = [((4, 2), False), ((4, 2), False), ((4,), halved), ((3,), halved), ((), halved)]
    return leads + ([((4, 2), True)] if halved else [])


def layer_scratch(row_count, width, hidden_width, shards):
    tile = 256
    seqs = row_count // LENGTH
    pairs = dict(
        active=((tile, hidden_width), BF16),
        slope=((tile, hidden_width), BF16),
        two_t=((width, tile), BF16),
        unit=((tile, width), F32),
        last=((tile, width), F32),
        scale=((tile, 1), F32),
    )
    both = {(name, side): item for name, item in pairs.items() for side in range(2)}
    return both | dict(
        tokens=((row_count, width), BF16),
        middle_grad=((row_count, width), F32),
        normed_t=((width, row_count), BF16),
        qkv=((row_count, 3 * width), BF16),
        attended=((row_count, width), BF16),
        totals=((seqs, width), F32),
        causal=((LENGTH, WIDE), F32),
        advantage=((1, row_count), F32),
        action_row=((1, row_count), jnp.int32),
        two_low=((tile, width), BF16),
        low=((tile, width), BF16),
        low_t=((width, tile), BF16),
        middle_low=((tile, width), BF16),
        hidden_grad=((tile, hidden_width // 4), BF16),
        two_in=((tile, width), F32),
        scale_last=((tile, 1), F32),
        local_sem=pltpu.SemaphoreType.DMA((2,)),
    )


def grad_shapes(width, hidden_width, shards):
    split = SPLIT
    part, hidden_part = width // shards, hidden_width // shards
    return dict(
        g_qkv=(split + (part, 3 * width), F32),
        g_out=(split + (part, width), F32),
        g_up=(split + (part, hidden_width), F32),
        g_down=(split + (width, hidden_part), F32),
        g_actor=((SLOTS, width), F32),
        g_small=((7, 8, width), F32),
        g_up_bias=((8, hidden_width), F32),
        g_positions=((LENGTH, width), F32),
        head_sums=((SLOTS + 8, 128), F32),
    )


def at_step(i, table):
    for step, actions in table.items():

        @pl.when(i == step)
        def _(actions=actions):
            for action in actions:
                action()


def spread_kernel(names, scale, *refs):
    r = Names(names, refs)
    place = Place()
    load = pltpu.make_async_copy(r.tokens_in, r.tokens, r.local_sem.at[0])
    load.start()
    partners = place.partners()
    barrier = pltpu.get_barrier_semaphore()
    for device in partners:
        pl.semaphore_signal(barrier, inc=1, device_id=device, device_id_type=MESH)
    pack_shards(r)
    pl.semaphore_wait(barrier, len(partners))
    width, hidden_width = r.w_out.shape[-1], r.w_up.shape[-1]
    plan = [(r.pack, r.pack_own, 0, 128)]
    plan += [(r.w_qkv, r.qkv_in, k * width, width) for k in range(3)]
    plan += [(r.w_out, r.out_in, 0, width)]
    half = hidden_width // 2
    plan += [(r.w_up, r.up_in, k * half, half, True) for k in range(2)]
    plan += [(r.w_down, r.down_in, k * width // 2, width // 2, True) for k in range(2)]
    gathers = [Gather(r, place, k, *item) for k, item in enumerate(plan)]
    pack, q, k, v, out, up0, up1, down0, down1 = gathers
    pack.start_z()
    q.start_z()
    k.start_z()
    v.start_z()
    pack.start_y()
    q.start_y()
    pack.start_c()
    clear(r)
    frame_values(r)
    pack.ready()
    unpack_shards(r)
    k.start_y()
    q.start_c()
    load.wait()
    out.start_z()
    up0.start_z()
    norm_pass(r)
    v.start_y()
    k.start_c()
    up1.start_z()
    down0.start_z()
    down1.start_z()
    v.start_c()
    for group in (q, k, v):
        group.ready()

    front(
        r,
        lambda i: at_step(
            i,
            {
                1: [out.start_y],
                3: [up0.start_y, out.start_c],
                5: [up1.start_y, up0.start_x],
                7: [down0.start_y, up1.start_x, up0.start_c],
                9: [down1.start_y, down0.start_x, up1.start_c],
            },
        ),
    )
    out.ready()

    def arrive():
        down1.start_x()
        down0.start_c()
        down1.start_c()
        for group in (up0, up1, down0, down1):
            group.ready()

    middle_part(r, scale, arrive)

    plan = [(r.g_down,), (r.g_up,), (r.g_out,)]
    plan += [(r.g_qkv, k * width) for k in range(3)] + [(r.g_pack,)]
    reduces = [Reduce(r, place, k, *item) for k, item in enumerate(plan)]
    down, up, out, q, k, v, pack = reduces
    down.start_c()
    up.start_c()
    out.start_c()
    attend_back(
        r,
        lambda i: at_step(
            i,
            {
                1: [down.start_y, up.start_x1],
                2: [out.start_x1],
                6: [down.start_z, up.start_y],
                7: [out.start_y],
                9: [up.start_z],
            },
        ),
    )
    qkv_weight_grad(r, 0)
    q.start_c()
    qkv_weight_grad(r, 2)
    v.start_c()
    q.start_y()
    qkv_weight_grad(r, 1)
    k.start_c()
    v.start_x1()
    out.start_z()
    k.start_y()

    def stored(i):
        rows = pl.ds(pl.multiple_of(i * 4 * LENGTH, 4 * LENGTH), 4 * LENGTH)
        return pltpu.make_async_copy(
            r.middle_grad.at[rows, :], r.tokens_grad.at[rows, :], r.store_sem.at[i]
        )

    start_back(
        r,
        lambda i: at_step(
            i,
            {
                2: [down.start_x],
                3: [up.start_x, q.start_z],
                5: [v.start_y, out.start_x],
                6: [k.start_z],
                8: [v.start_z, q.start_x],
            },
        ),
        lambda i: stored(i).start(),
    )
    pack_grads(r)
    pack.start_c()
    k.start_x()
    v.start_x()
    pack.start_y()
    down.finish(r.down_out)
    up.finish(r.up_out)
    pack.start_z()
    out.finish(r.out_out)
    for group in (q, k, v):
        group.finish(r.qkv_out)
    pack.start_x()
    for i in range(r.middle_grad.shape[0] // (4 * LENGTH)):
        stored(i).wait()
    for group in gathers + reduces:
        group.close()
    pack.finish(r.pack_out)


def finish_kernel(names, count, *refs):
    r = Names(names, refs)
    step = 4 * LENGTH
    parts = [pl.ds(at, step) for at in range(0, r.tokens.shape[0], step)]
    loads = [
        pltpu.make_async_copy(r.tokens.at[part, :], r.held.at[part, :], r.load_sem.at[k])
        for k, part in enumerate(parts)
    ]
    stores = [
        pltpu.make_async_copy(r.held.at[part, :], r.o_tokens.at[part, :], r.store_sem.at[k])
        for k, part in enumerate(parts)
    ]
    for load in loads:
        load.start()
    r.o_qkv[...] = r.qkv[...]
    r.o_out[...] = r.out[...]
    r.o_up[...] = r.up[...]
    r.o_down[...] = r.down[...].T
    r.o_stats[...] = DECAY_RATE * r.running[...] + (1.0 - DECAY_RATE) * r.percentiles[...]
    part, positions = r.o_positions.shape
    slots = r.o_actor.shape[0]
    features = r.pack[0:part, :]
    r.o_positions[...] = features[:, POSITION_AT : POSITION_AT + positions]
    turned = features.T
    vectors = (r.gain1, r.bias1, r.gain2, r.bias2, r.bias_down, r.gain3, r.bias3)
    for k, ref in enumerate(vectors):
        ref[...] = turned[SMALL_AT + k : SMALL_AT + k + 1, :].reshape(part)
    r.o_actor[...] = turned[SMALL_AT + 7 : SMALL_AT + 7 + slots, :]
    r.o_actor_bias[...] = turned[BIAS_AT : BIAS_AT + 1, :].reshape(part)[0:slots]
    r.o_loss[...] = features[0:1, LOSS_AT : LOSS_AT + 1] * (1.0 / count)
    r.o_up_bias[...] = r.pack[part : part + 1, :].reshape(128)
    for load, store in zip(loads, stores, strict=True):
        load.wait()
        store.start()
    for store in stores:
        store.wait()


def local_kernel(names, scale, *refs):
    r = Names(names, refs)
    load = pltpu.make_async_copy(r.tokens_in, r.tokens, r.local_sem.at[0])
    load.start()
    clear(r)
    frame_values(r)
    load.wait()
    norm_pass(r)
    front(r, lambda i: None)
    middle_part(r, scale, lambda: None)
    attend_back(r, lambda i: None)
    for third in range(3):
        qkv_weight_grad(r, third)
    start_back(r, lambda i: None, lambda i: None)
    store = pltpu.make_async_copy(r.middle_grad, r.tokens_grad, r.local_sem.at[1])
    store.start()
    store.wait()


def run(kernel, constant, ins, outs, scratch, flops=0, side_effects=False, collective=None):
    vmem = pl.BlockSpec(memory_space=pltpu.VMEM)
    anywhere = pl.BlockSpec(memory_space=pl.ANY)
    in_specs = [anywhere if array.size > LARGE else vmem for array in ins.values()]
    out_specs = [anywhere if math.prod(shape) > LARGE else vmem for shape, _ in outs.values()]
    return pl.pallas_call(
        functools.partial(kernel, (*ins, *outs, *scratch), constant),
        out_shape=[jax.ShapeDtypeStruct(shape, kind) for shape, kind in outs.values()],
        in_specs=in_specs,
        out_specs=out_specs,
        scratch_shapes=[
            item if not isinstance(item, tuple) else pltpu.VMEM(item[0], item[1])
            for item in scratch.values()
        ],
        compiler_params=pltpu.CompilerParams(
            vmem_limit_bytes=VMEM_BYTES, has_side_effects=side_effects, collective_id=collective
        ),
        cost_estimate=pl.CostEstimate(flops=flops, bytes_accessed=1 << 24, transcendentals=0),
    )(*ins.values())


def on_device(
    tokens,
    positions,
    norm_one_gain,
    norm_one_bias,
    qkv_weight,
    out_weight,
    norm_two_gain,
    norm_two_bias,
    up_weight,
    up_bias,
    down_weight,
    down_bias,
    final_gain,
    final_bias,
    actor_weight,
    actor_bias,
    actions,
    action_masks,
    game_ids,
    returns,
    values,
    running,
    percentiles,
):
    row_count, width = tokens.shape
    seq_count = row_count // LENGTH
    hidden_width = up_weight.shape[1]
    slots = actor_weight.shape[1]
    fsdp = lax.axis_size("fsdp")
    device_count = lax.axis_size("dp") * fsdp
    token_total = row_count * device_count
    scale = float(seq_count * device_count) / token_total
    flops = 6 * row_count * width * (4 * width + 2 * hidden_width)
    part, hidden_part = width // fsdp, hidden_width // fsdp

    vectors = dict(
        gain1=norm_one_gain,
        bias1=norm_one_bias,
        gain2=norm_two_gain,
        bias2=norm_two_bias,
        bias_down=down_bias,
        gain3=final_gain,
        bias3=final_bias,
    )
    stats = dict(running=running, percentiles=percentiles)
    frames = stats | dict(
        tokens_in=tokens,
        actor_bias=actor_bias,
        actions=actions,
        masks=action_masks.T,
        game_ids=game_ids,
        returns=returns,
        values=values,
    )
    scratch = layer_scratch(row_count, width, hidden_width, 16)
    grads = grad_shapes(width, hidden_width, 16)
    weight_shapes = dict(
        w_qkv=(SPLIT + (width // 16, 3 * width), BF16),
        w_out=(SPLIT + (width // 16, width), BF16),
        w_up=(SPLIT + (width // 16, hidden_width), BF16),
        w_down=(SPLIT + (hidden_width // 16, width), BF16),
    )

    if fsdp == 16 and lax.axis_size("dp") == 2:
        ins = frames | vectors
        ins |= dict(qkv_in=qkv_weight, out_in=out_weight, up_in=up_weight, down_in=down_weight)
        ins |= dict(up_bias_in=up_bias, positions_in=positions.T, actor_in=actor_weight.T)
        shard_grads = dict(
            qkv_out=((part, 3 * width), F32),
            out_out=((part, width), F32),
            up_out=((part, hidden_width), F32),
            down_out=((width, hidden_part), F32),
        )
        outs = dict(
            tokens_grad=((row_count, width), F32), pack_out=((PACK_GRAD_ROWS, 128), F32)
        )
        scratch |= grads | weight_shapes
        scratch |= dict(
            pack=(SPLIT + (PACK_ROWS, 128), BF16),
            pack_own=((PACK_ROWS, 128), BF16),
            g_pack=(SPLIT + (PACK_GRAD_ROWS, 128), F32),
            positions=((LENGTH, width), F32),
            small=((8, width), F32),
            actor=((SLOTS, width), BF16),
            up_bias=((1, hidden_width), F32),
            gather_send=pltpu.SemaphoreType.DMA((GATHERS, 6)),
            gather_recv=pltpu.SemaphoreType.DMA((GATHERS, 6)),
            reduce_send=pltpu.SemaphoreType.DMA((len(REDUCES), 7)),
            reduce_recv=pltpu.SemaphoreType.DMA((len(REDUCES), 7)),
            store_sem=pltpu.SemaphoreType.DMA((row_count // (4 * LENGTH),)),
        )
        for index, (count, rows, kind, halved) in enumerate(REDUCES):
            for item, (lead, half) in enumerate(reduce_leads(halved)):
                scratch[index, item] = (lead + (rows, count // 2 if half else count), kind)
        tokens_grad, pack, qkv_g, out_g, up_g, down_g = run(
            spread_kernel, scale, ins, outs | shard_grads, scratch, flops, True, 0
        )
        vector = ((part,), F32)
        final = dict(
            o_loss=((1, 1), F32),
            o_stats=(running.shape, F32),
            o_positions=((part, LENGTH), F32),
            o_qkv=shard_grads["qkv_out"],
            o_out=shard_grads["out_out"],
            o_up=shard_grads["up_out"],
            o_down=((hidden_part, width), F32),
            o_up_bias=((hidden_part,), F32),
            o_actor=((slots, part), F32),
            o_actor_bias=((slots,), F32),
            o_tokens=((row_count, width), F32),
        )
        copies = pltpu.SemaphoreType.DMA((row_count // (4 * LENGTH),))
        done = run(
            finish_kernel,
            token_total,
            stats
            | dict(pack=pack, qkv=qkv_g, out=out_g, up=up_g, down=down_g, tokens=tokens_grad),
            final | dict.fromkeys(vectors, vector),
            dict(held=((row_count, width), F32), load_sem=copies, store_sem=copies),
        )
        loss, new_stats, pos_g, qkv_g, out_g, up_g, down_g = done[:7]
        up_bias_g, actor_g, actor_bias_g, tokens_grad = done[7:11]
        gain1, bias1, gain2, bias2, bias_down, gain3, bias3 = done[11:]
        return (
            loss.reshape(()),
            new_stats,
            tokens_grad,
            pos_g.T,
            gain1,
            bias1,
            qkv_g,
            out_g,
            gain2,
            bias2,
            up_g,
            up_bias_g,
            down_g,
            bias_down,
            gain3,
            bias3,
            actor_g.T,
            actor_bias_g,
        )

    def gather(array, axis):
        return lax.all_gather(array, "fsdp", axis=axis, tiled=True)

    packed = gather(
        jnp.concatenate([jnp.stack(list(vectors.values())), actor_weight.T, positions], 0), 1
    )
    fulls = [gather(weight, 0) for weight in (qkv_weight, out_weight, up_weight, down_weight)]
    ins = frames | {
        name: full.reshape(weight_shapes[name][0])
        for name, full in zip(weight_shapes, fulls, strict=True)
    }
    ins |= dict(
        positions=packed[7 + slots :].astype(F32),
        small=jnp.pad(packed[0:7].astype(F32), ((0, 1), (0, 0))),
        actor=jnp.pad(packed[7 : 7 + slots], ((0, SLOTS - slots), (0, 0))),
        up_bias=gather(up_bias, 0).astype(F32).reshape(1, hidden_width),
    )
    outs = dict(tokens_grad=((row_count, width), F32)) | grads
    tokens_grad, *sums = run(local_kernel, scale, ins, outs, scratch, flops)
    sums = Names(grads, sums)

    def scatter(array, axis):
        piece = lax.psum_scatter(array, "fsdp", scatter_dimension=axis, tiled=True)
        return lax.psum(piece.astype(BF16), "dp").astype(F32)

    down_sum = jnp.swapaxes(sums.g_down, 3, 4)
    qkv_part, out_part, up_part, down_part = (
        scatter(merged(grad), 0) for grad in (sums.g_qkv, sums.g_out, sums.g_up, down_sum)
    )
    rows = [jnp.sum(sums.g_small, 1), sums.g_actor[:slots], sums.g_positions]
    side = scatter(jnp.concatenate(rows, 0), 1)
    up_bias_part = scatter(jnp.sum(sums.g_up_bias, 0), 0)
    head_total = lax.psum(jnp.sum(sums.head_sums[: SLOTS + 1], 1), ("dp", "fsdp"))
    return (
        head_total[SLOTS] / token_total,
        DECAY_RATE * running + (1.0 - DECAY_RATE) * percentiles,
        tokens_grad,
        side[7 + slots :],
        side[G1],
        side[B1],
        qkv_part,
        out_part,
        side[G2],
        side[B2],
        up_part,
        up_bias_part,
        down_part,
        side[DB],
        side[GL],
        side[BL],
        side[7 : 7 + slots].T,
        head_total[:slots],
    )


def solution(mesh):
    rows, cols, both = P(("dp", "fsdp"), None), P(None, "fsdp"), P(("dp", "fsdp"))
    weight, vector, whole = P("fsdp", None), P("fsdp"), P()
    in_specs = (rows, cols, vector, vector, weight, weight, vector, vector, weight, vector)
    in_specs += (weight, vector, vector, vector, weight, whole, both, rows, both, both, both)
    in_specs += (whole, whole)
    out_specs = (whole, whole, rows, cols, vector, vector, weight, weight, vector, vector)
    out_specs += (weight, vector, weight, vector, vector, vector, weight, whole)
    return jax.shard_map(
        on_device, mesh=mesh, in_specs=in_specs, out_specs=out_specs, check_vma=False
    )
```

```python
import functools
import math
import math

import jax
import jax.numpy as jnp
from jax import lax
from jax.experimental import pallas as pl
from jax.experimental.pallas import tpu as pltpu
from jax.sharding import PartitionSpec as P

HEADS = 8
HEAD = 64
LENGTH = 64
QUAD = 4
WIDE = QUAD * HEAD
MASKED = -1e30
EPSILON = 1e-05
DECAY_RATE = 0.9
ENTROPY_WEIGHT = 0.1
SLOTS = 32
VMEM_BYTES = 63 * 1024 * 1024
BF16 = jnp.bfloat16
F32 = jnp.float32

G1, B1, G2, B2, DB, GL, BL = range(7)
MESH = pl.DeviceIdType.MESH


def dot(left, right, left_dim, right_dim):
    return lax.dot_general(
        left, right, (((left_dim,), (right_dim,)), ((), ())), preferred_element_type=F32
    )


def mean_last(values):
    return jnp.sum(values, -1, keepdims=True) * (1.0 / values.shape[-1])


def normalise(values):
    centred = values - mean_last(values)
    scale = lax.rsqrt(mean_last(centred * centred) + EPSILON)
    return centred * scale, scale


def norm_back(unit, scale, gain, upstream):
    inner = upstream * gain
    return scale * (inner - mean_last(inner) - unit * mean_last(inner * unit))


def fold_rows(values):
    rows, width = values.shape
    return jnp.sum(values.reshape(rows // 8, 8, width), 0)


def gelu_pair(values):
    half = jnp.exp2(values * values * (-0.5 * 1.4426950408889634))
    span = 1.0 + jnp.abs(values) * (0.3275911 * 0.7071067811865476)
    guess = pl.reciprocal(span, approx=True)
    t = guess * (2.0 - span * guess)
    poly = t * (
        0.5 * 0.254829592
        + t
        * (
            0.5 * -0.284496736
            + t * (0.5 * 1.421413741 + t * (0.5 * -1.453152027 + t * (0.5 * 1.061405429)))
        )
    )
    tail = poly * half
    cdf = jnp.where(values < 0.0, tail, 1.0 - tail)
    density = half * 0.3989422804014327
    return values * cdf, cdf + values * density


def pair_masks():
    lane = lax.broadcasted_iota(jnp.int32, (LENGTH, 2 * HEAD), 1)
    first = jnp.where(lane < HEAD, 1.0, 0.0)
    return first.astype(BF16), (1.0 - first).astype(BF16)


def spread_heads(rows, masks):
    zero = jnp.zeros((LENGTH, 2 * HEAD), BF16)
    left, right = rows[:, : 2 * HEAD], rows[:, 2 * HEAD :]
    blocks = [jnp.concatenate([left * mask, zero], 1) for mask in masks]
    blocks += [jnp.concatenate([zero, right * mask], 1) for mask in masks]
    return jnp.concatenate(blocks, 0)


def gather_heads(blocks):
    lane = lax.broadcasted_iota(jnp.int32, (LENGTH, 2 * HEAD), 1)
    pairs = []
    for pair in range(QUAD // 2):
        lanes = slice(pair * 2 * HEAD, (pair + 1) * 2 * HEAD)
        low = 2 * pair * HEAD
        first, second = blocks[low : low + HEAD, lanes], blocks[low + HEAD : low + 2 * HEAD, lanes]
        pairs.append(jnp.where(lane < HEAD, first, second))
    return jnp.concatenate(pairs, 1)


def causal_bias():
    key = lax.broadcasted_iota(jnp.int32, (LENGTH, WIDE), 0)
    query = lax.rem(lax.broadcasted_iota(jnp.int32, (LENGTH, WIDE), 1), HEAD)
    return jnp.where(key <= query, 0.0, MASKED)


LOG2E = 1.4426950408889634
SCORE_SCALE = HEAD ** (-0.5) * LOG2E


def chains(r, i):
    width = r.tokens.shape[1]
    found = []
    for s in range(4):
        row = pl.multiple_of((4 * i + s) * LENGTH, LENGTH)
        for half in range(width // WIDE):
            at = half * WIDE
            columns = [slice(k * width + at, k * width + at + WIDE) for k in range(3)]
            found.append((4 * i + s, pl.ds(row, LENGTH), columns))
    return found


def attend_group(r, i):
    masks, bias = pair_masks(), r.causal[...]
    group = chains(r, i)
    loaded = [[r.qkv[rows, part] for part in parts] for _, rows, parts in group]
    scores = [dot(key, spread_heads(query, masks), 1, 1) for query, key, _ in loaded]
    probs, totals = [], []
    for score in scores:
        score = score * SCORE_SCALE + bias
        highest = jnp.max(score, 0, keepdims=True)
        weights = jnp.exp2(score - highest)
        summed = jnp.sum(weights, 0, keepdims=True)
        probs.append((weights * (1.0 / summed)).astype(BF16))
        totals.append(highest + jnp.log(summed) * LOG2E)
    blocks = [dot(prob, value, 0, 0) for prob, (_, _, value) in zip(probs, loaded, strict=True)]
    done = [gather_heads(block).astype(BF16) for block in blocks]
    for (seq, rows, (q, _, _)), result, total in zip(group, done, totals, strict=True):
        r.attended[rows, q] = result
        r.totals[pl.ds(seq, 1), q] = total


def attend_back_group(r, i):
    masks, bias = pair_masks(), r.causal[...]
    done = []
    for half in range(2):
        group = chains(r, i)[half::2]
        queries = [spread_heads(r.qkv[rows, q], masks) for _, rows, (q, _, _) in group]
        aboves = [spread_heads(r.attended[rows, q], masks) for _, rows, (q, _, _) in group]
        scores = [
            dot(r.qkv[rows, k], query, 1, 1)
            for (_, rows, (_, k, _)), query in zip(group, queries, strict=True)
        ]
        prob_grads = [
            dot(r.qkv[rows, v], above, 1, 1)
            for (_, rows, (_, _, v)), above in zip(group, aboves, strict=True)
        ]
        probs, score_grads = [], []
        for (seq, _, (q, _, _)), score, pull in zip(group, scores, prob_grads, strict=True):
            prob = jnp.exp2(score * SCORE_SCALE + bias - r.totals[pl.ds(seq, 1), q])
            row_terms = jnp.sum(pull * prob, 0, keepdims=True)
            score_grads.append((prob * (pull - row_terms)).astype(BF16))
            probs.append(prob.astype(BF16))
        value_grads = [dot(prob, above, 1, 0) for prob, above in zip(probs, aboves, strict=True)]
        key_grads = [dot(grad, query, 1, 0) for grad, query in zip(score_grads, queries, strict=True)]
        query_grads = [
            dot(grad, r.qkv[rows, k], 0, 0)
            for (_, rows, (_, k, _)), grad in zip(group, score_grads, strict=True)
        ]
        for (_, rows, (q, k, v)), dq, dk, dv in zip(
            group, query_grads, key_grads, value_grads, strict=True
        ):
            done.append((rows, q, (gather_heads(dq) * HEAD ** (-0.5)).astype(BF16)))
            done.append((rows, k, (dk * HEAD ** (-0.5)).astype(BF16)))
            done.append((rows, v, dv.astype(BF16)))
    for rows, columns, grad in done:
        r.qkv[rows, columns] = grad


def policy(logits, masks, actions, advantage, scale):
    allowed = masks > 0
    held = jnp.where(allowed, logits, MASKED)
    shifted = held - jnp.max(held, 0, keepdims=True)
    weights = jnp.exp(shifted)
    summed = jnp.sum(weights, 0, keepdims=True)
    log_probs = shifted - jnp.log(summed)
    probs = weights * (1.0 / summed)
    plogp = jnp.where(allowed, probs * log_probs, 0.0)
    entropy = -jnp.sum(plogp, 0, keepdims=True)
    slot = lax.broadcasted_iota(jnp.int32, logits.shape, 0)
    taken = slot == actions
    chosen = jnp.sum(jnp.where(taken, log_probs, 0.0), 0, keepdims=True)
    loss = -advantage * chosen - ENTROPY_WEIGHT * entropy
    pull = advantage * (probs - jnp.where(taken, 1.0, 0.0)) + ENTROPY_WEIGHT * (
        plogp + probs * entropy
    )
    return loss, jnp.where(allowed, pull * scale, 0.0)


STRIP = 32
THIN = 16
LARGE = 1 << 20


class Names:
    def __init__(self, names, refs):
        self.table = dict(zip(names, refs, strict=True))

    def __getattr__(self, name):
        return self.table[name]


SPLIT = (4, 2, 2)
PACK_ROWS = 48
PACK_GRAD_ROWS = 40
POSITION_AT, SMALL_AT, BIAS_AT, LOSS_AT = 0, 64, 96, 97


def merged(block):
    return block.reshape(-1, block.shape[-1])


def strip_rows(row, count):
    return [pl.ds(pl.multiple_of(row + at, STRIP), STRIP) for at in range(0, count, STRIP)]


def load_starts(r, row, count):
    starts = [r.tokens[rows, :].astype(F32) for rows in strip_rows(row, count)]
    frames = [r.positions[at : at + STRIP, :] for at in range(0, LENGTH, STRIP)]
    return [start + frames[k % len(frames)] for k, start in enumerate(starts)]


def norm_pass(r):
    count = r.tokens.shape[0]
    rows = 4 * LENGTH

    def body(i, carry):
        row = pl.multiple_of(i * rows, rows)
        normed = [
            (normalise(start)[0] * r.small[G1 : G1 + 1, :] + r.small[B1 : B1 + 1, :]).astype(BF16)
            for start in load_starts(r, row, rows)
        ]
        normed = jnp.concatenate(normed, 0)
        turned = normed.T
        r.attended[pl.ds(row, rows), :] = normed
        r.normed_t[:, pl.ds(row, rows)] = turned
        return carry

    lax.fori_loop(0, count // rows, body, 0)


def project_third(r, third):
    count, width = r.tokens.shape
    rows = 8 * LENGTH
    columns = slice(third * width, (third + 1) * width)

    def body(i, carry):
        here = pl.ds(pl.multiple_of(i * rows, rows), rows)
        weight = merged(r.w_qkv[:, :, :, :, columns])
        r.qkv[here, columns] = dot(r.attended[here, :], weight, 1, 0).astype(BF16)
        return carry

    lax.fori_loop(0, count // rows, body, 0)


def front(r, pump):
    count = r.tokens.shape[0]

    def body(i, carry):
        pump(i)
        attend_group(r, i)
        return carry

    lax.fori_loop(0, count // (4 * LENGTH), body, 0)


def add_grad(ref, index, values):
    ref[index] += values.reshape(ref[index].shape)


def add_columns(ref, values):
    count = ref.shape[-1]
    for k in range(values.shape[1] // count):
        ref[k // 2, k % 2] += values[:, k * count : (k + 1) * count]


def clear(r):
    for ref in (r.g_out, r.g_up, r.g_down):

        def body(z, carry, ref=ref):
            ref[z] = jnp.zeros(ref.shape[1:], F32)
            return carry

        lax.fori_loop(0, ref.shape[0], body, 0)
    for ref in (r.g_actor, r.g_small, r.g_up_bias, r.g_positions, r.head_sums):
        ref[...] = jnp.zeros_like(ref)


def frame_values(r):
    r.causal[...] = causal_bias()
    fresh = DECAY_RATE * r.running[...] + (1.0 - DECAY_RATE) * r.percentiles[...]
    spread = jnp.maximum(1.0, fresh[1:2, :] - fresh[0:1, :])
    seqs = r.game_ids.shape[0]
    game = r.game_ids[...].reshape(seqs, 1)
    slot = lax.broadcasted_iota(jnp.int32, (seqs, spread.shape[1]), 1)
    column = jnp.sum(jnp.where(slot == game, spread, 0.0), 1, keepdims=True)
    count = 8 * LENGTH
    owner = lax.broadcasted_iota(jnp.int32, (8, count), 0)
    frame = lax.broadcasted_iota(jnp.int32, (8, count), 1)
    for k in range(seqs // 8):
        here = slice(k * count, (k + 1) * count)
        near = jnp.where(frame // LENGTH == owner, column[8 * k : 8 * k + 8], 0.0)
        wide = jnp.sum(near, 0, keepdims=True)
        r.advantage[:, here] = (r.returns[here] - r.values[here]).reshape(1, count) / wide
        r.action_row[:, here] = r.actions[here].reshape(1, count)


class Tile:
    def __init__(self, r, side):
        def pick(name):
            return r.table[name, side]

        self.active, self.slope = pick("active"), pick("slope")
        self.two_t, self.unit, self.last = pick("two_t"), pick("unit"), pick("last")
        self.scale = pick("scale")


def middle_part(r, scale, arrive):
    count, width = r.tokens.shape
    rows = r.low.shape[0]
    shards = r.w_up.shape[0]
    chunk = r.w_up.shape[-1] // shards
    slots = r.masks.shape[0]
    out_weight = r.w_out
    head_bias = jnp.concatenate(
        [r.actor_bias[...].astype(F32).reshape(slots, 1), jnp.zeros((SLOTS - slots, 1), F32)], 0
    )
    everything = slice(None)
    strips = [slice(at, at + STRIP) for at in range(0, rows, STRIP)]

    def gain(k):
        return r.small[k : k + 1, :]

    def tile_rows(i):
        return pl.ds(pl.multiple_of(i * rows, rows), rows)

    def before(t, tokens, attended):
        projected = dot(attended, merged(out_weight[...]), 1, 0)
        for k, strip in enumerate(strips):
            frame = k * STRIP % LENGTH
            start = tokens[k].astype(F32) + r.positions[frame : frame + STRIP, :]
            mid = start + projected[strip]
            unit, spread = normalise(mid)
            r.two_low[strip, :] = (unit * gain(G2) + gain(B2)).astype(BF16)
            t.unit[strip, :] = unit
            t.scale[strip, :] = spread
            t.last[strip, :] = mid + gain(DB)
        t.two_t[...] = r.two_low[...].T

    def columns(j):
        return pl.ds(pl.multiple_of(j * chunk, chunk), chunk)

    def up_weight(j):
        return merged(r.w_up[:, :, :, :, columns(j)])

    def activate(hidden, bias):
        done = [gelu_pair(hidden[at : at + THIN] + bias) for at in range(0, rows, THIN)]
        values = jnp.concatenate([value.astype(BF16) for value, _ in done], 0)
        return values, jnp.concatenate([slope.astype(BF16) for _, slope in done], 0)

    def forward_only(j, t):
        cols = columns(j)
        weight, bias, down = up_weight(j), r.up_bias[:, cols], merged(r.w_down[j])
        active, slope = activate(dot(r.two_low[...], weight, 1, 0), bias)
        t.last[...] += dot(active, down, 1, 0)
        t.active[:, cols], t.slope[:, cols] = active, slope

    def both_ways(j, here, there):
        cols = columns(j)
        bias, total = r.up_bias[:, cols], r.g_up_bias[:, cols]
        if there is not None:
            hidden = dot(r.two_low[...], up_weight(j), 1, 0)
        above = dot(r.low[...], merged(r.w_down[j]), 1, 1)
        for at in range(0, rows, THIN):
            strip = slice(at, at + THIN)
            part = (above[strip] * here.slope[strip, cols].astype(F32)).astype(BF16)
            r.hidden_grad[strip, :] = part
            total += fold_rows(part.astype(F32))
        add_columns(r.g_down.at[j], dot(r.low_t[...], here.active[:, cols], 1, 0))
        r.two_in[...] += dot(r.hidden_grad[...], up_weight(j), 1, 1)
        add_grad(
            r.g_up,
            (everything, everything, everything, everything, cols),
            dot(here.two_t[...], r.hidden_grad[...], 1, 0),
        )
        r.g_up_bias[:, cols] = total
        if there is not None:
            active, slope = activate(hidden, bias)
            there.last[...] += dot(active, merged(r.w_down[j]), 1, 0)
            there.active[:, cols], there.slope[:, cols] = active, slope

    def chunks(step):
        def body(j, carry):
            step(j)
            return carry

        lax.fori_loop(0, shards, body, 0)

    def last_norm(t):
        spreads = []
        for strip in strips:
            unit, spread = normalise(t.last[strip, :])
            r.low[strip, :] = (unit * gain(GL) + gain(BL)).astype(BF16)
            t.last[strip, :] = unit
            spreads.append(spread)
        return spreads, dot(r.actor[...], r.low[...], 1, 1) + head_bias

    def head(logits, masks, actions, advantage):
        masks = jnp.concatenate([masks, jnp.zeros((SLOTS - slots, rows), jnp.int32)], 0)
        loss, pull = policy(logits, masks, actions, advantage, scale)
        logit_grad = pull.astype(BF16)
        last_in = dot(logit_grad, r.actor[...], 0, 0)
        r.g_actor[...] += dot(logit_grad, r.low[...], 1, 0)
        wide_grad = logit_grad.astype(F32)
        fold = r.head_sums[0:SLOTS, :]
        for at in range(0, rows, 128):
            fold += wide_grad[:, at : at + 128]
        r.head_sums[0:SLOTS, :] = fold
        fold = r.head_sums[SLOTS : SLOTS + 1, :]
        for at in range(0, rows, 128):
            fold += loss[:, at : at + 128]
        r.head_sums[SLOTS : SLOTS + 1, :] = fold
        return last_in

    def last_norm_back(t, spreads, last_in):
        sums = [r.g_small[k] for k in (GL, BL, DB)]
        for strip, spread in zip(strips, spreads, strict=True):
            above, unit = last_in[strip], t.last[strip, :]
            grad = norm_back(unit, spread, gain(GL), above)
            sums[0] += fold_rows(above * unit)
            sums[1] += fold_rows(above)
            sums[2] += fold_rows(grad)
            t.last[strip, :] = grad
            r.low[strip, :] = grad.astype(BF16)
        for k, total in zip((GL, BL, DB), sums, strict=True):
            r.g_small[k] = total
        r.low_t[...] = r.low[...].T
        r.two_in[...] = jnp.zeros((rows, width), F32)

    def two_norm_back(t):
        sums = [r.g_small[k] for k in (G2, B2)]
        for strip in strips:
            above, unit = r.two_in[strip, :], t.unit[strip, :]
            sums[0] += fold_rows(above * unit)
            sums[1] += fold_rows(above)
            grad = t.last[strip, :] + norm_back(unit, t.scale[strip, :], gain(G2), above)
            t.last[strip, :] = grad
            r.hidden_grad[strip, :] = grad.astype(BF16)
        for k, total in zip((G2, B2), sums, strict=True):
            r.g_small[k] = total

    def out_back(i, t, attended):
        low = r.hidden_grad[...]
        add_grad(r.g_out, ..., dot(attended, low, 0, 0))
        r.attended[tile_rows(i), :] = dot(low, merged(out_weight[...]), 1, 1).astype(BF16)
        r.middle_grad[tile_rows(i), :] = t.last[...]

    sides = [Tile(r, 0), Tile(r, 1)]
    tiles = count // rows

    def begin(i):
        row = pl.multiple_of(i * rows, rows)
        return [r.tokens[part, :] for part in strip_rows(row, rows)], r.attended[tile_rows(i), :]

    def step(i, side, first=False, last=False):
        here, there = sides[side], sides[1 - side]
        at = tile_rows(i)
        side_data = r.masks[:, at], r.action_row[:, at], r.advantage[:, at]
        if not first:
            attended = r.attended[tile_rows(i - 1), :]
        if not last:
            ahead = begin(i + 1)
        spreads, logits = last_norm(here)
        if not first:
            two_norm_back(there)
        last_in = head(logits, *side_data)
        if not first:
            out_back(i - 1, there, attended)
        last_norm_back(here, spreads, last_in)
        if not last:
            before(there, *ahead)
        chunks(lambda j: both_ways(j, here, None if last else there))

    before(sides[0], *begin(0))
    arrive()
    chunks(lambda j: forward_only(j, sides[0]))
    step(0, 0, first=True)

    def pair(p, carry):
        step(2 * p + 1, 1)
        step(2 * p + 2, 0)
        return carry

    lax.fori_loop(0, (tiles - 2) // 2, pair, 0)
    step(tiles - 1, 1, last=True)
    two_norm_back(sides[1])
    out_back(tiles - 1, sides[1], r.attended[tile_rows(tiles - 1), :])


def attend_back(r, pump):
    count = r.tokens.shape[0]
    rows = 4 * LENGTH

    def body(i, carry):
        pump(i)
        attend_back_group(r, i)
        return carry

    lax.fori_loop(0, count // rows, body, 0)


def qkv_weight_grad(r, third):
    width = r.tokens.shape[1]
    step = width // 2
    for at in range(third * width, (third + 1) * width, step):
        values = dot(r.normed_t[...], r.qkv[:, at : at + step], 1, 0)
        values = values.astype(BF16).reshape(r.g_qkv.shape[:4] + (step,))
        r.g_qkv[:, :, :, :, at : at + step] = values


def start_back(r, pump, tile_done):
    count = r.tokens.shape[0]
    rows = 4 * LENGTH
    gain = r.small[G1 : G1 + 1, :]

    def body(i, carry):
        pump(i)
        row = pl.multiple_of(i * rows, rows)
        starts = load_starts(r, row, rows)
        one_in = dot(r.qkv[pl.ds(row, rows), :], merged(r.w_qkv[...]), 1, 1)
        sums = [r.g_small[k] for k in (G1, B1)]
        frames = [r.g_positions[at : at + STRIP, :] for at in range(0, LENGTH, STRIP)]
        grads = []
        for k, (start, there) in enumerate(zip(starts, strip_rows(row, rows), strict=True)):
            unit, scale = normalise(start)
            above = one_in[k * STRIP : (k + 1) * STRIP]
            sums[0] += fold_rows(above * unit)
            sums[1] += fold_rows(above)
            grads.append(r.middle_grad[there, :] + norm_back(unit, scale, gain, above))
            frames[k % len(frames)] += grads[k]
        r.g_positions[...] = jnp.concatenate(frames, 0)
        for k, total in zip((G1, B1), sums, strict=True):
            r.g_small[k] = total
        r.middle_grad[pl.ds(row, rows), :] = jnp.concatenate(grads, 0)
        tile_done(i)
        return carry

    lax.fori_loop(0, count // rows, body, 0)


def pack_shards(r):
    part = r.positions_in.shape[0]
    slots = r.masks.shape[0]
    rows = [
        ref[...].astype(F32).reshape(1, part)
        for ref in (r.gain1, r.bias1, r.gain2, r.bias2, r.bias_down, r.gain3, r.bias3)
    ]
    rows += [r.actor_in[...].astype(F32), jnp.zeros((32 - 7 - slots, part), F32)]
    features = jnp.concatenate(
        [r.positions_in[...].astype(F32), jnp.concatenate(rows, 0).T, jnp.zeros((part, 32), F32)], 1
    )
    bias = r.up_bias_in[...].astype(F32).reshape(1, 128)
    packed = jnp.concatenate([features, bias, jnp.zeros((PACK_ROWS - part - 1, 128), F32)], 0)
    r.pack_own[...] = packed.astype(BF16)


def unpack_shards(r):
    slots = r.masks.shape[0]
    blocks = r.pack[...].astype(F32).reshape(-1, PACK_ROWS, 128)
    part = r.positions_in.shape[0]
    features = merged(blocks[:, :part, :]).T
    r.positions[...] = features[POSITION_AT : POSITION_AT + LENGTH]
    small = features[SMALL_AT : SMALL_AT + 32]
    r.small[...] = small[0:8]
    width = small.shape[1]
    r.actor[...] = jnp.concatenate(
        [small[7 : 7 + slots], jnp.zeros((SLOTS - slots, width), F32)], 0
    ).astype(BF16)
    r.up_bias[...] = jnp.concatenate(
        [blocks[f, part : part + 1, :] for f in range(blocks.shape[0])], 1
    )


def small_rows(r):
    slots = r.masks.shape[0]
    rows = [jnp.sum(r.g_small[k], 0, keepdims=True) for k in range(7)]
    return jnp.concatenate(
        rows + [r.g_actor[0:slots, :], jnp.zeros((32 - 7 - slots, rows[0].shape[1]), F32)], 0
    )


def pack_grads(r):
    width = r.tokens.shape[1]
    part = r.positions_in.shape[0]
    features = jnp.concatenate(
        [r.g_positions[...], small_rows(r), jnp.zeros((128 - SMALL_AT - 32, width), F32)], 0
    ).T
    sums = jnp.sum(r.head_sums[0 : SLOTS + 8, :], 1, keepdims=True)
    lane = lax.broadcasted_iota(jnp.int32, (part, 128), 1)
    bias = jnp.sum(r.g_up_bias[...], 0, keepdims=True)
    shape = r.g_pack.shape
    for f in range(width // part):
        block = features[f * part : (f + 1) * part]
        block = jnp.where(lane == BIAS_AT, sums[0:SLOTS], block)
        block = jnp.where(lane == LOSS_AT, sums[SLOTS : SLOTS + 1], block)
        owner = (f // 4, f // 2 % 2, f % 2)
        rows = [block, bias[:, f * 128 : (f + 1) * 128], jnp.zeros((shape[3] - part - 1, 128), F32)]
        r.g_pack[owner] = jnp.concatenate(rows, 0)


GATHERS = 9
REDUCES = (
    (128, 512, BF16, False),
    (2048, 32, BF16, True),
    (512, 32, BF16, True),
    (512, 32, BF16, False),
    (512, 32, BF16, False),
    (512, 32, BF16, True),
    (128, PACK_GRAD_ROWS, F32, False),
)


class Place:
    def __init__(self):
        self.x = lax.axis_index("dp")
        f = lax.axis_index("fsdp")
        self.z, self.y, self.c = f // 4, f // 2 % 2, f % 2

    def at(self, x=None, z=None, y=None, c=None):
        pick = lambda new, old: old if new is None else new
        f = pick(z, self.z) * 4 + pick(y, self.y) * 2 + pick(c, self.c)
        return (pick(x, self.x), f)

    def z_partner(self, k):
        return (self.z + 1 - 2 * (self.z % 2), (self.z + 2) % 4, 3 - self.z)[k]

    def partners(self):
        return [self.at(z=self.z_partner(k)) for k in range(3)] + [
            self.at(y=1 - self.y),
            self.at(c=1 - self.c),
            self.at(x=1 - self.x),
        ]


def remote(r_send, r_recv, index):
    def copy(src, dst, k, device):
        return pltpu.make_async_remote_copy(
            src_ref=src,
            dst_ref=dst,
            send_sem=r_send.at[index, k],
            recv_sem=r_recv.at[index, k],
            device_id=device,
            device_id_type=MESH,
        )

    return copy


class Gather:
    def __init__(self, r, place, index, full, own, at, count, halved=False):
        p = place
        copy = remote(r.gather_send, r.gather_recv, index)
        cols = part = slice(at, at + count)
        if halved:
            part = pl.ds(pl.multiple_of(at + p.x * (count // 2), 128), count // 2)
        self.full, self.own, self.part, self.place = full, own, part, place
        mine = full.at[p.z, p.y, p.c, :, part]
        self.z = [copy(own.at[:, part], mine, k, p.at(z=p.z_partner(k))) for k in range(3)]
        line = full.at[:, p.y, p.c, :, part]
        self.y = copy(line, line, 3, p.at(y=1 - p.y))
        plane = full.at[:, :, p.c, :, part]
        self.x = copy(plane, plane, 4, p.at(x=1 - p.x)) if halved else None
        plane = full.at[:, :, p.c, :, cols]
        self.c = copy(plane, plane, 5, p.at(c=1 - p.c))

    def start_z(self):
        for copy in self.z:
            copy.start()
        p = self.place
        self.full[p.z, p.y, p.c, :, self.part] = self.own[:, self.part]

    def start_y(self):
        for copy in self.z:
            copy.wait_recv()
        self.y.start()

    def start_x(self):
        self.y.wait_recv()
        self.x.start()

    def start_c(self):
        (self.y if self.x is None else self.x).wait_recv()
        self.c.start()

    def ready(self):
        self.c.wait_recv()

    def close(self):
        for copy in self.z + [self.y, self.c] + ([] if self.x is None else [self.x]):
            copy.wait_send()


class Reduce:
    def __init__(self, r, place, index, grad, at=0):
        count, _, kind, halved = REDUCES[index]
        self.grad, self.place, self.kind, self.halved = grad, place, kind, halved
        p = place
        copy = remote(r.reduce_send, r.reduce_recv, index)
        self.cols = slice(at, at + count)
        self.buffers = [r.table[index, part] for part in range(len(reduce_leads(halved)))]
        sc, rc, ry, rz, rx = self.buffers[:5]
        keep = count
        self.part = self.cols
        if halved:
            keep = count // 2
            self.part = self.half(at, keep, p.x)
            self.away = self.half(at, keep, 1 - p.x)
            self.local, self.local_away = self.half(0, keep, p.x), self.half(0, keep, 1 - p.x)
            self.sx1 = sc.at[:, :, :, 0:keep]
            self.x1 = copy(self.sx1, self.buffers[5], 6, p.at(x=1 - p.x))
        tail = slice(count - keep, count)
        self.sy = sc.at[:, 0, :, tail]
        self.sz = [sc.at[k, 1, :, tail] for k in range(3)]
        self.sx = sc.at[3, 1, :, tail]
        self.c = copy(sc, rc, 0, p.at(c=1 - p.c))
        self.y = copy(self.sy, ry, 1, p.at(y=1 - p.y))
        self.z = [copy(self.sz[k], rz.at[k], 2 + k, p.at(z=p.z_partner(k))) for k in range(3)]
        self.x = copy(self.sx, rx, 5, p.at(x=1 - p.x))

    @staticmethod
    def half(at, keep, x):
        return pl.ds(pl.multiple_of(at + x * keep, 128), keep)

    def add(self, index, values):
        total = self.grad[index].astype(F32) + values.astype(F32)
        self.grad[index] = total.astype(self.grad.dtype)

    def start_c(self):
        sc, p = self.buffers[0], self.place

        def body(z, carry):
            sc[z] = self.grad[z, :, 1 - p.c, :, self.cols].astype(self.kind)
            return carry

        lax.fori_loop(0, 4, body, 0)
        self.c.start()

    def start_x1(self):
        rc, p = self.buffers[1], self.place
        self.c.wait()

        def body(z, carry):
            away = self.grad[z, :, p.c, :, self.away].astype(F32) + rc[z, :, :, self.local_away].astype(F32)
            self.sx1[z] = away.astype(self.kind)
            self.add((z, slice(None), p.c, slice(None), self.part), rc[z, :, :, self.local])
            return carry

        lax.fori_loop(0, 4, body, 0)
        self.x1.start()

    def start_y(self):
        p = self.place
        if self.halved:
            held = self.buffers[5]
            self.x1.wait_recv()
        else:
            held = self.buffers[1]
            self.c.wait()

        def body(z, carry):
            away = self.grad[z, 1 - p.y, p.c, :, self.part].astype(F32) + held[z, 1 - p.y].astype(F32)
            self.sy[z] = away.astype(self.kind)
            self.add((z, p.y, p.c, slice(None), self.part), held[z, p.y])
            return carry

        lax.fori_loop(0, 4, body, 0)
        self.y.start()

    def start_z(self):
        ry, p = self.buffers[2], self.place
        self.y.wait_recv()
        for k in (2, 1, 0):
            owner = p.z_partner(k)
            away = self.grad[owner, p.y, p.c, :, self.part].astype(F32) + ry[owner].astype(F32)
            self.sz[k][...] = away.astype(self.kind)
            self.z[k].start()
        self.add((p.z, p.y, p.c, slice(None), self.part), ry[p.z])

    def start_x(self):
        rz, p = self.buffers[3], self.place
        for copy in self.z:
            copy.wait_recv()
        near = self.grad[p.z, p.y, p.c, :, self.part].astype(F32) + rz[0].astype(F32)
        self.sx[...] = (near + (rz[1].astype(F32) + rz[2].astype(F32))).astype(self.kind)
        self.x.start()

    def finish(self, out):
        rx = self.buffers[4]
        self.x.wait_recv()
        if self.halved:
            out[:, self.part] = self.sx[...].astype(F32)
            out[:, self.away] = rx[...].astype(F32)
        else:
            out[:, self.cols] = self.sx[...].astype(F32) + rx[...].astype(F32)

    def close(self):
        for copy in self.z + [self.y, self.x] + ([self.x1] if self.halved else []):
            copy.wait_send()


def reduce_leads(halved):
    leads = [((4, 2), False), ((4, 2), False), ((4,), halved), ((3,), halved), ((), halved)]
    return leads + ([((4, 2), True)] if halved else [])


def layer_scratch(row_count, width, hidden_width, shards):
    tile = 256
    seqs = row_count // LENGTH
    pairs = dict(
        active=((tile, hidden_width), BF16),
        slope=((tile, hidden_width), BF16),
        two_t=((width, tile), BF16),
        unit=((tile, width), F32),
        last=((tile, width), F32),
        scale=((tile, 1), F32),
    )
    both = {(name, side): item for name, item in pairs.items() for side in range(2)}
    return both | dict(
        tokens=((row_count, width), BF16),
        middle_grad=((row_count, width), F32),
        normed_t=((width, row_count), BF16),
        qkv=((row_count, 3 * width), BF16),
        attended=((row_count, width), BF16),
        totals=((seqs, width), F32),
        causal=((LENGTH, WIDE), F32),
        advantage=((1, row_count), F32),
        action_row=((1, row_count), jnp.int32),
        two_low=((tile, width), BF16),
        low=((tile, width), BF16),
        low_t=((width, tile), BF16),
        two_in=((tile, width), F32),
        hidden_grad=((tile, hidden_width // 4), BF16),
        local_sem=pltpu.SemaphoreType.DMA((2,)),
    )


def grad_shapes(width, hidden_width, shards):
    split = SPLIT
    part, hidden_part = width // shards, hidden_width // shards
    return dict(
        g_qkv=(split + (part, 3 * width), BF16),
        g_out=(split + (part, width), F32),
        g_up=(split + (part, hidden_width), F32),
        g_down=(split + (width, hidden_part), F32),
        g_actor=((SLOTS, width), F32),
        g_small=((7, 8, width), F32),
        g_up_bias=((8, hidden_width), F32),
        g_positions=((LENGTH, width), F32),
        head_sums=((SLOTS + 8, 128), F32),
    )


def at_step(i, table):
    for step, actions in table.items():

        @pl.when(i == step)
        def _(actions=actions):
            for action in actions:
                action()


def spread_kernel(names, scale, *refs):
    r = Names(names, refs)
    place = Place()
    load = pltpu.make_async_copy(r.tokens_in, r.tokens, r.local_sem.at[0])
    load.start()
    partners = place.partners()
    barrier = pltpu.get_barrier_semaphore()
    for device in partners:
        pl.semaphore_signal(barrier, inc=1, device_id=device, device_id_type=MESH)
    pack_shards(r)
    pl.semaphore_wait(barrier, len(partners))
    width, hidden_width = r.w_out.shape[-1], r.w_up.shape[-1]
    plan = [(r.pack, r.pack_own, 0, 128)]
    plan += [(r.w_qkv, r.qkv_in, k * width, width) for k in range(3)]
    plan += [(r.w_out, r.out_in, 0, width)]
    half = hidden_width // 2
    plan += [(r.w_up, r.up_in, k * half, half, True) for k in range(2)]
    plan += [(r.w_down, r.down_in, k * width // 2, width // 2, True) for k in range(2)]
    gathers = [Gather(r, place, k, *item) for k, item in enumerate(plan)]
    pack, q, k, v, out, up0, up1, down0, down1 = gathers
    pack.start_z()
    q.start_z()
    k.start_z()
    v.start_z()
    pack.start_y()
    q.start_y()
    pack.start_c()
    frame_values(r)
    pack.ready()
    unpack_shards(r)
    k.start_y()
    q.start_c()
    load.wait()
    out.start_z()
    up0.start_z()
    norm_pass(r)
    v.start_y()
    k.start_c()
    up1.start_z()
    down0.start_z()
    down1.start_z()
    q.ready()
    project_third(r, 0)
    v.start_c()
    clear(r)
    k.ready()
    project_third(r, 1)
    v.ready()
    project_third(r, 2)

    front(
        r,
        lambda i: at_step(
            i,
            {
                1: [out.start_y],
                3: [up0.start_y, out.start_c],
                5: [up1.start_y, up0.start_x],
                7: [down0.start_y, up1.start_x, up0.start_c],
                9: [down1.start_y, down0.start_x, up1.start_c],
            },
        ),
    )
    out.ready()

    def arrive():
        down1.start_x()
        down0.start_c()
        down1.start_c()
        for group in (up0, up1, down0, down1):
            group.ready()

    middle_part(r, scale, arrive)

    plan = [(r.g_down,), (r.g_up,), (r.g_out,)]
    plan += [(r.g_qkv, k * width) for k in range(3)] + [(r.g_pack,)]
    reduces = [Reduce(r, place, k, *item) for k, item in enumerate(plan)]
    down, up, out, q, k, v, pack = reduces
    down.start_c()
    up.start_c()
    out.start_c()
    attend_back(
        r,
        lambda i: at_step(
            i,
            {
                1: [down.start_y, up.start_x1],
                2: [out.start_x1],
                6: [down.start_z, up.start_y],
                7: [out.start_y],
                9: [up.start_z],
            },
        ),
    )
    qkv_weight_grad(r, 0)
    q.start_c()
    qkv_weight_grad(r, 2)
    v.start_c()
    q.start_y()
    qkv_weight_grad(r, 1)
    k.start_c()
    v.start_x1()
    out.start_z()
    k.start_y()

    def stored(i):
        rows = pl.ds(pl.multiple_of(i * 4 * LENGTH, 4 * LENGTH), 4 * LENGTH)
        return pltpu.make_async_copy(
            r.middle_grad.at[rows, :], r.tokens_grad.at[rows, :], r.store_sem.at[i]
        )

    start_back(
        r,
        lambda i: at_step(
            i,
            {
                2: [down.start_x],
                3: [up.start_x, q.start_z],
                5: [v.start_y, out.start_x],
                6: [k.start_z],
                8: [v.start_z, q.start_x],
            },
        ),
        lambda i: stored(i).start(),
    )
    pack_grads(r)
    pack.start_c()
    k.start_x()
    v.start_x()
    pack.start_y()
    down.finish(r.down_out)
    up.finish(r.up_out)
    pack.start_z()
    out.finish(r.out_out)
    for group in (q, k, v):
        group.finish(r.qkv_out)
    pack.start_x()
    for i in range(r.middle_grad.shape[0] // (4 * LENGTH)):
        stored(i).wait()
    for group in gathers + reduces:
        group.close()
    pack.finish(r.pack_out)


def finish_kernel(names, count, *refs):
    r = Names(names, refs)
    step = 4 * LENGTH
    parts = [pl.ds(at, step) for at in range(0, r.tokens.shape[0], step)]
    loads = [
        pltpu.make_async_copy(r.tokens.at[part, :], r.held.at[part, :], r.load_sem.at[k])
        for k, part in enumerate(parts)
    ]
    stores = [
        pltpu.make_async_copy(r.held.at[part, :], r.o_tokens.at[part, :], r.store_sem.at[k])
        for k, part in enumerate(parts)
    ]
    for load in loads:
        load.start()
    r.o_qkv[...] = r.qkv[...]
    r.o_out[...] = r.out[...]
    r.o_up[...] = r.up[...]
    r.o_down[...] = r.down[...].T
    r.o_stats[...] = DECAY_RATE * r.running[...] + (1.0 - DECAY_RATE) * r.percentiles[...]
    part, positions = r.o_positions.shape
    slots = r.o_actor.shape[0]
    features = r.pack[0:part, :]
    r.o_positions[...] = features[:, POSITION_AT : POSITION_AT + positions]
    turned = features.T
    vectors = (r.gain1, r.bias1, r.gain2, r.bias2, r.bias_down, r.gain3, r.bias3)
    for k, ref in enumerate(vectors):
        ref[...] = turned[SMALL_AT + k : SMALL_AT + k + 1, :].reshape(part)
    r.o_actor[...] = turned[SMALL_AT + 7 : SMALL_AT + 7 + slots, :]
    r.o_actor_bias[...] = turned[BIAS_AT : BIAS_AT + 1, :].reshape(part)[0:slots]
    r.o_loss[...] = features[0:1, LOSS_AT : LOSS_AT + 1] * (1.0 / count)
    r.o_up_bias[...] = r.pack[part : part + 1, :].reshape(128)
    for load, store in zip(loads, stores, strict=True):
        load.wait()
        store.start()
    for store in stores:
        store.wait()


def local_kernel(names, scale, *refs):
    r = Names(names, refs)
    load = pltpu.make_async_copy(r.tokens_in, r.tokens, r.local_sem.at[0])
    load.start()
    clear(r)
    frame_values(r)
    load.wait()
    norm_pass(r)
    for third in range(3):
        project_third(r, third)
    front(r, lambda i: None)
    middle_part(r, scale, lambda: None)
    attend_back(r, lambda i: None)
    for third in range(3):
        qkv_weight_grad(r, third)
    start_back(r, lambda i: None, lambda i: None)
    store = pltpu.make_async_copy(r.middle_grad, r.tokens_grad, r.local_sem.at[1])
    store.start()
    store.wait()


def run(kernel, constant, ins, outs, scratch, flops=0, side_effects=False, collective=None):
    vmem = pl.BlockSpec(memory_space=pltpu.VMEM)
    anywhere = pl.BlockSpec(memory_space=pl.ANY)
    in_specs = [anywhere if array.size > LARGE else vmem for array in ins.values()]
    out_specs = [anywhere if math.prod(shape) > LARGE else vmem for shape, _ in outs.values()]
    return pl.pallas_call(
        functools.partial(kernel, (*ins, *outs, *scratch), constant),
        out_shape=[jax.ShapeDtypeStruct(shape, kind) for shape, kind in outs.values()],
        in_specs=in_specs,
        out_specs=out_specs,
        scratch_shapes=[
            item if not isinstance(item, tuple) else pltpu.VMEM(item[0], item[1])
            for item in scratch.values()
        ],
        compiler_params=pltpu.CompilerParams(
            vmem_limit_bytes=VMEM_BYTES, has_side_effects=side_effects, collective_id=collective
        ),
        cost_estimate=pl.CostEstimate(flops=flops, bytes_accessed=1 << 24, transcendentals=0),
    )(*ins.values())


def on_device(
    tokens,
    positions,
    norm_one_gain,
    norm_one_bias,
    qkv_weight,
    out_weight,
    norm_two_gain,
    norm_two_bias,
    up_weight,
    up_bias,
    down_weight,
    down_bias,
    final_gain,
    final_bias,
    actor_weight,
    actor_bias,
    actions,
    action_masks,
    game_ids,
    returns,
    values,
    running,
    percentiles,
):
    row_count, width = tokens.shape
    seq_count = row_count // LENGTH
    hidden_width = up_weight.shape[1]
    slots = actor_weight.shape[1]
    fsdp = lax.axis_size("fsdp")
    device_count = lax.axis_size("dp") * fsdp
    token_total = row_count * device_count
    scale = float(seq_count * device_count) / token_total
    flops = 6 * row_count * width * (4 * width + 2 * hidden_width)
    part, hidden_part = width // fsdp, hidden_width // fsdp

    vectors = dict(
        gain1=norm_one_gain,
        bias1=norm_one_bias,
        gain2=norm_two_gain,
        bias2=norm_two_bias,
        bias_down=down_bias,
        gain3=final_gain,
        bias3=final_bias,
    )
    stats = dict(running=running, percentiles=percentiles)
    frames = stats | dict(
        tokens_in=tokens,
        actor_bias=actor_bias,
        actions=actions,
        masks=action_masks.T,
        game_ids=game_ids,
        returns=returns,
        values=values,
    )
    scratch = layer_scratch(row_count, width, hidden_width, 16)
    grads = grad_shapes(width, hidden_width, 16)
    weight_shapes = dict(
        w_qkv=(SPLIT + (width // 16, 3 * width), BF16),
        w_out=(SPLIT + (width // 16, width), BF16),
        w_up=(SPLIT + (width // 16, hidden_width), BF16),
        w_down=(SPLIT + (hidden_width // 16, width), BF16),
    )

    if fsdp == 16 and lax.axis_size("dp") == 2:
        ins = frames | vectors
        ins |= dict(qkv_in=qkv_weight, out_in=out_weight, up_in=up_weight, down_in=down_weight)
        ins |= dict(up_bias_in=up_bias, positions_in=positions.T, actor_in=actor_weight.T)
        shard_grads = dict(
            qkv_out=((part, 3 * width), F32),
            out_out=((part, width), F32),
            up_out=((part, hidden_width), F32),
            down_out=((width, hidden_part), F32),
        )
        outs = dict(
            tokens_grad=((row_count, width), F32), pack_out=((PACK_GRAD_ROWS, 128), F32)
        )
        scratch |= grads | weight_shapes
        scratch |= dict(
            pack=(SPLIT + (PACK_ROWS, 128), BF16),
            pack_own=((PACK_ROWS, 128), BF16),
            g_pack=(SPLIT + (PACK_GRAD_ROWS, 128), F32),
            positions=((LENGTH, width), F32),
            small=((8, width), F32),
            actor=((SLOTS, width), BF16),
            up_bias=((1, hidden_width), F32),
            gather_send=pltpu.SemaphoreType.DMA((GATHERS, 6)),
            gather_recv=pltpu.SemaphoreType.DMA((GATHERS, 6)),
            reduce_send=pltpu.SemaphoreType.DMA((len(REDUCES), 7)),
            reduce_recv=pltpu.SemaphoreType.DMA((len(REDUCES), 7)),
            store_sem=pltpu.SemaphoreType.DMA((row_count // (4 * LENGTH),)),
        )
        for index, (count, rows, kind, halved) in enumerate(REDUCES):
            for item, (lead, half) in enumerate(reduce_leads(halved)):
                scratch[index, item] = (lead + (rows, count // 2 if half else count), kind)
        tokens_grad, pack, qkv_g, out_g, up_g, down_g = run(
            spread_kernel, scale, ins, outs | shard_grads, scratch, flops, True, 0
        )
        vector = ((part,), F32)
        final = dict(
            o_loss=((1, 1), F32),
            o_stats=(running.shape, F32),
            o_positions=((part, LENGTH), F32),
            o_qkv=shard_grads["qkv_out"],
            o_out=shard_grads["out_out"],
            o_up=shard_grads["up_out"],
            o_down=((hidden_part, width), F32),
            o_up_bias=((hidden_part,), F32),
            o_actor=((slots, part), F32),
            o_actor_bias=((slots,), F32),
            o_tokens=((row_count, width), F32),
        )
        copies = pltpu.SemaphoreType.DMA((row_count // (4 * LENGTH),))
        done = run(
            finish_kernel,
            token_total,
            stats
            | dict(pack=pack, qkv=qkv_g, out=out_g, up=up_g, down=down_g, tokens=tokens_grad),
            final | dict.fromkeys(vectors, vector),
            dict(held=((row_count, width), F32), load_sem=copies, store_sem=copies),
        )
        loss, new_stats, pos_g, qkv_g, out_g, up_g, down_g = done[:7]
        up_bias_g, actor_g, actor_bias_g, tokens_grad = done[7:11]
        gain1, bias1, gain2, bias2, bias_down, gain3, bias3 = done[11:]
        return (
            loss.reshape(()),
            new_stats,
            tokens_grad,
            pos_g.T,
            gain1,
            bias1,
            qkv_g,
            out_g,
            gain2,
            bias2,
            up_g,
            up_bias_g,
            down_g,
            bias_down,
            gain3,
            bias3,
            actor_g.T,
            actor_bias_g,
        )

    def gather(array, axis):
        return lax.all_gather(array, "fsdp", axis=axis, tiled=True)

    packed = gather(
        jnp.concatenate([jnp.stack(list(vectors.values())), actor_weight.T, positions], 0), 1
    )
    fulls = [gather(weight, 0) for weight in (qkv_weight, out_weight, up_weight, down_weight)]
    ins = frames | {
        name: full.reshape(weight_shapes[name][0])
        for name, full in zip(weight_shapes, fulls, strict=True)
    }
    ins |= dict(
        positions=packed[7 + slots :].astype(F32),
        small=jnp.pad(packed[0:7].astype(F32), ((0, 1), (0, 0))),
        actor=jnp.pad(packed[7 : 7 + slots], ((0, SLOTS - slots), (0, 0))),
        up_bias=gather(up_bias, 0).astype(F32).reshape(1, hidden_width),
    )
    outs = dict(tokens_grad=((row_count, width), F32)) | grads
    tokens_grad, *sums = run(local_kernel, scale, ins, outs, scratch, flops)
    sums = Names(grads, sums)

    def scatter(array, axis):
        piece = lax.psum_scatter(array, "fsdp", scatter_dimension=axis, tiled=True)
        return lax.psum(piece.astype(BF16), "dp").astype(F32)

    down_sum = jnp.swapaxes(sums.g_down, 3, 4)
    qkv_part, out_part, up_part, down_part = (
        scatter(merged(grad).astype(F32), 0)
        for grad in (sums.g_qkv, sums.g_out, sums.g_up, down_sum)
    )
    rows = [jnp.sum(sums.g_small, 1), sums.g_actor[:slots], sums.g_positions]
    side = scatter(jnp.concatenate(rows, 0), 1)
    up_bias_part = scatter(jnp.sum(sums.g_up_bias, 0), 0)
    head_total = lax.psum(jnp.sum(sums.head_sums[: SLOTS + 1], 1), ("dp", "fsdp"))
    return (
        head_total[SLOTS] / token_total,
        DECAY_RATE * running + (1.0 - DECAY_RATE) * percentiles,
        tokens_grad,
        side[7 + slots :],
        side[G1],
        side[B1],
        qkv_part,
        out_part,
        side[G2],
        side[B2],
        up_part,
        up_bias_part,
        down_part,
        side[DB],
        side[GL],
        side[BL],
        side[7 : 7 + slots].T,
        head_total[:slots],
    )


def solution(mesh):
    rows, cols, both = P(("dp", "fsdp"), None), P(None, "fsdp"), P(("dp", "fsdp"))
    weight, vector, whole = P("fsdp", None), P("fsdp"), P()
    in_specs = (rows, cols, vector, vector, weight, weight, vector, vector, weight, vector)
    in_specs += (weight, vector, vector, vector, weight, whole, both, rows, both, both, both)
    in_specs += (whole, whole)
    out_specs = (whole, whole, rows, cols, vector, vector, weight, weight, vector, vector)
    out_specs += (weight, vector, weight, vector, vector, vector, weight, whole)
    return jax.shard_map(
        on_device, mesh=mesh, in_specs=in_specs, out_specs=out_specs, check_vma=False
    )
```

```python
import functools
import math
import math

import jax
import jax.numpy as jnp
from jax import lax
from jax.experimental import pallas as pl
from jax.experimental.pallas import tpu as pltpu
from jax.sharding import PartitionSpec as P

HEADS = 8
HEAD = 64
LENGTH = 64
QUAD = 4
WIDE = QUAD * HEAD
MASKED = -1e30
EPSILON = 1e-05
DECAY_RATE = 0.9
ENTROPY_WEIGHT = 0.1
SLOTS = 32
VMEM_BYTES = 63 * 1024 * 1024
BF16 = jnp.bfloat16
F32 = jnp.float32

G1, B1, G2, B2, DB, GL, BL = range(7)
MESH = pl.DeviceIdType.MESH


def dot(left, right, left_dim, right_dim):
    return lax.dot_general(
        left, right, (((left_dim,), (right_dim,)), ((), ())), preferred_element_type=F32
    )


def mean_last(values):
    return jnp.sum(values, -1, keepdims=True) * (1.0 / values.shape[-1])


def normalise(values):
    centred = values - mean_last(values)
    scale = lax.rsqrt(mean_last(centred * centred) + EPSILON)
    return centred * scale, scale


def norm_back(unit, scale, gain, upstream):
    inner = upstream * gain
    return scale * (inner - mean_last(inner) - unit * mean_last(inner * unit))


def fold_rows(values):
    rows, width = values.shape
    return jnp.sum(values.reshape(rows // 8, 8, width), 0)


def gelu_pair(values):
    half = jnp.exp2(values * values * (-0.5 * 1.4426950408889634))
    span = 1.0 + jnp.abs(values) * (0.3275911 * 0.7071067811865476)
    guess = pl.reciprocal(span, approx=True)
    t = guess * (2.0 - span * guess)
    poly = t * (
        0.5 * 0.254829592
        + t
        * (
            0.5 * -0.284496736
            + t * (0.5 * 1.421413741 + t * (0.5 * -1.453152027 + t * (0.5 * 1.061405429)))
        )
    )
    tail = poly * half
    cdf = jnp.where(values < 0.0, tail, 1.0 - tail)
    density = half * 0.3989422804014327
    return values * cdf, cdf + values * density


def pair_masks():
    lane = lax.broadcasted_iota(jnp.int32, (LENGTH, 2 * HEAD), 1)
    first = jnp.where(lane < HEAD, 1.0, 0.0)
    return first.astype(BF16), (1.0 - first).astype(BF16)


def spread_heads(rows, masks):
    zero = jnp.zeros((LENGTH, 2 * HEAD), BF16)
    left, right = rows[:, : 2 * HEAD], rows[:, 2 * HEAD :]
    blocks = [jnp.concatenate([left * mask, zero], 1) for mask in masks]
    blocks += [jnp.concatenate([zero, right * mask], 1) for mask in masks]
    return jnp.concatenate(blocks, 0)


def gather_heads(blocks):
    lane = lax.broadcasted_iota(jnp.int32, (LENGTH, 2 * HEAD), 1)
    pairs = []
    for pair in range(QUAD // 2):
        lanes = slice(pair * 2 * HEAD, (pair + 1) * 2 * HEAD)
        low = 2 * pair * HEAD
        first, second = blocks[low : low + HEAD, lanes], blocks[low + HEAD : low + 2 * HEAD, lanes]
        pairs.append(jnp.where(lane < HEAD, first, second))
    return jnp.concatenate(pairs, 1)


def causal_bias():
    key = lax.broadcasted_iota(jnp.int32, (LENGTH, WIDE), 0)
    query = lax.rem(lax.broadcasted_iota(jnp.int32, (LENGTH, WIDE), 1), HEAD)
    return jnp.where(key <= query, 0.0, MASKED)


LOG2E = 1.4426950408889634
SCORE_SCALE = HEAD ** (-0.5) * LOG2E


def chains(r, i):
    width = r.tokens.shape[1]
    found = []
    for s in range(4):
        row = pl.multiple_of((4 * i + s) * LENGTH, LENGTH)
        for half in range(width // WIDE):
            at = half * WIDE
            columns = [slice(k * width + at, k * width + at + WIDE) for k in range(3)]
            found.append((4 * i + s, pl.ds(row, LENGTH), columns))
    return found


def attend_group(r, i):
    masks, bias = pair_masks(), r.causal[...]
    group = chains(r, i)
    loaded = [[r.qkv[rows, part] for part in parts] for _, rows, parts in group]
    scores = [dot(key, spread_heads(query, masks), 1, 1) for query, key, _ in loaded]
    probs, totals = [], []
    for score in scores:
        score = score * SCORE_SCALE + bias
        highest = jnp.max(score, 0, keepdims=True)
        weights = jnp.exp2(score - highest)
        summed = jnp.sum(weights, 0, keepdims=True)
        probs.append((weights * (1.0 / summed)).astype(BF16))
        totals.append(highest + jnp.log(summed) * LOG2E)
    blocks = [dot(prob, value, 0, 0) for prob, (_, _, value) in zip(probs, loaded, strict=True)]
    done = [gather_heads(block).astype(BF16) for block in blocks]
    for (seq, rows, (q, _, _)), result, total in zip(group, done, totals, strict=True):
        r.attended[rows, q] = result
        r.totals[pl.ds(seq, 1), q] = total


def attend_back_group(r, i):
    masks, bias = pair_masks(), r.causal[...]
    done = []
    for half in range(2):
        group = chains(r, i)[half::2]
        queries = [spread_heads(r.qkv[rows, q], masks) for _, rows, (q, _, _) in group]
        aboves = [spread_heads(r.attended[rows, q], masks) for _, rows, (q, _, _) in group]
        scores = [
            dot(r.qkv[rows, k], query, 1, 1)
            for (_, rows, (_, k, _)), query in zip(group, queries, strict=True)
        ]
        prob_grads = [
            dot(r.qkv[rows, v], above, 1, 1)
            for (_, rows, (_, _, v)), above in zip(group, aboves, strict=True)
        ]
        probs, score_grads = [], []
        for (seq, _, (q, _, _)), score, pull in zip(group, scores, prob_grads, strict=True):
            prob = jnp.exp2(score * SCORE_SCALE + bias - r.totals[pl.ds(seq, 1), q])
            row_terms = jnp.sum(pull * prob, 0, keepdims=True)
            score_grads.append((prob * (pull - row_terms)).astype(BF16))
            probs.append(prob.astype(BF16))
        value_grads = [dot(prob, above, 1, 0) for prob, above in zip(probs, aboves, strict=True)]
        key_grads = [dot(grad, query, 1, 0) for grad, query in zip(score_grads, queries, strict=True)]
        query_grads = [
            dot(grad, r.qkv[rows, k], 0, 0)
            for (_, rows, (_, k, _)), grad in zip(group, score_grads, strict=True)
        ]
        for (_, rows, (q, k, v)), dq, dk, dv in zip(
            group, query_grads, key_grads, value_grads, strict=True
        ):
            done.append((rows, q, (gather_heads(dq) * HEAD ** (-0.5)).astype(BF16)))
            done.append((rows, k, (dk * HEAD ** (-0.5)).astype(BF16)))
            done.append((rows, v, dv.astype(BF16)))
    for rows, columns, grad in done:
        r.qkv[rows, columns] = grad


def policy(logits, masks, actions, advantage, scale):
    allowed = masks > 0
    held = jnp.where(allowed, logits, MASKED)
    shifted = held - jnp.max(held, 0, keepdims=True)
    weights = jnp.exp(shifted)
    summed = jnp.sum(weights, 0, keepdims=True)
    log_probs = shifted - jnp.log(summed)
    probs = weights * (1.0 / summed)
    plogp = jnp.where(allowed, probs * log_probs, 0.0)
    entropy = -jnp.sum(plogp, 0, keepdims=True)
    slot = lax.broadcasted_iota(jnp.int32, logits.shape, 0)
    taken = slot == actions
    chosen = jnp.sum(jnp.where(taken, log_probs, 0.0), 0, keepdims=True)
    loss = -advantage * chosen - ENTROPY_WEIGHT * entropy
    pull = advantage * (probs - jnp.where(taken, 1.0, 0.0)) + ENTROPY_WEIGHT * (
        plogp + probs * entropy
    )
    return loss, jnp.where(allowed, pull * scale, 0.0)


STRIP = 32
THIN = 16
LARGE = 1 << 20


class Names:
    def __init__(self, names, refs):
        self.table = dict(zip(names, refs, strict=True))

    def __getattr__(self, name):
        return self.table[name]


SPLIT = (4, 2, 2)
PACK_ROWS = 48
PACK_GRAD_ROWS = 40
POSITION_AT, SMALL_AT, BIAS_AT, LOSS_AT = 0, 64, 96, 97


def merged(block):
    return block.reshape(-1, block.shape[-1])


def strip_rows(row, count):
    return [pl.ds(pl.multiple_of(row + at, STRIP), STRIP) for at in range(0, count, STRIP)]


def load_starts(r, row, count):
    starts = [r.tokens[rows, :].astype(F32) for rows in strip_rows(row, count)]
    frames = [r.positions[at : at + STRIP, :] for at in range(0, LENGTH, STRIP)]
    return [start + frames[k % len(frames)] for k, start in enumerate(starts)]


def norm_pass(r):
    count = r.tokens.shape[0]
    rows = 4 * LENGTH

    def body(i, carry):
        row = pl.multiple_of(i * rows, rows)
        normed = [
            (normalise(start)[0] * r.small[G1 : G1 + 1, :] + r.small[B1 : B1 + 1, :]).astype(BF16)
            for start in load_starts(r, row, rows)
        ]
        normed = jnp.concatenate(normed, 0)
        turned = normed.T
        r.attended[pl.ds(row, rows), :] = normed
        r.normed_t[:, pl.ds(row, rows)] = turned
        return carry

    lax.fori_loop(0, count // rows, body, 0)


def project_third(r, third):
    count, width = r.tokens.shape
    rows = 8 * LENGTH
    columns = slice(third * width, (third + 1) * width)

    def body(i, carry):
        here = pl.ds(pl.multiple_of(i * rows, rows), rows)
        weight = merged(r.w_qkv[:, :, :, :, columns])
        r.qkv[here, columns] = dot(r.attended[here, :], weight, 1, 0).astype(BF16)
        return carry

    lax.fori_loop(0, count // rows, body, 0)


def front(r, pump):
    count = r.tokens.shape[0]

    def body(i, carry):
        pump(i)
        attend_group(r, i)
        return carry

    lax.fori_loop(0, count // (4 * LENGTH), body, 0)


def add_grad(ref, index, values):
    ref[index] += values.reshape(ref[index].shape)


def add_columns(ref, values):
    count = ref.shape[-1]
    for k in range(values.shape[1] // count):
        ref[k // 2, k % 2] += values[:, k * count : (k + 1) * count]


def clear(r):
    for ref in (r.g_out, r.g_up, r.g_down):

        def body(z, carry, ref=ref):
            ref[z] = jnp.zeros(ref.shape[1:], F32)
            return carry

        lax.fori_loop(0, ref.shape[0], body, 0)
    for ref in (r.g_actor, r.g_small, r.g_up_bias, r.g_positions, r.head_sums):
        ref[...] = jnp.zeros_like(ref)


def frame_values(r):
    r.causal[...] = causal_bias()
    fresh = DECAY_RATE * r.running[...] + (1.0 - DECAY_RATE) * r.percentiles[...]
    spread = jnp.maximum(1.0, fresh[1:2, :] - fresh[0:1, :])
    seqs = r.game_ids.shape[0]
    game = r.game_ids[...].reshape(seqs, 1)
    slot = lax.broadcasted_iota(jnp.int32, (seqs, spread.shape[1]), 1)
    column = jnp.sum(jnp.where(slot == game, spread, 0.0), 1, keepdims=True)
    count = 8 * LENGTH
    owner = lax.broadcasted_iota(jnp.int32, (8, count), 0)
    frame = lax.broadcasted_iota(jnp.int32, (8, count), 1)
    for k in range(seqs // 8):
        here = slice(k * count, (k + 1) * count)
        near = jnp.where(frame // LENGTH == owner, column[8 * k : 8 * k + 8], 0.0)
        wide = jnp.sum(near, 0, keepdims=True)
        r.advantage[:, here] = (r.returns[here] - r.values[here]).reshape(1, count) / wide
        r.action_row[:, here] = r.actions[here].reshape(1, count)


class Tile:
    def __init__(self, r, side):
        def pick(name):
            return r.table[name, side]

        self.active, self.slope = pick("active"), pick("slope")
        self.two_t, self.unit, self.last = pick("two_t"), pick("unit"), pick("last")
        self.scale = pick("scale")


def middle_part(r, scale, arrive):
    count, width = r.tokens.shape
    rows = r.low.shape[0]
    shards = r.w_up.shape[0]
    chunk = r.w_up.shape[-1] // shards
    slots = r.masks.shape[0]
    out_weight = r.w_out
    head_bias = jnp.concatenate(
        [r.actor_bias[...].astype(F32).reshape(slots, 1), jnp.zeros((SLOTS - slots, 1), F32)], 0
    )
    everything = slice(None)
    strips = [slice(at, at + STRIP) for at in range(0, rows, STRIP)]

    def gain(k):
        return r.small[k : k + 1, :]

    def tile_rows(i):
        return pl.ds(pl.multiple_of(i * rows, rows), rows)

    def before(t, tokens, attended):
        projected = dot(attended, merged(out_weight[...]), 1, 0)
        for k, strip in enumerate(strips):
            frame = k * STRIP % LENGTH
            start = tokens[k].astype(F32) + r.positions[frame : frame + STRIP, :]
            mid = start + projected[strip]
            unit, spread = normalise(mid)
            r.two_low[strip, :] = (unit * gain(G2) + gain(B2)).astype(BF16)
            t.unit[strip, :] = unit
            t.scale[strip, :] = spread
            t.last[strip, :] = mid + gain(DB)
        t.two_t[...] = r.two_low[...].T

    def columns(j):
        return pl.ds(pl.multiple_of(j * chunk, chunk), chunk)

    def up_weight(j):
        return merged(r.w_up[:, :, :, :, columns(j)])

    def activate(hidden, bias):
        done = [gelu_pair(hidden[at : at + THIN] + bias) for at in range(0, rows, THIN)]
        values = jnp.concatenate([value.astype(BF16) for value, _ in done], 0)
        return values, jnp.concatenate([slope.astype(BF16) for _, slope in done], 0)

    def forward_only(j, t):
        cols = columns(j)
        weight, bias, down = up_weight(j), r.up_bias[:, cols], merged(r.w_down[j])
        active, slope = activate(dot(r.two_low[...], weight, 1, 0), bias)
        t.last[...] += dot(active, down, 1, 0)
        t.active[:, cols], t.slope[:, cols] = active, slope

    def both_ways(j, here, there):
        cols = columns(j)
        bias, total = r.up_bias[:, cols], r.g_up_bias[:, cols]
        if there is not None:
            hidden = dot(r.two_low[...], up_weight(j), 1, 0)
        above = dot(r.low[...], merged(r.w_down[j]), 1, 1)
        for at in range(0, rows, THIN):
            strip = slice(at, at + THIN)
            part = (above[strip] * here.slope[strip, cols].astype(F32)).astype(BF16)
            r.hidden_grad[strip, :] = part
            total += fold_rows(part.astype(F32))
        add_columns(r.g_down.at[j], dot(r.low_t[...], here.active[:, cols], 1, 0))
        r.two_in[...] += dot(r.hidden_grad[...], up_weight(j), 1, 1)
        add_grad(
            r.g_up,
            (everything, everything, everything, everything, cols),
            dot(here.two_t[...], r.hidden_grad[...], 1, 0),
        )
        r.g_up_bias[:, cols] = total
        if there is not None:
            active, slope = activate(hidden, bias)
            there.last[...] += dot(active, merged(r.w_down[j]), 1, 0)
            there.active[:, cols], there.slope[:, cols] = active, slope

    def chunks(step):
        def body(j, carry):
            step(j)
            return carry

        lax.fori_loop(0, shards, body, 0)

    def last_norm(t):
        spreads = []
        for strip in strips:
            unit, spread = normalise(t.last[strip, :])
            r.low[strip, :] = (unit * gain(GL) + gain(BL)).astype(BF16)
            t.last[strip, :] = unit
            spreads.append(spread)
        return spreads, dot(r.actor[...], r.low[...], 1, 1) + head_bias

    def head(logits, masks, actions, advantage):
        masks = jnp.concatenate([masks, jnp.zeros((SLOTS - slots, rows), jnp.int32)], 0)
        loss, pull = policy(logits, masks, actions, advantage, scale)
        logit_grad = pull.astype(BF16)
        last_in = dot(logit_grad, r.actor[...], 0, 0)
        r.g_actor[...] += dot(logit_grad, r.low[...], 1, 0)
        wide_grad = logit_grad.astype(F32)
        fold = r.head_sums[0:SLOTS, :]
        for at in range(0, rows, 128):
            fold += wide_grad[:, at : at + 128]
        r.head_sums[0:SLOTS, :] = fold
        fold = r.head_sums[SLOTS : SLOTS + 1, :]
        for at in range(0, rows, 128):
            fold += loss[:, at : at + 128]
        r.head_sums[SLOTS : SLOTS + 1, :] = fold
        return last_in

    def last_norm_back(t, spreads, last_in):
        sums = [r.g_small[k] for k in (GL, BL, DB)]
        for strip, spread in zip(strips, spreads, strict=True):
            above, unit = last_in[strip], t.last[strip, :]
            grad = norm_back(unit, spread, gain(GL), above)
            sums[0] += fold_rows(above * unit)
            sums[1] += fold_rows(above)
            sums[2] += fold_rows(grad)
            t.last[strip, :] = grad
            r.low[strip, :] = grad.astype(BF16)
        for k, total in zip((GL, BL, DB), sums, strict=True):
            r.g_small[k] = total
        r.low_t[...] = r.low[...].T
        r.two_in[...] = jnp.zeros((rows, width), F32)

    def two_norm_back(t):
        sums = [r.g_small[k] for k in (G2, B2)]
        for strip in strips:
            above, unit = r.two_in[strip, :], t.unit[strip, :]
            sums[0] += fold_rows(above * unit)
            sums[1] += fold_rows(above)
            grad = t.last[strip, :] + norm_back(unit, t.scale[strip, :], gain(G2), above)
            t.last[strip, :] = grad
            r.hidden_grad[strip, :] = grad.astype(BF16)
        for k, total in zip((G2, B2), sums, strict=True):
            r.g_small[k] = total

    def out_back(i, t, attended):
        low = r.hidden_grad[...]
        add_grad(r.g_out, ..., dot(attended, low, 0, 0))
        r.attended[tile_rows(i), :] = dot(low, merged(out_weight[...]), 1, 1).astype(BF16)
        r.middle_grad[tile_rows(i), :] = t.last[...]

    sides = [Tile(r, 0), Tile(r, 1)]
    tiles = count // rows

    def begin(i):
        row = pl.multiple_of(i * rows, rows)
        return [r.tokens[part, :] for part in strip_rows(row, rows)], r.attended[tile_rows(i), :]

    def step(i, side, first=False, last=False):
        here, there = sides[side], sides[1 - side]
        at = tile_rows(i)
        side_data = r.masks[:, at], r.action_row[:, at], r.advantage[:, at]
        if not first:
            attended = r.attended[tile_rows(i - 1), :]
        if not last:
            ahead = begin(i + 1)
        spreads, logits = last_norm(here)
        if not first:
            two_norm_back(there)
        last_in = head(logits, *side_data)
        if not first:
            out_back(i - 1, there, attended)
        last_norm_back(here, spreads, last_in)
        if not last:
            before(there, *ahead)
        chunks(lambda j: both_ways(j, here, None if last else there))

    before(sides[0], *begin(0))
    arrive()
    chunks(lambda j: forward_only(j, sides[0]))
    step(0, 0, first=True)

    def pair(p, carry):
        step(2 * p + 1, 1)
        step(2 * p + 2, 0)
        return carry

    lax.fori_loop(0, (tiles - 2) // 2, pair, 0)
    step(tiles - 1, 1, last=True)
    two_norm_back(sides[1])
    out_back(tiles - 1, sides[1], r.attended[tile_rows(tiles - 1), :])


def attend_back(r, pump):
    count = r.tokens.shape[0]
    rows = 4 * LENGTH

    def body(i, carry):
        pump(i)
        attend_back_group(r, i)
        return carry

    lax.fori_loop(0, count // rows, body, 0)


def qkv_weight_grad(r, third):
    width = r.tokens.shape[1]
    step = width // 2
    for at in range(third * width, (third + 1) * width, step):
        values = dot(r.normed_t[...], r.qkv[:, at : at + step], 1, 0)
        values = values.astype(BF16).reshape(r.g_qkv.shape[:4] + (step,))
        r.g_qkv[:, :, :, :, at : at + step] = values


def start_back(r, pump, tile_done):
    count = r.tokens.shape[0]
    rows = 4 * LENGTH
    gain = r.small[G1 : G1 + 1, :]

    def body(i, carry):
        pump(i)
        row = pl.multiple_of(i * rows, rows)
        starts = load_starts(r, row, rows)
        one_in = dot(r.qkv[pl.ds(row, rows), :], merged(r.w_qkv[...]), 1, 1)
        sums = [r.g_small[k] for k in (G1, B1)]
        frames = [r.g_positions[at : at + STRIP, :] for at in range(0, LENGTH, STRIP)]
        grads = []
        for k, (start, there) in enumerate(zip(starts, strip_rows(row, rows), strict=True)):
            unit, scale = normalise(start)
            above = one_in[k * STRIP : (k + 1) * STRIP]
            sums[0] += fold_rows(above * unit)
            sums[1] += fold_rows(above)
            grads.append(r.middle_grad[there, :] + norm_back(unit, scale, gain, above))
            frames[k % len(frames)] += grads[k]
        r.g_positions[...] = jnp.concatenate(frames, 0)
        for k, total in zip((G1, B1), sums, strict=True):
            r.g_small[k] = total
        r.middle_grad[pl.ds(row, rows), :] = jnp.concatenate(grads, 0)
        tile_done(i)
        return carry

    lax.fori_loop(0, count // rows, body, 0)


def pack_shards(r):
    part = r.positions_in.shape[0]
    slots = r.masks.shape[0]
    rows = [
        ref[...].astype(F32).reshape(1, part)
        for ref in (r.gain1, r.bias1, r.gain2, r.bias2, r.bias_down, r.gain3, r.bias3)
    ]
    rows += [r.actor_in[...].astype(F32), jnp.zeros((32 - 7 - slots, part), F32)]
    features = jnp.concatenate(
        [r.positions_in[...].astype(F32), jnp.concatenate(rows, 0).T, jnp.zeros((part, 32), F32)], 1
    )
    bias = r.up_bias_in[...].astype(F32).reshape(1, 128)
    packed = jnp.concatenate([features, bias, jnp.zeros((PACK_ROWS - part - 1, 128), F32)], 0)
    r.pack_own[...] = packed.astype(BF16)


def unpack_shards(r):
    slots = r.masks.shape[0]
    blocks = r.pack[...].astype(F32).reshape(-1, PACK_ROWS, 128)
    part = r.positions_in.shape[0]
    features = merged(blocks[:, :part, :]).T
    r.positions[...] = features[POSITION_AT : POSITION_AT + LENGTH]
    small = features[SMALL_AT : SMALL_AT + 32]
    r.small[...] = small[0:8]
    width = small.shape[1]
    r.actor[...] = jnp.concatenate(
        [small[7 : 7 + slots], jnp.zeros((SLOTS - slots, width), F32)], 0
    ).astype(BF16)
    r.up_bias[...] = jnp.concatenate(
        [blocks[f, part : part + 1, :] for f in range(blocks.shape[0])], 1
    )


def small_rows(r):
    slots = r.masks.shape[0]
    rows = [jnp.sum(r.g_small[k], 0, keepdims=True) for k in range(7)]
    return jnp.concatenate(
        rows + [r.g_actor[0:slots, :], jnp.zeros((32 - 7 - slots, rows[0].shape[1]), F32)], 0
    )


def pack_grads(r):
    width = r.tokens.shape[1]
    part = r.positions_in.shape[0]
    features = jnp.concatenate(
        [r.g_positions[...], small_rows(r), jnp.zeros((128 - SMALL_AT - 32, width), F32)], 0
    ).T
    sums = jnp.sum(r.head_sums[0 : SLOTS + 8, :], 1, keepdims=True)
    lane = lax.broadcasted_iota(jnp.int32, (part, 128), 1)
    bias = jnp.sum(r.g_up_bias[...], 0, keepdims=True)
    shape = r.g_pack.shape
    for f in range(width // part):
        block = features[f * part : (f + 1) * part]
        block = jnp.where(lane == BIAS_AT, sums[0:SLOTS], block)
        block = jnp.where(lane == LOSS_AT, sums[SLOTS : SLOTS + 1], block)
        owner = (f // 4, f // 2 % 2, f % 2)
        rows = [block, bias[:, f * 128 : (f + 1) * 128], jnp.zeros((shape[3] - part - 1, 128), F32)]
        r.g_pack[owner] = jnp.concatenate(rows, 0)


GATHERS = 9
REDUCES = (
    (128, 512, BF16, False),
    (2048, 32, BF16, True),
    (512, 32, BF16, True),
    (512, 32, BF16, False),
    (512, 32, BF16, False),
    (512, 32, BF16, True),
    (128, PACK_GRAD_ROWS, F32, False),
)


class Place:
    def __init__(self):
        self.x = lax.axis_index("dp")
        f = lax.axis_index("fsdp")
        self.z, self.y, self.c = f // 4, f // 2 % 2, f % 2

    def at(self, x=None, z=None, y=None, c=None):
        pick = lambda new, old: old if new is None else new
        f = pick(z, self.z) * 4 + pick(y, self.y) * 2 + pick(c, self.c)
        return (pick(x, self.x), f)

    def z_partner(self, k):
        return (self.z + 1 - 2 * (self.z % 2), (self.z + 2) % 4, 3 - self.z)[k]

    def lines(self):
        return [self.z] + [self.z_partner(k) for k in range(3)]

    def partners(self):
        return [self.at(z=self.z_partner(k)) for k in range(3)] + [
            self.at(y=1 - self.y),
            self.at(c=1 - self.c),
            self.at(x=1 - self.x),
        ]


def remote(r_send, r_recv, index):
    def copy(src, dst, k, device):
        return pltpu.make_async_remote_copy(
            src_ref=src,
            dst_ref=dst,
            send_sem=r_send.at[index, k],
            recv_sem=r_recv.at[index, k],
            device_id=device,
            device_id_type=MESH,
        )

    return copy


class Gather:
    def __init__(self, r, place, index, full, own, at, count, halved=False):
        p = place
        copy = remote(r.gather_send, r.gather_recv, index)
        cols = part = slice(at, at + count)
        if halved:
            part = pl.ds(pl.multiple_of(at + p.x * (count // 2), 128), count // 2)
        self.full, self.own, self.part, self.place, self.halved = full, own, part, place, halved
        mine = full.at[p.z, p.y, p.c, :, part]
        self.z = [copy(own.at[:, part], mine, k, p.at(z=p.z_partner(k))) for k in range(3)]
        self.y, self.x, self.near, self.far = [], [], [], []
        for k, z in enumerate(p.lines()):
            shard = full.at[z, p.y, p.c, :, part]
            self.y.append(copy(shard, shard, 3 + k, p.at(y=1 - p.y)))
            if halved:
                pair = full.at[z, :, p.c, :, part]
                self.x.append(copy(pair, pair, 7 + k, p.at(x=1 - p.x)))
                pair = full.at[z, :, p.c, :, cols]
                self.far.append(copy(pair, pair, 11 + k, p.at(c=1 - p.c)))
            else:
                self.near.append(copy(shard, shard, 7 + k, p.at(c=1 - p.c)))
                shard = full.at[z, 1 - p.y, p.c, :, part]
                self.far.append(copy(shard, shard, 11 + k, p.at(c=1 - p.c)))

    def start_z(self):
        for copy in self.z:
            copy.start()
        p = self.place
        self.full[p.z, p.y, p.c, :, self.part] = self.own[:, self.part]
        self.y[0].start()
        if not self.halved:
            self.near[0].start()

    def start_y(self):
        for k, copy in enumerate(self.z):
            copy.wait_recv()
            self.y[k + 1].start()
            if not self.halved:
                self.near[k + 1].start()

    def start_x(self):
        for arrived, copy in zip(self.y, self.x, strict=True):
            arrived.wait_recv()
            copy.start()

    def start_c(self):
        for arrived, copy in zip(self.x if self.halved else self.y, self.far, strict=True):
            arrived.wait_recv()
            copy.start()

    def ready(self):
        for copy in self.near + self.far:
            copy.wait_recv()

    def close(self):
        for copy in self.z + self.y + self.x + self.near + self.far:
            copy.wait_send()


class Reduce:
    def __init__(self, r, place, index, grad, at=0):
        count, _, kind, halved = REDUCES[index]
        self.grad, self.place, self.kind, self.halved = grad, place, kind, halved
        p = place
        copy = remote(r.reduce_send, r.reduce_recv, index)
        self.cols = slice(at, at + count)
        self.buffers = [r.table[index, part] for part in range(len(reduce_leads(halved)))]
        sc, rc, ry, rz, rx = self.buffers[:5]
        keep = count
        self.part = self.cols
        self.lines = p.lines()
        if halved:
            keep = count // 2
            self.part = self.half(at, keep, p.x)
            self.away = self.half(at, keep, 1 - p.x)
            self.local, self.local_away = self.half(0, keep, p.x), self.half(0, keep, 1 - p.x)
            held = self.buffers[5]
            self.sx1 = sc.at[:, :, :, 0:keep]
            self.x1 = [
                copy(self.sx1.at[z], held.at[z], 12 + k, p.at(x=1 - p.x))
                for k, z in enumerate(self.lines)
            ]
        tail = slice(count - keep, count)
        self.sy = sc.at[:, 0, :, tail]
        self.sz = [sc.at[k, 1, :, tail] for k in range(3)]
        self.sx = sc.at[3, 1, :, tail]
        self.c, self.y = [], []
        for k, z in enumerate(self.lines):
            self.c.append(copy(sc.at[z], rc.at[z], k, p.at(c=1 - p.c)))
            self.y.append(copy(self.sy.at[z], ry.at[z], 4 + k, p.at(y=1 - p.y)))
        self.z = [copy(self.sz[k], rz.at[k], 8 + k, p.at(z=p.z_partner(k))) for k in range(3)]
        self.x = copy(self.sx, rx, 11, p.at(x=1 - p.x))

    @staticmethod
    def half(at, keep, x):
        return pl.ds(pl.multiple_of(at + x * keep, 128), keep)

    def add(self, index, values):
        total = self.grad[index].astype(F32) + values.astype(F32)
        self.grad[index] = total.astype(self.grad.dtype)

    def start_c(self):
        sc, p = self.buffers[0], self.place
        for z, copy in zip(self.lines, self.c, strict=True):
            sc[z] = self.grad[z, :, 1 - p.c, :, self.cols].astype(self.kind)
            copy.start()

    def start_x1(self):
        rc, p = self.buffers[1], self.place
        for z, arrived, copy in zip(self.lines, self.c, self.x1, strict=True):
            arrived.wait()
            away = self.grad[z, :, p.c, :, self.away].astype(F32)
            away += rc[z, :, :, self.local_away].astype(F32)
            self.sx1[z] = away.astype(self.kind)
            copy.start()
            self.add((z, slice(None), p.c, slice(None), self.part), rc[z, :, :, self.local])

    def start_y(self):
        p = self.place
        held = self.buffers[5 if self.halved else 1]
        for k, z in enumerate(self.lines):
            if self.halved:
                self.x1[k].wait_recv()
            else:
                self.c[k].wait()
            away = self.grad[z, 1 - p.y, p.c, :, self.part].astype(F32)
            away += held[z, 1 - p.y].astype(F32)
            self.sy[z] = away.astype(self.kind)
            self.y[k].start()
            self.add((z, p.y, p.c, slice(None), self.part), held[z, p.y])

    def start_z(self):
        ry, p = self.buffers[2], self.place
        for k in range(3):
            owner = self.lines[k + 1]
            self.y[k + 1].wait_recv()
            away = self.grad[owner, p.y, p.c, :, self.part].astype(F32) + ry[owner].astype(F32)
            self.sz[k][...] = away.astype(self.kind)
            self.z[k].start()
        self.y[0].wait_recv()
        self.add((p.z, p.y, p.c, slice(None), self.part), ry[p.z])

    def start_x(self):
        rz, p = self.buffers[3], self.place
        for copy in self.z:
            copy.wait_recv()
        near = self.grad[p.z, p.y, p.c, :, self.part].astype(F32) + rz[0].astype(F32)
        self.sx[...] = (near + (rz[1].astype(F32) + rz[2].astype(F32))).astype(self.kind)
        self.x.start()

    def finish(self, out):
        rx = self.buffers[4]
        self.x.wait_recv()
        if self.halved:
            out[:, self.part] = self.sx[...].astype(F32)
            out[:, self.away] = rx[...].astype(F32)
        else:
            out[:, self.cols] = self.sx[...].astype(F32) + rx[...].astype(F32)

    def close(self):
        for copy in self.z + self.y + [self.x] + (self.x1 if self.halved else []):
            copy.wait_send()


def reduce_leads(halved):
    leads = [((4, 2), False), ((4, 2), False), ((4,), halved), ((3,), halved), ((), halved)]
    return leads + ([((4, 2), True)] if halved else [])


def layer_scratch(row_count, width, hidden_width, shards):
    tile = 256
    seqs = row_count // LENGTH
    pairs = dict(
        active=((tile, hidden_width), BF16),
        slope=((tile, hidden_width), BF16),
        two_t=((width, tile), BF16),
        unit=((tile, width), F32),
        last=((tile, width), F32),
        scale=((tile, 1), F32),
    )
    both = {(name, side): item for name, item in pairs.items() for side in range(2)}
    return both | dict(
        tokens=((row_count, width), BF16),
        middle_grad=((row_count, width), F32),
        normed_t=((width, row_count), BF16),
        qkv=((row_count, 3 * width), BF16),
        attended=((row_count, width), BF16),
        totals=((seqs, width), F32),
        causal=((LENGTH, WIDE), F32),
        advantage=((1, row_count), F32),
        action_row=((1, row_count), jnp.int32),
        two_low=((tile, width), BF16),
        low=((tile, width), BF16),
        low_t=((width, tile), BF16),
        two_in=((tile, width), F32),
        hidden_grad=((tile, hidden_width // 4), BF16),
        local_sem=pltpu.SemaphoreType.DMA((2,)),
    )


def grad_shapes(width, hidden_width, shards):
    split = SPLIT
    part, hidden_part = width // shards, hidden_width // shards
    return dict(
        g_qkv=(split + (part, 3 * width), BF16),
        g_out=(split + (part, width), F32),
        g_up=(split + (part, hidden_width), F32),
        g_down=(split + (width, hidden_part), F32),
        g_actor=((SLOTS, width), F32),
        g_small=((7, 8, width), F32),
        g_up_bias=((8, hidden_width), F32),
        g_positions=((LENGTH, width), F32),
        head_sums=((SLOTS + 8, 128), F32),
    )


def at_step(i, table):
    for step, actions in table.items():

        @pl.when(i == step)
        def _(actions=actions):
            for action in actions:
                action()


def spread_kernel(names, scale, *refs):
    r = Names(names, refs)
    place = Place()
    load = pltpu.make_async_copy(r.tokens_in, r.tokens, r.local_sem.at[0])
    load.start()
    partners = place.partners()
    barrier = pltpu.get_barrier_semaphore()
    for device in partners:
        pl.semaphore_signal(barrier, inc=1, device_id=device, device_id_type=MESH)
    pack_shards(r)
    pl.semaphore_wait(barrier, len(partners))
    width, hidden_width = r.w_out.shape[-1], r.w_up.shape[-1]
    plan = [(r.pack, r.pack_own, 0, 128)]
    plan += [(r.w_qkv, r.qkv_in, k * width, width) for k in range(3)]
    plan += [(r.w_out, r.out_in, 0, width)]
    half = hidden_width // 2
    plan += [(r.w_up, r.up_in, k * half, half, True) for k in range(2)]
    plan += [(r.w_down, r.down_in, k * width // 2, width // 2, True) for k in range(2)]
    gathers = [Gather(r, place, k, *item) for k, item in enumerate(plan)]
    pack, q, k, v, out, up0, up1, down0, down1 = gathers
    pack.start_z()
    q.start_z()
    k.start_z()
    v.start_z()
    pack.start_y()
    q.start_y()
    pack.start_c()
    frame_values(r)
    k.start_y()
    pack.ready()
    unpack_shards(r)
    v.start_y()
    q.start_c()
    load.wait()
    norm_pass(r)
    k.start_c()
    v.start_c()
    for group in (out, up0, up1, down0, down1):
        group.start_z()
    q.ready()
    project_third(r, 0)
    clear(r)
    k.ready()
    project_third(r, 1)
    v.ready()
    project_third(r, 2)

    front(
        r,
        lambda i: at_step(
            i,
            {
                1: [out.start_y],
                3: [up0.start_y, out.start_c],
                5: [up1.start_y, up0.start_x],
                7: [down0.start_y, up1.start_x, up0.start_c],
                9: [down1.start_y, down0.start_x, up1.start_c],
            },
        ),
    )
    out.ready()

    def arrive():
        down1.start_x()
        down0.start_c()
        down1.start_c()
        for group in (up0, up1, down0, down1):
            group.ready()

    middle_part(r, scale, arrive)

    plan = [(r.g_down,), (r.g_up,), (r.g_out,)]
    plan += [(r.g_qkv, k * width) for k in range(3)] + [(r.g_pack,)]
    reduces = [Reduce(r, place, k, *item) for k, item in enumerate(plan)]
    down, up, out, q, k, v, pack = reduces
    down.start_c()
    up.start_c()
    out.start_c()
    attend_back(
        r,
        lambda i: at_step(
            i,
            {
                1: [down.start_y, up.start_x1],
                2: [out.start_x1],
                6: [down.start_z, up.start_y],
                7: [out.start_y],
                9: [up.start_z],
            },
        ),
    )
    qkv_weight_grad(r, 0)
    q.start_c()
    qkv_weight_grad(r, 2)
    v.start_c()
    q.start_y()
    qkv_weight_grad(r, 1)
    k.start_c()
    v.start_x1()
    out.start_z()
    k.start_y()

    def stored(i):
        rows = pl.ds(pl.multiple_of(i * 4 * LENGTH, 4 * LENGTH), 4 * LENGTH)
        return pltpu.make_async_copy(
            r.middle_grad.at[rows, :], r.tokens_grad.at[rows, :], r.store_sem.at[i]
        )

    start_back(
        r,
        lambda i: at_step(
            i,
            {
                2: [down.start_x],
                3: [up.start_x, q.start_z],
                5: [v.start_y, out.start_x],
                6: [k.start_z],
                8: [v.start_z, q.start_x],
            },
        ),
        lambda i: stored(i).start(),
    )
    pack_grads(r)
    pack.start_c()
    k.start_x()
    v.start_x()
    pack.start_y()
    down.finish(r.down_out)
    up.finish(r.up_out)
    pack.start_z()
    out.finish(r.out_out)
    for group in (q, k, v):
        group.finish(r.qkv_out)
    pack.start_x()
    for i in range(r.middle_grad.shape[0] // (4 * LENGTH)):
        stored(i).wait()
    for group in gathers + reduces:
        group.close()
    pack.finish(r.pack_out)


def finish_kernel(names, count, *refs):
    r = Names(names, refs)
    step = 4 * LENGTH
    parts = [pl.ds(at, step) for at in range(0, r.tokens.shape[0], step)]
    loads = [
        pltpu.make_async_copy(r.tokens.at[part, :], r.held.at[part, :], r.load_sem.at[k])
        for k, part in enumerate(parts)
    ]
    stores = [
        pltpu.make_async_copy(r.held.at[part, :], r.o_tokens.at[part, :], r.store_sem.at[k])
        for k, part in enumerate(parts)
    ]
    for load in loads:
        load.start()
    r.o_qkv[...] = r.qkv[...]
    r.o_out[...] = r.out[...]
    r.o_up[...] = r.up[...]
    r.o_down[...] = r.down[...].T
    r.o_stats[...] = DECAY_RATE * r.running[...] + (1.0 - DECAY_RATE) * r.percentiles[...]
    part, positions = r.o_positions.shape
    slots = r.o_actor.shape[0]
    features = r.pack[0:part, :]
    r.o_positions[...] = features[:, POSITION_AT : POSITION_AT + positions]
    turned = features.T
    vectors = (r.gain1, r.bias1, r.gain2, r.bias2, r.bias_down, r.gain3, r.bias3)
    for k, ref in enumerate(vectors):
        ref[...] = turned[SMALL_AT + k : SMALL_AT + k + 1, :].reshape(part)
    r.o_actor[...] = turned[SMALL_AT + 7 : SMALL_AT + 7 + slots, :]
    r.o_actor_bias[...] = turned[BIAS_AT : BIAS_AT + 1, :].reshape(part)[0:slots]
    r.o_loss[...] = features[0:1, LOSS_AT : LOSS_AT + 1] * (1.0 / count)
    r.o_up_bias[...] = r.pack[part : part + 1, :].reshape(128)
    for load, store in zip(loads, stores, strict=True):
        load.wait()
        store.start()
    for store in stores:
        store.wait()


def local_kernel(names, scale, *refs):
    r = Names(names, refs)
    load = pltpu.make_async_copy(r.tokens_in, r.tokens, r.local_sem.at[0])
    load.start()
    clear(r)
    frame_values(r)
    load.wait()
    norm_pass(r)
    for third in range(3):
        project_third(r, third)
    front(r, lambda i: None)
    middle_part(r, scale, lambda: None)
    attend_back(r, lambda i: None)
    for third in range(3):
        qkv_weight_grad(r, third)
    start_back(r, lambda i: None, lambda i: None)
    store = pltpu.make_async_copy(r.middle_grad, r.tokens_grad, r.local_sem.at[1])
    store.start()
    store.wait()


def run(kernel, constant, ins, outs, scratch, flops=0, side_effects=False, collective=None):
    vmem = pl.BlockSpec(memory_space=pltpu.VMEM)
    anywhere = pl.BlockSpec(memory_space=pl.ANY)
    in_specs = [anywhere if array.size > LARGE else vmem for array in ins.values()]
    out_specs = [anywhere if math.prod(shape) > LARGE else vmem for shape, _ in outs.values()]
    return pl.pallas_call(
        functools.partial(kernel, (*ins, *outs, *scratch), constant),
        out_shape=[jax.ShapeDtypeStruct(shape, kind) for shape, kind in outs.values()],
        in_specs=in_specs,
        out_specs=out_specs,
        scratch_shapes=[
            item if not isinstance(item, tuple) else pltpu.VMEM(item[0], item[1])
            for item in scratch.values()
        ],
        compiler_params=pltpu.CompilerParams(
            vmem_limit_bytes=VMEM_BYTES, has_side_effects=side_effects, collective_id=collective
        ),
        cost_estimate=pl.CostEstimate(flops=flops, bytes_accessed=1 << 24, transcendentals=0),
    )(*ins.values())


def on_device(
    tokens,
    positions,
    norm_one_gain,
    norm_one_bias,
    qkv_weight,
    out_weight,
    norm_two_gain,
    norm_two_bias,
    up_weight,
    up_bias,
    down_weight,
    down_bias,
    final_gain,
    final_bias,
    actor_weight,
    actor_bias,
    actions,
    action_masks,
    game_ids,
    returns,
    values,
    running,
    percentiles,
):
    row_count, width = tokens.shape
    seq_count = row_count // LENGTH
    hidden_width = up_weight.shape[1]
    slots = actor_weight.shape[1]
    fsdp = lax.axis_size("fsdp")
    device_count = lax.axis_size("dp") * fsdp
    token_total = row_count * device_count
    scale = float(seq_count * device_count) / token_total
    flops = 6 * row_count * width * (4 * width + 2 * hidden_width)
    part, hidden_part = width // fsdp, hidden_width // fsdp

    vectors = dict(
        gain1=norm_one_gain,
        bias1=norm_one_bias,
        gain2=norm_two_gain,
        bias2=norm_two_bias,
        bias_down=down_bias,
        gain3=final_gain,
        bias3=final_bias,
    )
    stats = dict(running=running, percentiles=percentiles)
    frames = stats | dict(
        tokens_in=tokens,
        actor_bias=actor_bias,
        actions=actions,
        masks=action_masks.T,
        game_ids=game_ids,
        returns=returns,
        values=values,
    )
    scratch = layer_scratch(row_count, width, hidden_width, 16)
    grads = grad_shapes(width, hidden_width, 16)
    weight_shapes = dict(
        w_qkv=(SPLIT + (width // 16, 3 * width), BF16),
        w_out=(SPLIT + (width // 16, width), BF16),
        w_up=(SPLIT + (width // 16, hidden_width), BF16),
        w_down=(SPLIT + (hidden_width // 16, width), BF16),
    )

    if fsdp == 16 and lax.axis_size("dp") == 2:
        ins = frames | vectors
        ins |= dict(qkv_in=qkv_weight, out_in=out_weight, up_in=up_weight, down_in=down_weight)
        ins |= dict(up_bias_in=up_bias, positions_in=positions.T, actor_in=actor_weight.T)
        shard_grads = dict(
            qkv_out=((part, 3 * width), F32),
            out_out=((part, width), F32),
            up_out=((part, hidden_width), F32),
            down_out=((width, hidden_part), F32),
        )
        outs = dict(
            tokens_grad=((row_count, width), F32), pack_out=((PACK_GRAD_ROWS, 128), F32)
        )
        scratch |= grads | weight_shapes
        scratch |= dict(
            pack=(SPLIT + (PACK_ROWS, 128), BF16),
            pack_own=((PACK_ROWS, 128), BF16),
            g_pack=(SPLIT + (PACK_GRAD_ROWS, 128), F32),
            positions=((LENGTH, width), F32),
            small=((8, width), F32),
            actor=((SLOTS, width), BF16),
            up_bias=((1, hidden_width), F32),
            gather_send=pltpu.SemaphoreType.DMA((GATHERS, 15)),
            gather_recv=pltpu.SemaphoreType.DMA((GATHERS, 15)),
            reduce_send=pltpu.SemaphoreType.DMA((len(REDUCES), 16)),
            reduce_recv=pltpu.SemaphoreType.DMA((len(REDUCES), 16)),
            store_sem=pltpu.SemaphoreType.DMA((row_count // (4 * LENGTH),)),
        )
        for index, (count, rows, kind, halved) in enumerate(REDUCES):
            for item, (lead, half) in enumerate(reduce_leads(halved)):
                scratch[index, item] = (lead + (rows, count // 2 if half else count), kind)
        tokens_grad, pack, qkv_g, out_g, up_g, down_g = run(
            spread_kernel, scale, ins, outs | shard_grads, scratch, flops, True, 0
        )
        vector = ((part,), F32)
        final = dict(
            o_loss=((1, 1), F32),
            o_stats=(running.shape, F32),
            o_positions=((part, LENGTH), F32),
            o_qkv=shard_grads["qkv_out"],
            o_out=shard_grads["out_out"],
            o_up=shard_grads["up_out"],
            o_down=((hidden_part, width), F32),
            o_up_bias=((hidden_part,), F32),
            o_actor=((slots, part), F32),
            o_actor_bias=((slots,), F32),
            o_tokens=((row_count, width), F32),
        )
        copies = pltpu.SemaphoreType.DMA((row_count // (4 * LENGTH),))
        done = run(
            finish_kernel,
            token_total,
            stats
            | dict(pack=pack, qkv=qkv_g, out=out_g, up=up_g, down=down_g, tokens=tokens_grad),
            final | dict.fromkeys(vectors, vector),
            dict(held=((row_count, width), F32), load_sem=copies, store_sem=copies),
        )
        loss, new_stats, pos_g, qkv_g, out_g, up_g, down_g = done[:7]
        up_bias_g, actor_g, actor_bias_g, tokens_grad = done[7:11]
        gain1, bias1, gain2, bias2, bias_down, gain3, bias3 = done[11:]
        return (
            loss.reshape(()),
            new_stats,
            tokens_grad,
            pos_g.T,
            gain1,
            bias1,
            qkv_g,
            out_g,
            gain2,
            bias2,
            up_g,
            up_bias_g,
            down_g,
            bias_down,
            gain3,
            bias3,
            actor_g.T,
            actor_bias_g,
        )

    def gather(array, axis):
        return lax.all_gather(array, "fsdp", axis=axis, tiled=True)

    packed = gather(
        jnp.concatenate([jnp.stack(list(vectors.values())), actor_weight.T, positions], 0), 1
    )
    fulls = [gather(weight, 0) for weight in (qkv_weight, out_weight, up_weight, down_weight)]
    ins = frames | {
        name: full.reshape(weight_shapes[name][0])
        for name, full in zip(weight_shapes, fulls, strict=True)
    }
    ins |= dict(
        positions=packed[7 + slots :].astype(F32),
        small=jnp.pad(packed[0:7].astype(F32), ((0, 1), (0, 0))),
        actor=jnp.pad(packed[7 : 7 + slots], ((0, SLOTS - slots), (0, 0))),
        up_bias=gather(up_bias, 0).astype(F32).reshape(1, hidden_width),
    )
    outs = dict(tokens_grad=((row_count, width), F32)) | grads
    tokens_grad, *sums = run(local_kernel, scale, ins, outs, scratch, flops)
    sums = Names(grads, sums)

    def scatter(array, axis):
        piece = lax.psum_scatter(array, "fsdp", scatter_dimension=axis, tiled=True)
        return lax.psum(piece.astype(BF16), "dp").astype(F32)

    down_sum = jnp.swapaxes(sums.g_down, 3, 4)
    qkv_part, out_part, up_part, down_part = (
        scatter(merged(grad).astype(F32), 0)
        for grad in (sums.g_qkv, sums.g_out, sums.g_up, down_sum)
    )
    rows = [jnp.sum(sums.g_small, 1), sums.g_actor[:slots], sums.g_positions]
    side = scatter(jnp.concatenate(rows, 0), 1)
    up_bias_part = scatter(jnp.sum(sums.g_up_bias, 0), 0)
    head_total = lax.psum(jnp.sum(sums.head_sums[: SLOTS + 1], 1), ("dp", "fsdp"))
    return (
        head_total[SLOTS] / token_total,
        DECAY_RATE * running + (1.0 - DECAY_RATE) * percentiles,
        tokens_grad,
        side[7 + slots :],
        side[G1],
        side[B1],
        qkv_part,
        out_part,
        side[G2],
        side[B2],
        up_part,
        up_bias_part,
        down_part,
        side[DB],
        side[GL],
        side[BL],
        side[7 : 7 + slots].T,
        head_total[:slots],
    )


def solution(mesh):
    rows, cols, both = P(("dp", "fsdp"), None), P(None, "fsdp"), P(("dp", "fsdp"))
    weight, vector, whole = P("fsdp", None), P("fsdp"), P()
    in_specs = (rows, cols, vector, vector, weight, weight, vector, vector, weight, vector)
    in_specs += (weight, vector, vector, vector, weight, whole, both, rows, both, both, both)
    in_specs += (whole, whole)
    out_specs = (whole, whole, rows, cols, vector, vector, weight, weight, vector, vector)
    out_specs += (weight, vector, weight, vector, vector, vector, weight, whole)
    return jax.shard_map(
        on_device, mesh=mesh, in_specs=in_specs, out_specs=out_specs, check_vma=False
    )
```

```python
import functools
import math
import math

import jax
import jax.numpy as jnp
from jax import lax
from jax.experimental import pallas as pl
from jax.experimental.pallas import tpu as pltpu
from jax.sharding import PartitionSpec as P

HEADS = 8
HEAD = 64
LENGTH = 64
QUAD = 4
WIDE = QUAD * HEAD
MASKED = -1e30
EPSILON = 1e-05
DECAY_RATE = 0.9
ENTROPY_WEIGHT = 0.1
SLOTS = 32
VMEM_BYTES = 63 * 1024 * 1024
BF16 = jnp.bfloat16
F32 = jnp.float32

G1, B1, G2, B2, DB, GL, BL = range(7)
MESH = pl.DeviceIdType.MESH


def dot(left, right, left_dim, right_dim):
    return lax.dot_general(
        left, right, (((left_dim,), (right_dim,)), ((), ())), preferred_element_type=F32
    )


def mean_last(values):
    return jnp.sum(values, -1, keepdims=True) * (1.0 / values.shape[-1])


def normalise(values):
    centred = values - mean_last(values)
    scale = lax.rsqrt(mean_last(centred * centred) + EPSILON)
    return centred * scale, scale


def norm_back(unit, scale, gain, upstream):
    inner = upstream * gain
    return scale * (inner - mean_last(inner) - unit * mean_last(inner * unit))


def fold_rows(values):
    rows, width = values.shape
    return jnp.sum(values.reshape(rows // 8, 8, width), 0)


def gelu_pair(values):
    half = jnp.exp2(values * values * (-0.5 * 1.4426950408889634))
    span = 1.0 + jnp.abs(values) * (0.3275911 * 0.7071067811865476)
    t = 1.0 / span
    poly = t * (
        0.5 * 0.254829592
        + t
        * (
            0.5 * -0.284496736
            + t * (0.5 * 1.421413741 + t * (0.5 * -1.453152027 + t * (0.5 * 1.061405429)))
        )
    )
    tail = poly * half
    cdf = jnp.where(values < 0.0, tail, 1.0 - tail)
    density = half * 0.3989422804014327
    return values * cdf, cdf + values * density


def pair_masks():
    lane = lax.broadcasted_iota(jnp.int32, (LENGTH, 2 * HEAD), 1)
    first = jnp.where(lane < HEAD, 1.0, 0.0)
    return first.astype(BF16), (1.0 - first).astype(BF16)


def spread_heads(rows, masks):
    zero = jnp.zeros((LENGTH, 2 * HEAD), BF16)
    left, right = rows[:, : 2 * HEAD], rows[:, 2 * HEAD :]
    blocks = [jnp.concatenate([left * mask, zero], 1) for mask in masks]
    blocks += [jnp.concatenate([zero, right * mask], 1) for mask in masks]
    return jnp.concatenate(blocks, 0)


def gather_heads(blocks):
    lane = lax.broadcasted_iota(jnp.int32, (LENGTH, 2 * HEAD), 1)
    pairs = []
    for pair in range(QUAD // 2):
        lanes = slice(pair * 2 * HEAD, (pair + 1) * 2 * HEAD)
        low = 2 * pair * HEAD
        first, second = blocks[low : low + HEAD, lanes], blocks[low + HEAD : low + 2 * HEAD, lanes]
        pairs.append(jnp.where(lane < HEAD, first, second))
    return jnp.concatenate(pairs, 1)


def causal_bias():
    key = lax.broadcasted_iota(jnp.int32, (LENGTH, WIDE), 0)
    query = lax.rem(lax.broadcasted_iota(jnp.int32, (LENGTH, WIDE), 1), HEAD)
    return jnp.where(key <= query, 0.0, MASKED)


LOG2E = 1.4426950408889634
SCORE_SCALE = HEAD ** (-0.5) * LOG2E


def chains(r, i):
    width = r.tokens.shape[1]
    found = []
    for s in range(4):
        row = pl.multiple_of((4 * i + s) * LENGTH, LENGTH)
        for half in range(width // WIDE):
            at = half * WIDE
            columns = [slice(k * width + at, k * width + at + WIDE) for k in range(3)]
            found.append((4 * i + s, pl.ds(row, LENGTH), columns))
    return found


def attend_group(r, i):
    masks, bias = pair_masks(), r.causal[...]
    group = chains(r, i)
    loaded = [[r.qkv[rows, part] for part in parts] for _, rows, parts in group]
    scores = [dot(key, spread_heads(query, masks), 1, 1) for query, key, _ in loaded]
    probs, totals = [], []
    for score in scores:
        score = score * SCORE_SCALE + bias
        highest = jnp.max(score, 0, keepdims=True)
        weights = jnp.exp2(score - highest)
        summed = jnp.sum(weights, 0, keepdims=True)
        probs.append((weights * (1.0 / summed)).astype(BF16))
        totals.append(highest + jnp.log(summed) * LOG2E)
    blocks = [dot(prob, value, 0, 0) for prob, (_, _, value) in zip(probs, loaded, strict=True)]
    done = [gather_heads(block).astype(BF16) for block in blocks]
    for (seq, rows, (q, _, _)), result, total in zip(group, done, totals, strict=True):
        r.attended[rows, q] = result
        r.totals[pl.ds(seq, 1), q] = total


def attend_back_group(r, i):
    masks, bias = pair_masks(), r.causal[...]
    done = []
    for half in range(2):
        group = chains(r, i)[half::2]
        queries = [spread_heads(r.qkv[rows, q], masks) for _, rows, (q, _, _) in group]
        aboves = [spread_heads(r.attended[rows, q], masks) for _, rows, (q, _, _) in group]
        scores = [
            dot(r.qkv[rows, k], query, 1, 1)
            for (_, rows, (_, k, _)), query in zip(group, queries, strict=True)
        ]
        prob_grads = [
            dot(r.qkv[rows, v], above, 1, 1)
            for (_, rows, (_, _, v)), above in zip(group, aboves, strict=True)
        ]
        probs, score_grads = [], []
        for (seq, _, (q, _, _)), score, pull in zip(group, scores, prob_grads, strict=True):
            prob = jnp.exp2(score * SCORE_SCALE + bias - r.totals[pl.ds(seq, 1), q])
            row_terms = jnp.sum(pull * prob, 0, keepdims=True)
            score_grads.append((prob * (pull - row_terms)).astype(BF16))
            probs.append(prob.astype(BF16))
        value_grads = [dot(prob, above, 1, 0) for prob, above in zip(probs, aboves, strict=True)]
        key_grads = [dot(grad, query, 1, 0) for grad, query in zip(score_grads, queries, strict=True)]
        query_grads = [
            dot(grad, r.qkv[rows, k], 0, 0)
            for (_, rows, (_, k, _)), grad in zip(group, score_grads, strict=True)
        ]
        for (_, rows, (q, k, v)), dq, dk, dv in zip(
            group, query_grads, key_grads, value_grads, strict=True
        ):
            done.append((rows, q, (gather_heads(dq) * HEAD ** (-0.5)).astype(BF16)))
            done.append((rows, k, (dk * HEAD ** (-0.5)).astype(BF16)))
            done.append((rows, v, dv.astype(BF16)))
    for rows, columns, grad in done:
        r.qkv[rows, columns] = grad


def policy(logits, masks, actions, advantage, scale):
    allowed = masks > 0
    held = jnp.where(allowed, logits, MASKED)
    shifted = held - jnp.max(held, 0, keepdims=True)
    weights = jnp.exp(shifted)
    summed = jnp.sum(weights, 0, keepdims=True)
    log_probs = shifted - jnp.log(summed)
    probs = weights * (1.0 / summed)
    plogp = jnp.where(allowed, probs * log_probs, 0.0)
    entropy = -jnp.sum(plogp, 0, keepdims=True)
    slot = lax.broadcasted_iota(jnp.int32, logits.shape, 0)
    taken = slot == actions
    chosen = jnp.sum(jnp.where(taken, log_probs, 0.0), 0, keepdims=True)
    loss = -advantage * chosen - ENTROPY_WEIGHT * entropy
    pull = advantage * (probs - jnp.where(taken, 1.0, 0.0)) + ENTROPY_WEIGHT * (
        plogp + probs * entropy
    )
    return loss, jnp.where(allowed, pull * scale, 0.0)


STRIP = 32
THIN = 16
LARGE = 1 << 20


class Names:
    def __init__(self, names, refs):
        self.table = dict(zip(names, refs, strict=True))

    def __getattr__(self, name):
        return self.table[name]


SPLIT = (4, 2, 2)
PACK_ROWS = 48
PACK_GRAD_ROWS = 40
POSITION_AT, SMALL_AT, BIAS_AT, LOSS_AT = 0, 64, 96, 97


def merged(block):
    return block.reshape(-1, block.shape[-1])


def strip_rows(row, count):
    return [pl.ds(pl.multiple_of(row + at, STRIP), STRIP) for at in range(0, count, STRIP)]


def load_starts(r, row, count):
    starts = [r.tokens[rows, :].astype(F32) for rows in strip_rows(row, count)]
    frames = [r.positions[at : at + STRIP, :] for at in range(0, LENGTH, STRIP)]
    return [start + frames[k % len(frames)] for k, start in enumerate(starts)]


def norm_pass(r):
    count = r.tokens.shape[0]
    rows = 4 * LENGTH

    def body(i, carry):
        row = pl.multiple_of(i * rows, rows)
        normed = [
            (normalise(start)[0] * r.small[G1 : G1 + 1, :] + r.small[B1 : B1 + 1, :]).astype(BF16)
            for start in load_starts(r, row, rows)
        ]
        normed = jnp.concatenate(normed, 0)
        turned = normed.T
        r.attended[pl.ds(row, rows), :] = normed
        r.normed_t[:, pl.ds(row, rows)] = turned
        return carry

    lax.fori_loop(0, count // rows, body, 0)


def project_third(r, third):
    count, width = r.tokens.shape
    rows = 8 * LENGTH
    columns = slice(third * width, (third + 1) * width)

    def body(i, carry):
        here = pl.ds(pl.multiple_of(i * rows, rows), rows)
        weight = merged(r.w_qkv[:, :, :, :, columns])
        r.qkv[here, columns] = dot(r.attended[here, :], weight, 1, 0).astype(BF16)
        return carry

    lax.fori_loop(0, count // rows, body, 0)


def front(r, pump):
    count = r.tokens.shape[0]

    def body(i, carry):
        pump(i)
        attend_group(r, i)
        return carry

    lax.fori_loop(0, count // (4 * LENGTH), body, 0)


def add_grad(ref, index, values):
    ref[index] += values.reshape(ref[index].shape)


def add_columns(ref, values):
    count = ref.shape[-1]
    for k in range(values.shape[1] // count):
        ref[k // 2, k % 2] += values[:, k * count : (k + 1) * count]


def clear(r):
    for ref in (r.g_out, r.g_up, r.g_down):

        def body(z, carry, ref=ref):
            ref[z] = jnp.zeros(ref.shape[1:], F32)
            return carry

        lax.fori_loop(0, ref.shape[0], body, 0)
    for ref in (r.g_actor, r.g_small, r.g_up_bias, r.g_positions, r.head_sums):
        ref[...] = jnp.zeros_like(ref)


def frame_values(r):
    r.causal[...] = causal_bias()
    fresh = DECAY_RATE * r.running[...] + (1.0 - DECAY_RATE) * r.percentiles[...]
    spread = jnp.maximum(1.0, fresh[1:2, :] - fresh[0:1, :])
    seqs = r.game_ids.shape[0]
    game = r.game_ids[...].reshape(seqs, 1)
    slot = lax.broadcasted_iota(jnp.int32, (seqs, spread.shape[1]), 1)
    column = jnp.sum(jnp.where(slot == game, spread, 0.0), 1, keepdims=True)
    count = 8 * LENGTH
    owner = lax.broadcasted_iota(jnp.int32, (8, count), 0)
    frame = lax.broadcasted_iota(jnp.int32, (8, count), 1)
    for k in range(seqs // 8):
        here = slice(k * count, (k + 1) * count)
        near = jnp.where(frame // LENGTH == owner, column[8 * k : 8 * k + 8], 0.0)
        wide = jnp.sum(near, 0, keepdims=True)
        r.advantage[:, here] = (r.returns[here] - r.values[here]).reshape(1, count) / wide
        r.action_row[:, here] = r.actions[here].reshape(1, count)


class Tile:
    def __init__(self, r, side):
        def pick(name):
            return r.table[name, side]

        self.active, self.slope = pick("active"), pick("slope")
        self.two_t, self.unit, self.last = pick("two_t"), pick("unit"), pick("last")
        self.scale = pick("scale")


def middle_part(r, scale, arrive):
    count, width = r.tokens.shape
    rows = r.low.shape[0]
    shards = r.w_up.shape[0]
    chunk = r.w_up.shape[-1] // shards
    slots = r.masks.shape[0]
    out_weight = r.w_out
    head_bias = jnp.concatenate(
        [r.actor_bias[...].astype(F32).reshape(slots, 1), jnp.zeros((SLOTS - slots, 1), F32)], 0
    )
    everything = slice(None)
    strips = [slice(at, at + STRIP) for at in range(0, rows, STRIP)]

    def gain(k):
        return r.small[k : k + 1, :]

    def tile_rows(i):
        return pl.ds(pl.multiple_of(i * rows, rows), rows)

    def before(t, tokens, attended):
        projected = dot(attended, merged(out_weight[...]), 1, 0)
        for k, strip in enumerate(strips):
            frame = k * STRIP % LENGTH
            start = tokens[k].astype(F32) + r.positions[frame : frame + STRIP, :]
            mid = start + projected[strip]
            unit, spread = normalise(mid)
            r.two_low[strip, :] = (unit * gain(G2) + gain(B2)).astype(BF16)
            t.unit[strip, :] = unit
            t.scale[strip, :] = spread
            t.last[strip, :] = mid + gain(DB)
        t.two_t[...] = r.two_low[...].T

    def columns(j):
        return slice(j * chunk, (j + 1) * chunk)

    def up_weight(j):
        return merged(r.w_up[:, :, :, :, columns(j)])

    def activate(hidden, bias):
        done = [gelu_pair(hidden[at : at + THIN] + bias) for at in range(0, rows, THIN)]
        values = jnp.concatenate([value.astype(BF16) for value, _ in done], 0)
        return values, jnp.concatenate([slope.astype(BF16) for _, slope in done], 0)

    def forward_only(j, t):
        cols = columns(j)
        weight, bias, down = up_weight(j), r.up_bias[:, cols], merged(r.w_down[j])
        active, slope = activate(dot(r.two_low[...], weight, 1, 0), bias)
        t.last[...] += dot(active, down, 1, 0)
        t.active[:, cols], t.slope[:, cols] = active, slope

    def both_ways(j, here, there):
        cols = columns(j)
        bias, total = r.up_bias[:, cols], r.g_up_bias[:, cols]
        if there is not None:
            hidden = dot(r.two_low[...], up_weight(j), 1, 0)
        above = dot(r.low[...], merged(r.w_down[j]), 1, 1)
        for at in range(0, rows, THIN):
            strip = slice(at, at + THIN)
            part = (above[strip] * here.slope[strip, cols].astype(F32)).astype(BF16)
            r.hidden_grad[strip, :] = part
            total += fold_rows(part.astype(F32))
        add_columns(r.g_down.at[j], dot(r.low_t[...], here.active[:, cols], 1, 0))
        r.two_in[...] += dot(r.hidden_grad[...], up_weight(j), 1, 1)
        add_grad(
            r.g_up,
            (everything, everything, everything, everything, cols),
            dot(here.two_t[...], r.hidden_grad[...], 1, 0),
        )
        r.g_up_bias[:, cols] = total
        if there is not None:
            active, slope = activate(hidden, bias)
            there.last[...] += dot(active, merged(r.w_down[j]), 1, 0)
            there.active[:, cols], there.slope[:, cols] = active, slope

    def chunks(step):
        for j in range(shards):
            step(j)

    def last_norm(t):
        spreads = []
        for strip in strips:
            unit, spread = normalise(t.last[strip, :])
            r.low[strip, :] = (unit * gain(GL) + gain(BL)).astype(BF16)
            t.last[strip, :] = unit
            spreads.append(spread)
        return spreads, dot(r.actor[...], r.low[...], 1, 1) + head_bias

    def head(logits, masks, actions, advantage):
        masks = jnp.concatenate([masks, jnp.zeros((SLOTS - slots, rows), jnp.int32)], 0)
        loss, pull = policy(logits, masks, actions, advantage, scale)
        logit_grad = pull.astype(BF16)
        last_in = dot(logit_grad, r.actor[...], 0, 0)
        r.g_actor[...] += dot(logit_grad, r.low[...], 1, 0)
        wide_grad = logit_grad.astype(F32)
        fold = r.head_sums[0:SLOTS, :]
        for at in range(0, rows, 128):
            fold += wide_grad[:, at : at + 128]
        r.head_sums[0:SLOTS, :] = fold
        fold = r.head_sums[SLOTS : SLOTS + 1, :]
        for at in range(0, rows, 128):
            fold += loss[:, at : at + 128]
        r.head_sums[SLOTS : SLOTS + 1, :] = fold
        return last_in

    def last_norm_back(t, spreads, last_in):
        sums = [r.g_small[k] for k in (GL, BL, DB)]
        for strip, spread in zip(strips, spreads, strict=True):
            above, unit = last_in[strip], t.last[strip, :]
            grad = norm_back(unit, spread, gain(GL), above)
            sums[0] += fold_rows(above * unit)
            sums[1] += fold_rows(above)
            sums[2] += fold_rows(grad)
            t.last[strip, :] = grad
            r.low[strip, :] = grad.astype(BF16)
        for k, total in zip((GL, BL, DB), sums, strict=True):
            r.g_small[k] = total
        r.low_t[...] = r.low[...].T
        r.two_in[...] = jnp.zeros((rows, width), F32)

    def two_norm_back(t):
        sums = [r.g_small[k] for k in (G2, B2)]
        for strip in strips:
            above, unit = r.two_in[strip, :], t.unit[strip, :]
            sums[0] += fold_rows(above * unit)
            sums[1] += fold_rows(above)
            grad = t.last[strip, :] + norm_back(unit, t.scale[strip, :], gain(G2), above)
            t.last[strip, :] = grad
            r.hidden_grad[strip, :] = grad.astype(BF16)
        for k, total in zip((G2, B2), sums, strict=True):
            r.g_small[k] = total

    def out_back(i, t, attended):
        low = r.hidden_grad[...]
        add_grad(r.g_out, ..., dot(attended, low, 0, 0))
        r.attended[tile_rows(i), :] = dot(low, merged(out_weight[...]), 1, 1).astype(BF16)
        r.middle_grad[tile_rows(i), :] = t.last[...]

    sides = [Tile(r, 0), Tile(r, 1)]
    tiles = count // rows

    def begin(i):
        row = pl.multiple_of(i * rows, rows)
        return [r.tokens[part, :] for part in strip_rows(row, rows)], r.attended[tile_rows(i), :]

    def step(i, side, first=False, last=False):
        here, there = sides[side], sides[1 - side]
        at = tile_rows(i)
        side_data = r.masks[:, at], r.action_row[:, at], r.advantage[:, at]
        if not first:
            attended = r.attended[tile_rows(i - 1), :]
        if not last:
            ahead = begin(i + 1)
        spreads, logits = last_norm(here)
        if not first:
            two_norm_back(there)
        last_in = head(logits, *side_data)
        if not first:
            out_back(i - 1, there, attended)
        last_norm_back(here, spreads, last_in)
        if not last:
            before(there, *ahead)
        chunks(lambda j: both_ways(j, here, None if last else there))

    before(sides[0], *begin(0))
    arrive()
    chunks(lambda j: forward_only(j, sides[0]))
    step(0, 0, first=True)

    def pair(p, carry):
        step(2 * p + 1, 1)
        step(2 * p + 2, 0)
        return carry

    lax.fori_loop(0, (tiles - 2) // 2, pair, 0)
    step(tiles - 1, 1, last=True)
    two_norm_back(sides[1])
    out_back(tiles - 1, sides[1], r.attended[tile_rows(tiles - 1), :])


def attend_back(r, pump):
    count = r.tokens.shape[0]
    rows = 4 * LENGTH

    def body(i, carry):
        pump(i)
        attend_back_group(r, i)
        return carry

    lax.fori_loop(0, count // rows, body, 0)


def qkv_weight_grad(r, third):
    width = r.tokens.shape[1]
    step = width // 2
    for at in range(third * width, (third + 1) * width, step):
        values = dot(r.normed_t[...], r.qkv[:, at : at + step], 1, 0)
        values = values.astype(BF16).reshape(r.g_qkv.shape[:4] + (step,))
        r.g_qkv[:, :, :, :, at : at + step] = values


def start_back(r, pump, tile_done):
    count = r.tokens.shape[0]
    rows = 4 * LENGTH
    gain = r.small[G1 : G1 + 1, :]

    def body(i, carry):
        pump(i)
        row = pl.multiple_of(i * rows, rows)
        starts = load_starts(r, row, rows)
        one_in = dot(r.qkv[pl.ds(row, rows), :], merged(r.w_qkv[...]), 1, 1)
        sums = [r.g_small[k] for k in (G1, B1)]
        frames = [r.g_positions[at : at + STRIP, :] for at in range(0, LENGTH, STRIP)]
        grads = []
        for k, (start, there) in enumerate(zip(starts, strip_rows(row, rows), strict=True)):
            unit, scale = normalise(start)
            above = one_in[k * STRIP : (k + 1) * STRIP]
            sums[0] += fold_rows(above * unit)
            sums[1] += fold_rows(above)
            grads.append(r.middle_grad[there, :] + norm_back(unit, scale, gain, above))
            frames[k % len(frames)] += grads[k]
        r.g_positions[...] = jnp.concatenate(frames, 0)
        for k, total in zip((G1, B1), sums, strict=True):
            r.g_small[k] = total
        r.middle_grad[pl.ds(row, rows), :] = jnp.concatenate(grads, 0)
        tile_done(i)
        return carry

    lax.fori_loop(0, count // rows, body, 0)


def pack_shards(r):
    part = r.positions_in.shape[0]
    slots = r.masks.shape[0]
    rows = [
        ref[...].astype(F32).reshape(1, part)
        for ref in (r.gain1, r.bias1, r.gain2, r.bias2, r.bias_down, r.gain3, r.bias3)
    ]
    rows += [r.actor_in[...].astype(F32), jnp.zeros((32 - 7 - slots, part), F32)]
    features = jnp.concatenate(
        [r.positions_in[...].astype(F32), jnp.concatenate(rows, 0).T, jnp.zeros((part, 32), F32)], 1
    )
    bias = r.up_bias_in[...].astype(F32).reshape(1, 128)
    packed = jnp.concatenate([features, bias, jnp.zeros((PACK_ROWS - part - 1, 128), F32)], 0)
    r.pack_own[...] = packed.astype(BF16)


def unpack_shards(r):
    slots = r.masks.shape[0]
    blocks = r.pack[...].astype(F32).reshape(-1, PACK_ROWS, 128)
    part = r.positions_in.shape[0]
    features = merged(blocks[:, :part, :]).T
    r.positions[...] = features[POSITION_AT : POSITION_AT + LENGTH]
    small = features[SMALL_AT : SMALL_AT + 32]
    r.small[...] = small[0:8]
    width = small.shape[1]
    r.actor[...] = jnp.concatenate(
        [small[7 : 7 + slots], jnp.zeros((SLOTS - slots, width), F32)], 0
    ).astype(BF16)
    r.up_bias[...] = jnp.concatenate(
        [blocks[f, part : part + 1, :] for f in range(blocks.shape[0])], 1
    )


def small_rows(r):
    slots = r.masks.shape[0]
    rows = [jnp.sum(r.g_small[k], 0, keepdims=True) for k in range(7)]
    return jnp.concatenate(
        rows + [r.g_actor[0:slots, :], jnp.zeros((32 - 7 - slots, rows[0].shape[1]), F32)], 0
    )


def pack_grads(r):
    width = r.tokens.shape[1]
    part = r.positions_in.shape[0]
    features = jnp.concatenate(
        [r.g_positions[...], small_rows(r), jnp.zeros((128 - SMALL_AT - 32, width), F32)], 0
    ).T
    sums = jnp.sum(r.head_sums[0 : SLOTS + 8, :], 1, keepdims=True)
    lane = lax.broadcasted_iota(jnp.int32, (part, 128), 1)
    bias = jnp.sum(r.g_up_bias[...], 0, keepdims=True)
    shape = r.g_pack.shape
    for f in range(width // part):
        block = features[f * part : (f + 1) * part]
        block = jnp.where(lane == BIAS_AT, sums[0:SLOTS], block)
        block = jnp.where(lane == LOSS_AT, sums[SLOTS : SLOTS + 1], block)
        owner = (f // 4, f // 2 % 2, f % 2)
        rows = [block, bias[:, f * 128 : (f + 1) * 128], jnp.zeros((shape[3] - part - 1, 128), F32)]
        r.g_pack[owner] = jnp.concatenate(rows, 0)


GATHERS = 9
REDUCES = (
    (128, 512, BF16, False),
    (2048, 32, BF16, True),
    (512, 32, BF16, True),
    (512, 32, BF16, False),
    (512, 32, BF16, False),
    (512, 32, BF16, True),
    (128, PACK_GRAD_ROWS, F32, False),
)


class Place:
    def __init__(self):
        self.x = lax.axis_index("dp")
        f = lax.axis_index("fsdp")
        self.z, self.y, self.c = f // 4, f // 2 % 2, f % 2

    def at(self, x=None, z=None, y=None, c=None):
        pick = lambda new, old: old if new is None else new
        f = pick(z, self.z) * 4 + pick(y, self.y) * 2 + pick(c, self.c)
        return (pick(x, self.x), f)

    def z_partner(self, k):
        return (self.z + 1 - 2 * (self.z % 2), (self.z + 2) % 4, 3 - self.z)[k]

    def lines(self):
        return [self.z] + [self.z_partner(k) for k in range(3)]

    def partners(self):
        return [self.at(z=self.z_partner(k)) for k in range(3)] + [
            self.at(y=1 - self.y),
            self.at(c=1 - self.c),
            self.at(x=1 - self.x),
        ]


def remote(r_send, r_recv, index):
    def copy(src, dst, k, device):
        return pltpu.make_async_remote_copy(
            src_ref=src,
            dst_ref=dst,
            send_sem=r_send.at[index, k],
            recv_sem=r_recv.at[index, k],
            device_id=device,
            device_id_type=MESH,
        )

    return copy


class Gather:
    def __init__(self, r, place, index, full, own, at, count, halved=False):
        p = place
        copy = remote(r.gather_send, r.gather_recv, index)
        cols = part = slice(at, at + count)
        if halved:
            part = pl.ds(pl.multiple_of(at + p.x * (count // 2), 128), count // 2)
        self.full, self.own, self.part, self.place, self.halved = full, own, part, place, halved
        mine = full.at[p.z, p.y, p.c, :, part]
        self.z = [copy(own.at[:, part], mine, k, p.at(z=p.z_partner(k))) for k in range(3)]
        self.y, self.x, self.near, self.far = [], [], [], []
        for k, z in enumerate(p.lines()):
            shard = full.at[z, p.y, p.c, :, part]
            self.y.append(copy(shard, shard, 3 + k, p.at(y=1 - p.y)))
            if halved:
                pair = full.at[z, :, p.c, :, part]
                self.x.append(copy(pair, pair, 7 + k, p.at(x=1 - p.x)))
                pair = full.at[z, :, p.c, :, cols]
                self.far.append(copy(pair, pair, 11 + k, p.at(c=1 - p.c)))
            else:
                self.near.append(copy(shard, shard, 7 + k, p.at(c=1 - p.c)))
                shard = full.at[z, 1 - p.y, p.c, :, part]
                self.far.append(copy(shard, shard, 11 + k, p.at(c=1 - p.c)))

    def start_z(self):
        for copy in self.z:
            copy.start()
        p = self.place
        self.full[p.z, p.y, p.c, :, self.part] = self.own[:, self.part]
        self.y[0].start()
        if not self.halved:
            self.near[0].start()

    def start_y(self):
        for k, copy in enumerate(self.z):
            copy.wait_recv()
            self.y[k + 1].start()
            if not self.halved:
                self.near[k + 1].start()

    def start_x(self):
        for arrived, copy in zip(self.y, self.x, strict=True):
            arrived.wait_recv()
            copy.start()

    def start_c(self):
        for arrived, copy in zip(self.x if self.halved else self.y, self.far, strict=True):
            arrived.wait_recv()
            copy.start()

    def ready(self):
        for copy in self.near + self.far:
            copy.wait_recv()

    def close(self):
        for copy in self.z + self.y + self.x + self.near + self.far:
            copy.wait_send()


class Reduce:
    def __init__(self, r, place, index, grad, at=0):
        count, _, kind, halved = REDUCES[index]
        self.grad, self.place, self.kind, self.halved = grad, place, kind, halved
        p = place
        copy = remote(r.reduce_send, r.reduce_recv, index)
        self.cols = slice(at, at + count)
        self.buffers = [r.table[index, part] for part in range(len(reduce_leads(halved)))]
        sc, rc, ry, rz, rx = self.buffers[:5]
        keep = count
        self.part = self.cols
        self.lines = p.lines()
        if halved:
            keep = count // 2
            self.part = self.half(at, keep, p.x)
            self.away = self.half(at, keep, 1 - p.x)
            self.local, self.local_away = self.half(0, keep, p.x), self.half(0, keep, 1 - p.x)
            held = self.buffers[5]
            self.sx1 = sc.at[:, :, :, 0:keep]
            self.x1 = [
                copy(self.sx1.at[z], held.at[z], 12 + k, p.at(x=1 - p.x))
                for k, z in enumerate(self.lines)
            ]
        tail = slice(count - keep, count)
        self.sy = sc.at[:, 0, :, tail]
        self.sz = [sc.at[k, 1, :, tail] for k in range(3)]
        self.sx = sc.at[3, 1, :, tail]
        self.c, self.y = [], []
        for k, z in enumerate(self.lines):
            self.c.append(copy(sc.at[z], rc.at[z], k, p.at(c=1 - p.c)))
            self.y.append(copy(self.sy.at[z], ry.at[z], 4 + k, p.at(y=1 - p.y)))
        self.z = [copy(self.sz[k], rz.at[k], 8 + k, p.at(z=p.z_partner(k))) for k in range(3)]
        self.x = copy(self.sx, rx, 11, p.at(x=1 - p.x))

    @staticmethod
    def half(at, keep, x):
        return pl.ds(pl.multiple_of(at + x * keep, 128), keep)

    def add(self, index, values):
        total = self.grad[index].astype(F32) + values.astype(F32)
        self.grad[index] = total.astype(self.grad.dtype)

    def start_c(self):
        sc, p = self.buffers[0], self.place
        for z, copy in zip(self.lines, self.c, strict=True):
            sc[z] = self.grad[z, :, 1 - p.c, :, self.cols].astype(self.kind)
            copy.start()

    def start_x1(self):
        rc, p = self.buffers[1], self.place
        for z, arrived, copy in zip(self.lines, self.c, self.x1, strict=True):
            arrived.wait()
            away = self.grad[z, :, p.c, :, self.away].astype(F32)
            away += rc[z, :, :, self.local_away].astype(F32)
            self.sx1[z] = away.astype(self.kind)
            copy.start()
            self.add((z, slice(None), p.c, slice(None), self.part), rc[z, :, :, self.local])

    def start_y(self):
        p = self.place
        held = self.buffers[5 if self.halved else 1]
        for k, z in enumerate(self.lines):
            if self.halved:
                self.x1[k].wait_recv()
            else:
                self.c[k].wait()
            away = self.grad[z, 1 - p.y, p.c, :, self.part].astype(F32)
            away += held[z, 1 - p.y].astype(F32)
            self.sy[z] = away.astype(self.kind)
            self.y[k].start()
            self.add((z, p.y, p.c, slice(None), self.part), held[z, p.y])

    def start_z(self):
        ry, p = self.buffers[2], self.place
        for k in range(3):
            owner = self.lines[k + 1]
            self.y[k + 1].wait_recv()
            away = self.grad[owner, p.y, p.c, :, self.part].astype(F32) + ry[owner].astype(F32)
            self.sz[k][...] = away.astype(self.kind)
            self.z[k].start()
        self.y[0].wait_recv()
        self.add((p.z, p.y, p.c, slice(None), self.part), ry[p.z])

    def start_x(self):
        rz, p = self.buffers[3], self.place
        for copy in self.z:
            copy.wait_recv()
        near = self.grad[p.z, p.y, p.c, :, self.part].astype(F32) + rz[0].astype(F32)
        self.sx[...] = (near + (rz[1].astype(F32) + rz[2].astype(F32))).astype(self.kind)
        self.x.start()

    def finish(self, out):
        rx = self.buffers[4]
        self.x.wait_recv()
        if self.halved:
            out[:, self.part] = self.sx[...].astype(F32)
            out[:, self.away] = rx[...].astype(F32)
        else:
            out[:, self.cols] = self.sx[...].astype(F32) + rx[...].astype(F32)

    def close(self):
        for copy in self.z + self.y + [self.x] + (self.x1 if self.halved else []):
            copy.wait_send()


def reduce_leads(halved):
    leads = [((4, 2), False), ((4, 2), False), ((4,), halved), ((3,), halved), ((), halved)]
    return leads + ([((4, 2), True)] if halved else [])


def layer_scratch(row_count, width, hidden_width, shards):
    tile = 256
    seqs = row_count // LENGTH
    pairs = dict(
        active=((tile, hidden_width), BF16),
        slope=((tile, hidden_width), BF16),
        two_t=((width, tile), BF16),
        unit=((tile, width), F32),
        last=((tile, width), F32),
        scale=((tile, 1), F32),
    )
    both = {(name, side): item for name, item in pairs.items() for side in range(2)}
    return both | dict(
        tokens=((row_count, width), BF16),
        middle_grad=((row_count, width), F32),
        normed_t=((width, row_count), BF16),
        qkv=((row_count, 3 * width), BF16),
        attended=((row_count, width), BF16),
        totals=((seqs, width), F32),
        causal=((LENGTH, WIDE), F32),
        advantage=((1, row_count), F32),
        action_row=((1, row_count), jnp.int32),
        two_low=((tile, width), BF16),
        low=((tile, width), BF16),
        low_t=((width, tile), BF16),
        two_in=((tile, width), F32),
        hidden_grad=((tile, hidden_width // 4), BF16),
        local_sem=pltpu.SemaphoreType.DMA((2,)),
    )


def grad_shapes(width, hidden_width, shards):
    split = SPLIT
    part, hidden_part = width // shards, hidden_width // shards
    return dict(
        g_qkv=(split + (part, 3 * width), BF16),
        g_out=(split + (part, width), F32),
        g_up=(split + (part, hidden_width), F32),
        g_down=(split + (width, hidden_part), F32),
        g_actor=((SLOTS, width), F32),
        g_small=((7, 8, width), F32),
        g_up_bias=((8, hidden_width), F32),
        g_positions=((LENGTH, width), F32),
        head_sums=((SLOTS + 8, 128), F32),
    )


def at_step(i, table):
    for step, actions in table.items():

        @pl.when(i == step)
        def _(actions=actions):
            for action in actions:
                action()


def spread_kernel(names, scale, *refs):
    r = Names(names, refs)
    place = Place()
    load = pltpu.make_async_copy(r.tokens_in, r.tokens, r.local_sem.at[0])
    load.start()
    partners = place.partners()
    barrier = pltpu.get_barrier_semaphore()
    for device in partners:
        pl.semaphore_signal(barrier, inc=1, device_id=device, device_id_type=MESH)
    pack_shards(r)
    pl.semaphore_wait(barrier, len(partners))
    width, hidden_width = r.w_out.shape[-1], r.w_up.shape[-1]
    plan = [(r.pack, r.pack_own, 0, 128)]
    plan += [(r.w_qkv, r.qkv_in, k * width, width) for k in range(3)]
    plan += [(r.w_out, r.out_in, 0, width)]
    half = hidden_width // 2
    plan += [(r.w_up, r.up_in, k * half, half, True) for k in range(2)]
    plan += [(r.w_down, r.down_in, k * width // 2, width // 2, True) for k in range(2)]
    gathers = [Gather(r, place, k, *item) for k, item in enumerate(plan)]
    pack, q, k, v, out, up0, up1, down0, down1 = gathers
    pack.start_z()
    q.start_z()
    k.start_z()
    v.start_z()
    pack.start_y()
    q.start_y()
    pack.start_c()
    frame_values(r)
    k.start_y()
    pack.ready()
    unpack_shards(r)
    v.start_y()
    q.start_c()
    load.wait()
    norm_pass(r)
    k.start_c()
    v.start_c()
    for group in (out, up0, up1, down0, down1):
        group.start_z()
    q.ready()
    project_third(r, 0)
    clear(r)
    k.ready()
    project_third(r, 1)
    v.ready()
    project_third(r, 2)

    front(
        r,
        lambda i: at_step(
            i,
            {
                1: [out.start_y],
                3: [up0.start_y, out.start_c],
                5: [up1.start_y, up0.start_x],
                7: [down0.start_y, up1.start_x, up0.start_c],
                9: [down1.start_y, down0.start_x, up1.start_c],
            },
        ),
    )
    out.ready()

    def arrive():
        down1.start_x()
        down0.start_c()
        down1.start_c()
        for group in (up0, up1, down0, down1):
            group.ready()

    middle_part(r, scale, arrive)

    plan = [(r.g_down,), (r.g_up,), (r.g_out,)]
    plan += [(r.g_qkv, k * width) for k in range(3)] + [(r.g_pack,)]
    reduces = [Reduce(r, place, k, *item) for k, item in enumerate(plan)]
    down, up, out, q, k, v, pack = reduces
    down.start_c()
    up.start_c()
    out.start_c()
    attend_back(
        r,
        lambda i: at_step(
            i,
            {
                1: [down.start_y, up.start_x1],
                2: [out.start_x1],
                6: [down.start_z, up.start_y],
                7: [out.start_y],
                9: [up.start_z],
            },
        ),
    )
    qkv_weight_grad(r, 0)
    q.start_c()
    qkv_weight_grad(r, 2)
    v.start_c()
    q.start_y()
    qkv_weight_grad(r, 1)
    k.start_c()
    v.start_x1()
    out.start_z()
    k.start_y()

    def stored(i):
        rows = pl.ds(pl.multiple_of(i * 4 * LENGTH, 4 * LENGTH), 4 * LENGTH)
        return pltpu.make_async_copy(
            r.middle_grad.at[rows, :], r.tokens_grad.at[rows, :], r.store_sem.at[i]
        )

    start_back(
        r,
        lambda i: at_step(
            i,
            {
                2: [down.start_x],
                3: [up.start_x, q.start_z],
                5: [v.start_y, out.start_x],
                6: [k.start_z],
                8: [v.start_z, q.start_x],
            },
        ),
        lambda i: stored(i).start(),
    )
    pack_grads(r)
    pack.start_c()
    k.start_x()
    v.start_x()
    pack.start_y()
    down.finish(r.down_out)
    up.finish(r.up_out)
    pack.start_z()
    out.finish(r.out_out)
    for group in (q, k, v):
        group.finish(r.qkv_out)
    pack.start_x()
    for i in range(r.middle_grad.shape[0] // (4 * LENGTH)):
        stored(i).wait()
    for group in gathers + reduces:
        group.close()
    pack.finish(r.pack_out)


def finish_kernel(names, count, *refs):
    r = Names(names, refs)
    step = 4 * LENGTH
    parts = [pl.ds(at, step) for at in range(0, r.tokens.shape[0], step)]
    loads = [
        pltpu.make_async_copy(r.tokens.at[part, :], r.held.at[part, :], r.load_sem.at[k])
        for k, part in enumerate(parts)
    ]
    stores = [
        pltpu.make_async_copy(r.held.at[part, :], r.o_tokens.at[part, :], r.store_sem.at[k])
        for k, part in enumerate(parts)
    ]
    for load in loads:
        load.start()
    r.o_qkv[...] = r.qkv[...]
    r.o_out[...] = r.out[...]
    r.o_up[...] = r.up[...]
    r.o_down[...] = r.down[...].T
    r.o_stats[...] = DECAY_RATE * r.running[...] + (1.0 - DECAY_RATE) * r.percentiles[...]
    part, positions = r.o_positions.shape
    slots = r.o_actor.shape[0]
    features = r.pack[0:part, :]
    r.o_positions[...] = features[:, POSITION_AT : POSITION_AT + positions]
    turned = features.T
    vectors = (r.gain1, r.bias1, r.gain2, r.bias2, r.bias_down, r.gain3, r.bias3)
    for k, ref in enumerate(vectors):
        ref[...] = turned[SMALL_AT + k : SMALL_AT + k + 1, :].reshape(part)
    r.o_actor[...] = turned[SMALL_AT + 7 : SMALL_AT + 7 + slots, :]
    r.o_actor_bias[...] = turned[BIAS_AT : BIAS_AT + 1, :].reshape(part)[0:slots]
    r.o_loss[...] = features[0:1, LOSS_AT : LOSS_AT + 1] * (1.0 / count)
    r.o_up_bias[...] = r.pack[part : part + 1, :].reshape(128)
    for load, store in zip(loads, stores, strict=True):
        load.wait()
        store.start()
    for store in stores:
        store.wait()


def local_kernel(names, scale, *refs):
    r = Names(names, refs)
    load = pltpu.make_async_copy(r.tokens_in, r.tokens, r.local_sem.at[0])
    load.start()
    clear(r)
    frame_values(r)
    load.wait()
    norm_pass(r)
    for third in range(3):
        project_third(r, third)
    front(r, lambda i: None)
    middle_part(r, scale, lambda: None)
    attend_back(r, lambda i: None)
    for third in range(3):
        qkv_weight_grad(r, third)
    start_back(r, lambda i: None, lambda i: None)
    store = pltpu.make_async_copy(r.middle_grad, r.tokens_grad, r.local_sem.at[1])
    store.start()
    store.wait()


def run(kernel, constant, ins, outs, scratch, flops=0, side_effects=False, collective=None):
    vmem = pl.BlockSpec(memory_space=pltpu.VMEM)
    anywhere = pl.BlockSpec(memory_space=pl.ANY)
    in_specs = [anywhere if array.size > LARGE else vmem for array in ins.values()]
    out_specs = [anywhere if math.prod(shape) > LARGE else vmem for shape, _ in outs.values()]
    return pl.pallas_call(
        functools.partial(kernel, (*ins, *outs, *scratch), constant),
        out_shape=[jax.ShapeDtypeStruct(shape, kind) for shape, kind in outs.values()],
        in_specs=in_specs,
        out_specs=out_specs,
        scratch_shapes=[
            item if not isinstance(item, tuple) else pltpu.VMEM(item[0], item[1])
            for item in scratch.values()
        ],
        compiler_params=pltpu.CompilerParams(
            vmem_limit_bytes=VMEM_BYTES, has_side_effects=side_effects, collective_id=collective
        ),
        cost_estimate=pl.CostEstimate(flops=flops, bytes_accessed=1 << 24, transcendentals=0),
    )(*ins.values())


def on_device(
    tokens,
    positions,
    norm_one_gain,
    norm_one_bias,
    qkv_weight,
    out_weight,
    norm_two_gain,
    norm_two_bias,
    up_weight,
    up_bias,
    down_weight,
    down_bias,
    final_gain,
    final_bias,
    actor_weight,
    actor_bias,
    actions,
    action_masks,
    game_ids,
    returns,
    values,
    running,
    percentiles,
):
    row_count, width = tokens.shape
    seq_count = row_count // LENGTH
    hidden_width = up_weight.shape[1]
    slots = actor_weight.shape[1]
    fsdp = lax.axis_size("fsdp")
    device_count = lax.axis_size("dp") * fsdp
    token_total = row_count * device_count
    scale = float(seq_count * device_count) / token_total
    flops = 6 * row_count * width * (4 * width + 2 * hidden_width)
    part, hidden_part = width // fsdp, hidden_width // fsdp

    vectors = dict(
        gain1=norm_one_gain,
        bias1=norm_one_bias,
        gain2=norm_two_gain,
        bias2=norm_two_bias,
        bias_down=down_bias,
        gain3=final_gain,
        bias3=final_bias,
    )
    stats = dict(running=running, percentiles=percentiles)
    frames = stats | dict(
        tokens_in=tokens,
        actor_bias=actor_bias,
        actions=actions,
        masks=action_masks.T,
        game_ids=game_ids,
        returns=returns,
        values=values,
    )
    scratch = layer_scratch(row_count, width, hidden_width, 16)
    grads = grad_shapes(width, hidden_width, 16)
    weight_shapes = dict(
        w_qkv=(SPLIT + (width // 16, 3 * width), BF16),
        w_out=(SPLIT + (width // 16, width), BF16),
        w_up=(SPLIT + (width // 16, hidden_width), BF16),
        w_down=(SPLIT + (hidden_width // 16, width), BF16),
    )

    if fsdp == 16 and lax.axis_size("dp") == 2:
        ins = frames | vectors
        ins |= dict(qkv_in=qkv_weight, out_in=out_weight, up_in=up_weight, down_in=down_weight)
        ins |= dict(up_bias_in=up_bias, positions_in=positions.T, actor_in=actor_weight.T)
        shard_grads = dict(
            qkv_out=((part, 3 * width), F32),
            out_out=((part, width), F32),
            up_out=((part, hidden_width), F32),
            down_out=((width, hidden_part), F32),
        )
        outs = dict(
            tokens_grad=((row_count, width), F32), pack_out=((PACK_GRAD_ROWS, 128), F32)
        )
        scratch |= grads | weight_shapes
        scratch |= dict(
            pack=(SPLIT + (PACK_ROWS, 128), BF16),
            pack_own=((PACK_ROWS, 128), BF16),
            g_pack=(SPLIT + (PACK_GRAD_ROWS, 128), F32),
            positions=((LENGTH, width), F32),
            small=((8, width), F32),
            actor=((SLOTS, width), BF16),
            up_bias=((1, hidden_width), F32),
            gather_send=pltpu.SemaphoreType.DMA((GATHERS, 15)),
            gather_recv=pltpu.SemaphoreType.DMA((GATHERS, 15)),
            reduce_send=pltpu.SemaphoreType.DMA((len(REDUCES), 16)),
            reduce_recv=pltpu.SemaphoreType.DMA((len(REDUCES), 16)),
            store_sem=pltpu.SemaphoreType.DMA((row_count // (4 * LENGTH),)),
        )
        for index, (count, rows, kind, halved) in enumerate(REDUCES):
            for item, (lead, half) in enumerate(reduce_leads(halved)):
                scratch[index, item] = (lead + (rows, count // 2 if half else count), kind)
        tokens_grad, pack, qkv_g, out_g, up_g, down_g = run(
            spread_kernel, scale, ins, outs | shard_grads, scratch, flops, True, 0
        )
        vector = ((part,), F32)
        final = dict(
            o_loss=((1, 1), F32),
            o_stats=(running.shape, F32),
            o_positions=((part, LENGTH), F32),
            o_qkv=shard_grads["qkv_out"],
            o_out=shard_grads["out_out"],
            o_up=shard_grads["up_out"],
            o_down=((hidden_part, width), F32),
            o_up_bias=((hidden_part,), F32),
            o_actor=((slots, part), F32),
            o_actor_bias=((slots,), F32),
            o_tokens=((row_count, width), F32),
        )
        copies = pltpu.SemaphoreType.DMA((row_count // (4 * LENGTH),))
        done = run(
            finish_kernel,
            token_total,
            stats
            | dict(pack=pack, qkv=qkv_g, out=out_g, up=up_g, down=down_g, tokens=tokens_grad),
            final | dict.fromkeys(vectors, vector),
            dict(held=((row_count, width), F32), load_sem=copies, store_sem=copies),
        )
        loss, new_stats, pos_g, qkv_g, out_g, up_g, down_g = done[:7]
        up_bias_g, actor_g, actor_bias_g, tokens_grad = done[7:11]
        gain1, bias1, gain2, bias2, bias_down, gain3, bias3 = done[11:]
        return (
            loss.reshape(()),
            new_stats,
            tokens_grad,
            pos_g.T,
            gain1,
            bias1,
            qkv_g,
            out_g,
            gain2,
            bias2,
            up_g,
            up_bias_g,
            down_g,
            bias_down,
            gain3,
            bias3,
            actor_g.T,
            actor_bias_g,
        )

    def gather(array, axis):
        return lax.all_gather(array, "fsdp", axis=axis, tiled=True)

    packed = gather(
        jnp.concatenate([jnp.stack(list(vectors.values())), actor_weight.T, positions], 0), 1
    )
    fulls = [gather(weight, 0) for weight in (qkv_weight, out_weight, up_weight, down_weight)]
    ins = frames | {
        name: full.reshape(weight_shapes[name][0])
        for name, full in zip(weight_shapes, fulls, strict=True)
    }
    ins |= dict(
        positions=packed[7 + slots :].astype(F32),
        small=jnp.pad(packed[0:7].astype(F32), ((0, 1), (0, 0))),
        actor=jnp.pad(packed[7 : 7 + slots], ((0, SLOTS - slots), (0, 0))),
        up_bias=gather(up_bias, 0).astype(F32).reshape(1, hidden_width),
    )
    outs = dict(tokens_grad=((row_count, width), F32)) | grads
    tokens_grad, *sums = run(local_kernel, scale, ins, outs, scratch, flops)
    sums = Names(grads, sums)

    def scatter(array, axis):
        piece = lax.psum_scatter(array, "fsdp", scatter_dimension=axis, tiled=True)
        return lax.psum(piece.astype(BF16), "dp").astype(F32)

    down_sum = jnp.swapaxes(sums.g_down, 3, 4)
    qkv_part, out_part, up_part, down_part = (
        scatter(merged(grad).astype(F32), 0)
        for grad in (sums.g_qkv, sums.g_out, sums.g_up, down_sum)
    )
    rows = [jnp.sum(sums.g_small, 1), sums.g_actor[:slots], sums.g_positions]
    side = scatter(jnp.concatenate(rows, 0), 1)
    up_bias_part = scatter(jnp.sum(sums.g_up_bias, 0), 0)
    head_total = lax.psum(jnp.sum(sums.head_sums[: SLOTS + 1], 1), ("dp", "fsdp"))
    return (
        head_total[SLOTS] / token_total,
        DECAY_RATE * running + (1.0 - DECAY_RATE) * percentiles,
        tokens_grad,
        side[7 + slots :],
        side[G1],
        side[B1],
        qkv_part,
        out_part,
        side[G2],
        side[B2],
        up_part,
        up_bias_part,
        down_part,
        side[DB],
        side[GL],
        side[BL],
        side[7 : 7 + slots].T,
        head_total[:slots],
    )


def solution(mesh):
    rows, cols, both = P(("dp", "fsdp"), None), P(None, "fsdp"), P(("dp", "fsdp"))
    weight, vector, whole = P("fsdp", None), P("fsdp"), P()
    in_specs = (rows, cols, vector, vector, weight, weight, vector, vector, weight, vector)
    in_specs += (weight, vector, vector, vector, weight, whole, both, rows, both, both, both)
    in_specs += (whole, whole)
    out_specs = (whole, whole, rows, cols, vector, vector, weight, weight, vector, vector)
    out_specs += (weight, vector, weight, vector, vector, vector, weight, whole)
    return jax.shard_map(
        on_device, mesh=mesh, in_specs=in_specs, out_specs=out_specs, check_vma=False
    )
```

```python
import functools
import math
import math

import jax
import jax.numpy as jnp
from jax import lax
from jax.experimental import pallas as pl
from jax.experimental.pallas import tpu as pltpu
from jax.sharding import PartitionSpec as P

HEADS = 8
HEAD = 64
LENGTH = 64
QUAD = 4
WIDE = QUAD * HEAD
MASKED = -1e30
EPSILON = 1e-05
DECAY_RATE = 0.9
ENTROPY_WEIGHT = 0.1
SLOTS = 32
VMEM_BYTES = 63 * 1024 * 1024
BF16 = jnp.bfloat16
F32 = jnp.float32

G1, B1, G2, B2, DB, GL, BL = range(7)
MESH = pl.DeviceIdType.MESH


def dot(left, right, left_dim, right_dim):
    return lax.dot_general(
        left, right, (((left_dim,), (right_dim,)), ((), ())), preferred_element_type=F32
    )


def mean_last(values):
    return jnp.sum(values, -1, keepdims=True) * (1.0 / values.shape[-1])


def normalise(values):
    centred = values - mean_last(values)
    scale = lax.rsqrt(mean_last(centred * centred) + EPSILON)
    return centred * scale, scale


def norm_back(unit, scale, gain, upstream):
    inner = upstream * gain
    return scale * (inner - mean_last(inner) - unit * mean_last(inner * unit))


def fold_rows(values):
    rows, width = values.shape
    return jnp.sum(values.reshape(rows // 8, 8, width), 0)


def gelu_pair(values):
    half = jnp.exp2(values * values * (-0.5 * 1.4426950408889634))
    span = 1.0 + jnp.abs(values) * (0.3275911 * 0.7071067811865476)
    t = 1.0 / span
    poly = t * (
        0.5 * 0.254829592
        + t
        * (
            0.5 * -0.284496736
            + t * (0.5 * 1.421413741 + t * (0.5 * -1.453152027 + t * (0.5 * 1.061405429)))
        )
    )
    tail = poly * half
    cdf = jnp.where(values < 0.0, tail, 1.0 - tail)
    density = half * 0.3989422804014327
    return values * cdf, cdf + values * density


def pair_masks():
    lane = lax.broadcasted_iota(jnp.int32, (LENGTH, 2 * HEAD), 1)
    first = jnp.where(lane < HEAD, 1.0, 0.0)
    return first.astype(BF16), (1.0 - first).astype(BF16)


def spread_heads(rows, masks):
    zero = jnp.zeros((LENGTH, 2 * HEAD), BF16)
    left, right = rows[:, : 2 * HEAD], rows[:, 2 * HEAD :]
    blocks = [jnp.concatenate([left * mask, zero], 1) for mask in masks]
    blocks += [jnp.concatenate([zero, right * mask], 1) for mask in masks]
    return jnp.concatenate(blocks, 0)


def pair_products(left, right):
    lane = lax.broadcasted_iota(jnp.int32, (LENGTH, 2 * HEAD), 1)
    pairs = []
    for at in range(0, WIDE, 2 * HEAD):
        block = dot(left[:, at : at + 2 * HEAD], right[:, at : at + 2 * HEAD], 0, 0)
        pairs.append(jnp.where(lane < HEAD, block[0:HEAD], block[HEAD : 2 * HEAD]))
    return jnp.concatenate(pairs, 1)


def causal_bias():
    key = lax.broadcasted_iota(jnp.int32, (LENGTH, WIDE), 0)
    query = lax.rem(lax.broadcasted_iota(jnp.int32, (LENGTH, WIDE), 1), HEAD)
    return jnp.where(key <= query, 0.0, MASKED)


LOG2E = 1.4426950408889634
SCORE_SCALE = HEAD ** (-0.5) * LOG2E


def chains(r, i):
    width = r.tokens.shape[1]
    found = []
    for s in range(4):
        row = pl.multiple_of((4 * i + s) * LENGTH, LENGTH)
        for half in range(width // WIDE):
            at = half * WIDE
            columns = [slice(k * width + at, k * width + at + WIDE) for k in range(3)]
            found.append((4 * i + s, pl.ds(row, LENGTH), columns))
    return found


def attend_group(r, i):
    masks, bias = pair_masks(), r.causal[...]
    group = chains(r, i)
    loaded = [[r.qkv[rows, part] for part in parts] for _, rows, parts in group]
    scores = [dot(key, spread_heads(query, masks), 1, 1) for query, key, _ in loaded]
    probs, totals = [], []
    for score in scores:
        score = score * SCORE_SCALE + bias
        highest = jnp.max(score, 0, keepdims=True)
        weights = jnp.exp2(score - highest)
        summed = jnp.sum(weights, 0, keepdims=True)
        probs.append((weights * (1.0 / summed)).astype(BF16))
        totals.append(highest + jnp.log(summed) * LOG2E)
    done = [
        pair_products(prob, value).astype(BF16)
        for prob, (_, _, value) in zip(probs, loaded, strict=True)
    ]
    for (seq, rows, (q, _, _)), result, total in zip(group, done, totals, strict=True):
        r.attended[rows, q] = result
        r.totals[pl.ds(seq, 1), q] = total


def attend_back_group(r, i):
    masks, bias = pair_masks(), r.causal[...]
    done = []
    for half in range(2):
        group = chains(r, i)[half::2]
        queries = [spread_heads(r.qkv[rows, q], masks) for _, rows, (q, _, _) in group]
        aboves = [spread_heads(r.attended[rows, q], masks) for _, rows, (q, _, _) in group]
        scores = [
            dot(r.qkv[rows, k], query, 1, 1)
            for (_, rows, (_, k, _)), query in zip(group, queries, strict=True)
        ]
        prob_grads = [
            dot(r.qkv[rows, v], above, 1, 1)
            for (_, rows, (_, _, v)), above in zip(group, aboves, strict=True)
        ]
        probs, score_grads = [], []
        for (seq, _, (q, _, _)), score, pull in zip(group, scores, prob_grads, strict=True):
            prob = jnp.exp2(score * SCORE_SCALE + bias - r.totals[pl.ds(seq, 1), q])
            row_terms = jnp.sum(pull * prob, 0, keepdims=True)
            score_grads.append((prob * (pull - row_terms)).astype(BF16))
            probs.append(prob.astype(BF16))
        value_grads = [dot(prob, above, 1, 0) for prob, above in zip(probs, aboves, strict=True)]
        key_grads = [dot(grad, query, 1, 0) for grad, query in zip(score_grads, queries, strict=True)]
        query_grads = [
            pair_products(grad, r.qkv[rows, k])
            for (_, rows, (_, k, _)), grad in zip(group, score_grads, strict=True)
        ]
        for (_, rows, (q, k, v)), dq, dk, dv in zip(
            group, query_grads, key_grads, value_grads, strict=True
        ):
            done.append((rows, q, (dq * HEAD ** (-0.5)).astype(BF16)))
            done.append((rows, k, (dk * HEAD ** (-0.5)).astype(BF16)))
            done.append((rows, v, dv.astype(BF16)))
    for rows, columns, grad in done:
        r.qkv[rows, columns] = grad


def policy(logits, masks, actions, advantage, scale):
    allowed = masks > 0
    held = jnp.where(allowed, logits, MASKED)
    shifted = held - jnp.max(held, 0, keepdims=True)
    weights = jnp.exp(shifted)
    summed = jnp.sum(weights, 0, keepdims=True)
    log_probs = shifted - jnp.log(summed)
    probs = weights * (1.0 / summed)
    plogp = jnp.where(allowed, probs * log_probs, 0.0)
    entropy = -jnp.sum(plogp, 0, keepdims=True)
    slot = lax.broadcasted_iota(jnp.int32, logits.shape, 0)
    taken = slot == actions
    chosen = jnp.sum(jnp.where(taken, log_probs, 0.0), 0, keepdims=True)
    loss = -advantage * chosen - ENTROPY_WEIGHT * entropy
    pull = advantage * (probs - jnp.where(taken, 1.0, 0.0)) + ENTROPY_WEIGHT * (
        plogp + probs * entropy
    )
    return loss, jnp.where(allowed, pull * scale, 0.0)


STRIP = 32
THIN = 16
LARGE = 1 << 20


class Names:
    def __init__(self, names, refs):
        self.table = dict(zip(names, refs, strict=True))

    def __getattr__(self, name):
        return self.table[name]


SPLIT = (4, 2, 2)
PACK_ROWS = 48
PACK_GRAD_ROWS = 40
POSITION_AT, SMALL_AT, BIAS_AT, LOSS_AT = 0, 64, 96, 97


def merged(block):
    return block.reshape(-1, block.shape[-1])


def strip_rows(row, count):
    return [pl.ds(pl.multiple_of(row + at, STRIP), STRIP) for at in range(0, count, STRIP)]


def load_starts(r, row, count):
    starts = [r.tokens[rows, :].astype(F32) for rows in strip_rows(row, count)]
    frames = [r.positions[at : at + STRIP, :] for at in range(0, LENGTH, STRIP)]
    return [start + frames[k % len(frames)] for k, start in enumerate(starts)]


def norm_pass(r):
    count = r.tokens.shape[0]
    rows = 4 * LENGTH

    def body(i, carry):
        row = pl.multiple_of(i * rows, rows)
        normed = [
            (normalise(start)[0] * r.small[G1 : G1 + 1, :] + r.small[B1 : B1 + 1, :]).astype(BF16)
            for start in load_starts(r, row, rows)
        ]
        normed = jnp.concatenate(normed, 0)
        turned = normed.T
        r.attended[pl.ds(row, rows), :] = normed
        r.normed_t[:, pl.ds(row, rows)] = turned
        return carry

    lax.fori_loop(0, count // rows, body, 0)


def project_third(r, third):
    count, width = r.tokens.shape
    rows = 8 * LENGTH
    columns = slice(third * width, (third + 1) * width)

    def body(i, carry):
        here = pl.ds(pl.multiple_of(i * rows, rows), rows)
        weight = merged(r.w_qkv[:, :, :, :, columns])
        r.qkv[here, columns] = dot(r.attended[here, :], weight, 1, 0).astype(BF16)
        return carry

    lax.fori_loop(0, count // rows, body, 0)


def front(r, pump):
    count = r.tokens.shape[0]

    def body(i, carry):
        pump(i)
        attend_group(r, i)
        return carry

    lax.fori_loop(0, count // (4 * LENGTH), body, 0)


def add_grad(ref, index, values):
    ref[index] += values.reshape(ref[index].shape)


def add_columns(ref, values):
    count = ref.shape[-1]
    for k in range(values.shape[1] // count):
        ref[k // 2, k % 2] += values[:, k * count : (k + 1) * count]


def clear(r):
    for ref in (r.g_out, r.g_up, r.g_down):

        def body(z, carry, ref=ref):
            ref[z] = jnp.zeros(ref.shape[1:], F32)
            return carry

        lax.fori_loop(0, ref.shape[0], body, 0)
    for ref in (r.g_actor, r.g_small, r.g_up_bias, r.g_positions, r.head_sums):
        ref[...] = jnp.zeros_like(ref)


def frame_values(r):
    r.causal[...] = causal_bias()
    fresh = DECAY_RATE * r.running[...] + (1.0 - DECAY_RATE) * r.percentiles[...]
    spread = jnp.maximum(1.0, fresh[1:2, :] - fresh[0:1, :])
    seqs = r.game_ids.shape[0]
    game = r.game_ids[...].reshape(seqs, 1)
    slot = lax.broadcasted_iota(jnp.int32, (seqs, spread.shape[1]), 1)
    column = jnp.sum(jnp.where(slot == game, spread, 0.0), 1, keepdims=True)
    count = 8 * LENGTH
    owner = lax.broadcasted_iota(jnp.int32, (8, count), 0)
    frame = lax.broadcasted_iota(jnp.int32, (8, count), 1)
    for k in range(seqs // 8):
        here = slice(k * count, (k + 1) * count)
        near = jnp.where(frame // LENGTH == owner, column[8 * k : 8 * k + 8], 0.0)
        wide = jnp.sum(near, 0, keepdims=True)
        r.advantage[:, here] = (r.returns[here] - r.values[here]).reshape(1, count) / wide
        r.action_row[:, here] = r.actions[here].reshape(1, count)


class Tile:
    def __init__(self, r, side):
        def pick(name):
            return r.table[name, side]

        self.active, self.slope = pick("active"), pick("slope")
        self.two_t, self.unit, self.last = pick("two_t"), pick("unit"), pick("last")
        self.scale = pick("scale")


def middle_part(r, scale, arrive):
    count, width = r.tokens.shape
    rows = r.low.shape[0]
    shards = r.w_up.shape[0]
    chunk = r.w_up.shape[-1] // shards
    slots = r.masks.shape[0]
    out_weight = r.w_out
    head_bias = jnp.concatenate(
        [r.actor_bias[...].astype(F32).reshape(slots, 1), jnp.zeros((SLOTS - slots, 1), F32)], 0
    )
    everything = slice(None)
    strips = [slice(at, at + STRIP) for at in range(0, rows, STRIP)]

    def gain(k):
        return r.small[k : k + 1, :]

    def tile_rows(i):
        return pl.ds(pl.multiple_of(i * rows, rows), rows)

    def before(t, tokens, attended):
        projected = dot(attended, merged(out_weight[...]), 1, 0)
        for k, strip in enumerate(strips):
            frame = k * STRIP % LENGTH
            start = tokens[k].astype(F32) + r.positions[frame : frame + STRIP, :]
            mid = start + projected[strip]
            unit, spread = normalise(mid)
            r.two_low[strip, :] = (unit * gain(G2) + gain(B2)).astype(BF16)
            t.unit[strip, :] = unit
            t.scale[strip, :] = spread
            t.last[strip, :] = mid + gain(DB)
        t.two_t[...] = r.two_low[...].T

    def columns(j):
        return slice(j * chunk, (j + 1) * chunk)

    def up_weight(j):
        return merged(r.w_up[:, :, :, :, columns(j)])

    def activate(hidden, bias):
        done = [gelu_pair(hidden[at : at + THIN] + bias) for at in range(0, rows, THIN)]
        values = jnp.concatenate([value.astype(BF16) for value, _ in done], 0)
        return values, jnp.concatenate([slope.astype(BF16) for _, slope in done], 0)

    def forward_only(j, t):
        cols = columns(j)
        weight, bias, down = up_weight(j), r.up_bias[:, cols], merged(r.w_down[j])
        active, slope = activate(dot(r.two_low[...], weight, 1, 0), bias)
        t.last[...] += dot(active, down, 1, 0)
        t.active[:, cols], t.slope[:, cols] = active, slope

    def both_ways(j, here, there):
        cols = columns(j)
        bias, total = r.up_bias[:, cols], r.g_up_bias[:, cols]
        if there is not None:
            hidden = dot(r.two_low[...], up_weight(j), 1, 0)
        above = dot(r.low[...], merged(r.w_down[j]), 1, 1)
        for at in range(0, rows, THIN):
            strip = slice(at, at + THIN)
            part = (above[strip] * here.slope[strip, cols].astype(F32)).astype(BF16)
            r.hidden_grad[strip, :] = part
            total += fold_rows(part.astype(F32))
        add_columns(r.g_down.at[j], dot(r.low_t[...], here.active[:, cols], 1, 0))
        r.two_in[...] += dot(r.hidden_grad[...], up_weight(j), 1, 1)
        add_grad(
            r.g_up,
            (everything, everything, everything, everything, cols),
            dot(here.two_t[...], r.hidden_grad[...], 1, 0),
        )
        r.g_up_bias[:, cols] = total
        if there is not None:
            active, slope = activate(hidden, bias)
            there.last[...] += dot(active, merged(r.w_down[j]), 1, 0)
            there.active[:, cols], there.slope[:, cols] = active, slope

    def chunks(step):
        for j in range(shards):
            step(j)

    def last_norm(t):
        spreads = []
        for strip in strips:
            unit, spread = normalise(t.last[strip, :])
            r.low[strip, :] = (unit * gain(GL) + gain(BL)).astype(BF16)
            t.last[strip, :] = unit
            spreads.append(spread)
        return spreads, dot(r.actor[...], r.low[...], 1, 1) + head_bias

    def head(logits, masks, actions, advantage):
        masks = jnp.concatenate([masks, jnp.zeros((SLOTS - slots, rows), jnp.int32)], 0)
        loss, pull = policy(logits, masks, actions, advantage, scale)
        logit_grad = pull.astype(BF16)
        last_in = dot(logit_grad, r.actor[...], 0, 0)
        r.g_actor[...] += dot(logit_grad, r.low[...], 1, 0)
        wide_grad = logit_grad.astype(F32)
        fold = r.head_sums[0:SLOTS, :]
        for at in range(0, rows, 128):
            fold += wide_grad[:, at : at + 128]
        r.head_sums[0:SLOTS, :] = fold
        fold = r.head_sums[SLOTS : SLOTS + 1, :]
        for at in range(0, rows, 128):
            fold += loss[:, at : at + 128]
        r.head_sums[SLOTS : SLOTS + 1, :] = fold
        return last_in

    def last_norm_back(t, spreads, last_in):
        sums = [r.g_small[k] for k in (GL, BL, DB)]
        for strip, spread in zip(strips, spreads, strict=True):
            above, unit = last_in[strip], t.last[strip, :]
            grad = norm_back(unit, spread, gain(GL), above)
            sums[0] += fold_rows(above * unit)
            sums[1] += fold_rows(above)
            sums[2] += fold_rows(grad)
            t.last[strip, :] = grad
            r.low[strip, :] = grad.astype(BF16)
        for k, total in zip((GL, BL, DB), sums, strict=True):
            r.g_small[k] = total
        r.low_t[...] = r.low[...].T
        r.two_in[...] = jnp.zeros((rows, width), F32)

    def two_norm_back(t):
        sums = [r.g_small[k] for k in (G2, B2)]
        for strip in strips:
            above, unit = r.two_in[strip, :], t.unit[strip, :]
            sums[0] += fold_rows(above * unit)
            sums[1] += fold_rows(above)
            grad = t.last[strip, :] + norm_back(unit, t.scale[strip, :], gain(G2), above)
            t.last[strip, :] = grad
            r.hidden_grad[strip, :] = grad.astype(BF16)
        for k, total in zip((G2, B2), sums, strict=True):
            r.g_small[k] = total

    def out_back(i, t, attended):
        low = r.hidden_grad[...]
        add_grad(r.g_out, ..., dot(attended, low, 0, 0))
        r.attended[tile_rows(i), :] = dot(low, merged(out_weight[...]), 1, 1).astype(BF16)
        r.middle_grad[tile_rows(i), :] = t.last[...]

    sides = [Tile(r, 0), Tile(r, 1)]
    tiles = count // rows

    def begin(i):
        row = pl.multiple_of(i * rows, rows)
        return [r.tokens[part, :] for part in strip_rows(row, rows)], r.attended[tile_rows(i), :]

    def step(i, side, first=False, last=False):
        here, there = sides[side], sides[1 - side]
        at = tile_rows(i)
        side_data = r.masks[:, at], r.action_row[:, at], r.advantage[:, at]
        if not first:
            attended = r.attended[tile_rows(i - 1), :]
        if not last:
            ahead = begin(i + 1)
        spreads, logits = last_norm(here)
        if not first:
            two_norm_back(there)
        last_in = head(logits, *side_data)
        if not first:
            out_back(i - 1, there, attended)
        last_norm_back(here, spreads, last_in)
        if not last:
            before(there, *ahead)
        chunks(lambda j: both_ways(j, here, None if last else there))

    before(sides[0], *begin(0))
    arrive()
    chunks(lambda j: forward_only(j, sides[0]))
    step(0, 0, first=True)

    def pair(p, carry):
        step(2 * p + 1, 1)
        step(2 * p + 2, 0)
        return carry

    lax.fori_loop(0, (tiles - 2) // 2, pair, 0)
    step(tiles - 1, 1, last=True)
    two_norm_back(sides[1])
    out_back(tiles - 1, sides[1], r.attended[tile_rows(tiles - 1), :])


def attend_back(r, pump):
    count = r.tokens.shape[0]
    rows = 4 * LENGTH

    def body(i, carry):
        pump(i)
        attend_back_group(r, i)
        return carry

    lax.fori_loop(0, count // rows, body, 0)


def qkv_weight_grad(r, third):
    width = r.tokens.shape[1]
    step = width // 2
    for at in range(third * width, (third + 1) * width, step):
        values = dot(r.normed_t[...], r.qkv[:, at : at + step], 1, 0)
        values = values.astype(BF16).reshape(r.g_qkv.shape[:4] + (step,))
        r.g_qkv[:, :, :, :, at : at + step] = values


def start_back(r, pump, tile_done):
    count = r.tokens.shape[0]
    rows = 4 * LENGTH
    gain = r.small[G1 : G1 + 1, :]

    def body(i, carry):
        pump(i)
        row = pl.multiple_of(i * rows, rows)
        starts = load_starts(r, row, rows)
        one_in = dot(r.qkv[pl.ds(row, rows), :], merged(r.w_qkv[...]), 1, 1)
        sums = [r.g_small[k] for k in (G1, B1)]
        frames = [r.g_positions[at : at + STRIP, :] for at in range(0, LENGTH, STRIP)]
        grads = []
        for k, (start, there) in enumerate(zip(starts, strip_rows(row, rows), strict=True)):
            unit, scale = normalise(start)
            above = one_in[k * STRIP : (k + 1) * STRIP]
            sums[0] += fold_rows(above * unit)
            sums[1] += fold_rows(above)
            grads.append(r.middle_grad[there, :] + norm_back(unit, scale, gain, above))
            frames[k % len(frames)] += grads[k]
        r.g_positions[...] = jnp.concatenate(frames, 0)
        for k, total in zip((G1, B1), sums, strict=True):
            r.g_small[k] = total
        r.middle_grad[pl.ds(row, rows), :] = jnp.concatenate(grads, 0)
        tile_done(i)
        return carry

    lax.fori_loop(0, count // rows, body, 0)


def pack_shards(r):
    part = r.positions_in.shape[0]
    slots = r.masks.shape[0]
    rows = [
        ref[...].astype(F32).reshape(1, part)
        for ref in (r.gain1, r.bias1, r.gain2, r.bias2, r.bias_down, r.gain3, r.bias3)
    ]
    rows += [r.actor_in[...].astype(F32), jnp.zeros((32 - 7 - slots, part), F32)]
    features = jnp.concatenate(
        [r.positions_in[...].astype(F32), jnp.concatenate(rows, 0).T, jnp.zeros((part, 32), F32)], 1
    )
    bias = r.up_bias_in[...].astype(F32).reshape(1, 128)
    packed = jnp.concatenate([features, bias, jnp.zeros((PACK_ROWS - part - 1, 128), F32)], 0)
    r.pack_own[...] = packed.astype(BF16)


def unpack_shards(r):
    slots = r.masks.shape[0]
    blocks = r.pack[...].astype(F32).reshape(-1, PACK_ROWS, 128)
    part = r.positions_in.shape[0]
    features = merged(blocks[:, :part, :]).T
    r.positions[...] = features[POSITION_AT : POSITION_AT + LENGTH]
    small = features[SMALL_AT : SMALL_AT + 32]
    r.small[...] = small[0:8]
    width = small.shape[1]
    r.actor[...] = jnp.concatenate(
        [small[7 : 7 + slots], jnp.zeros((SLOTS - slots, width), F32)], 0
    ).astype(BF16)
    r.up_bias[...] = jnp.concatenate(
        [blocks[f, part : part + 1, :] for f in range(blocks.shape[0])], 1
    )


def small_rows(r):
    slots = r.masks.shape[0]
    rows = [jnp.sum(r.g_small[k], 0, keepdims=True) for k in range(7)]
    return jnp.concatenate(
        rows + [r.g_actor[0:slots, :], jnp.zeros((32 - 7 - slots, rows[0].shape[1]), F32)], 0
    )


def pack_grads(r):
    width = r.tokens.shape[1]
    part = r.positions_in.shape[0]
    features = jnp.concatenate(
        [r.g_positions[...], small_rows(r), jnp.zeros((128 - SMALL_AT - 32, width), F32)], 0
    ).T
    sums = jnp.sum(r.head_sums[0 : SLOTS + 8, :], 1, keepdims=True)
    lane = lax.broadcasted_iota(jnp.int32, (part, 128), 1)
    bias = jnp.sum(r.g_up_bias[...], 0, keepdims=True)
    shape = r.g_pack.shape
    for f in range(width // part):
        block = features[f * part : (f + 1) * part]
        block = jnp.where(lane == BIAS_AT, sums[0:SLOTS], block)
        block = jnp.where(lane == LOSS_AT, sums[SLOTS : SLOTS + 1], block)
        owner = (f // 4, f // 2 % 2, f % 2)
        rows = [block, bias[:, f * 128 : (f + 1) * 128], jnp.zeros((shape[3] - part - 1, 128), F32)]
        r.g_pack[owner] = jnp.concatenate(rows, 0)


GATHERS = 9
REDUCES = (
    (128, 512, BF16, False),
    (2048, 32, BF16, True),
    (512, 32, BF16, True),
    (512, 32, BF16, False),
    (512, 32, BF16, False),
    (512, 32, BF16, True),
    (128, PACK_GRAD_ROWS, F32, False),
)


class Place:
    def __init__(self):
        self.x = lax.axis_index("dp")
        f = lax.axis_index("fsdp")
        self.z, self.y, self.c = f // 4, f // 2 % 2, f % 2

    def at(self, x=None, z=None, y=None, c=None):
        pick = lambda new, old: old if new is None else new
        f = pick(z, self.z) * 4 + pick(y, self.y) * 2 + pick(c, self.c)
        return (pick(x, self.x), f)

    def z_partner(self, k):
        return (self.z + 1 - 2 * (self.z % 2), (self.z + 2) % 4, 3 - self.z)[k]

    def lines(self):
        return [self.z] + [self.z_partner(k) for k in range(3)]

    def partners(self):
        return [self.at(z=self.z_partner(k)) for k in range(3)] + [
            self.at(y=1 - self.y),
            self.at(c=1 - self.c),
            self.at(x=1 - self.x),
        ]


def remote(r_send, r_recv, index):
    def copy(src, dst, k, device):
        return pltpu.make_async_remote_copy(
            src_ref=src,
            dst_ref=dst,
            send_sem=r_send.at[index, k],
            recv_sem=r_recv.at[index, k],
            device_id=device,
            device_id_type=MESH,
        )

    return copy


class Gather:
    def __init__(self, r, place, index, full, own, at, count, halved=False):
        p = place
        copy = remote(r.gather_send, r.gather_recv, index)
        cols = part = slice(at, at + count)
        if halved:
            part = pl.ds(pl.multiple_of(at + p.x * (count // 2), 128), count // 2)
        self.full, self.own, self.part, self.place, self.halved = full, own, part, place, halved
        mine = full.at[p.z, p.y, p.c, :, part]
        self.z = [copy(own.at[:, part], mine, k, p.at(z=p.z_partner(k))) for k in range(3)]
        self.y, self.x, self.near, self.far = [], [], [], []
        for k, z in enumerate(p.lines()):
            shard = full.at[z, p.y, p.c, :, part]
            self.y.append(copy(shard, shard, 3 + k, p.at(y=1 - p.y)))
            if halved:
                pair = full.at[z, :, p.c, :, part]
                self.x.append(copy(pair, pair, 7 + k, p.at(x=1 - p.x)))
                pair = full.at[z, :, p.c, :, cols]
                self.far.append(copy(pair, pair, 11 + k, p.at(c=1 - p.c)))
            else:
                self.near.append(copy(shard, shard, 7 + k, p.at(c=1 - p.c)))
                shard = full.at[z, 1 - p.y, p.c, :, part]
                self.far.append(copy(shard, shard, 11 + k, p.at(c=1 - p.c)))

    def start_z(self):
        for copy in self.z:
            copy.start()
        p = self.place
        self.full[p.z, p.y, p.c, :, self.part] = self.own[:, self.part]
        self.y[0].start()
        if not self.halved:
            self.near[0].start()

    def start_y(self):
        for k, copy in enumerate(self.z):
            copy.wait_recv()
            self.y[k + 1].start()
            if not self.halved:
                self.near[k + 1].start()

    def start_x(self):
        for arrived, copy in zip(self.y, self.x, strict=True):
            arrived.wait_recv()
            copy.start()

    def start_c(self):
        for arrived, copy in zip(self.x if self.halved else self.y, self.far, strict=True):
            arrived.wait_recv()
            copy.start()

    def ready(self):
        for copy in self.near + self.far:
            copy.wait_recv()

    def close(self):
        for copy in self.z + self.y + self.x + self.near + self.far:
            copy.wait_send()


class Reduce:
    def __init__(self, r, place, index, grad, at=0):
        count, _, kind, halved = REDUCES[index]
        self.grad, self.place, self.kind, self.halved = grad, place, kind, halved
        p = place
        copy = remote(r.reduce_send, r.reduce_recv, index)
        self.cols = slice(at, at + count)
        self.buffers = [r.table[index, part] for part in range(len(reduce_leads(halved)))]
        sc, rc, ry, rz, rx = self.buffers[:5]
        keep = count
        self.part = self.cols
        self.lines = p.lines()
        if halved:
            keep = count // 2
            self.part = self.half(at, keep, p.x)
            self.away = self.half(at, keep, 1 - p.x)
            self.local, self.local_away = self.half(0, keep, p.x), self.half(0, keep, 1 - p.x)
            held = self.buffers[5]
            self.sx1 = sc.at[:, :, :, 0:keep]
            self.x1 = [
                copy(self.sx1.at[z], held.at[z], 12 + k, p.at(x=1 - p.x))
                for k, z in enumerate(self.lines)
            ]
        tail = slice(count - keep, count)
        self.sy = sc.at[:, 0, :, tail]
        self.sz = [sc.at[k, 1, :, tail] for k in range(3)]
        self.sx = sc.at[3, 1, :, tail]
        self.c, self.y = [], []
        for k, z in enumerate(self.lines):
            self.c.append(copy(sc.at[z], rc.at[z], k, p.at(c=1 - p.c)))
            self.y.append(copy(self.sy.at[z], ry.at[z], 4 + k, p.at(y=1 - p.y)))
        self.z = [copy(self.sz[k], rz.at[k], 8 + k, p.at(z=p.z_partner(k))) for k in range(3)]
        self.x = copy(self.sx, rx, 11, p.at(x=1 - p.x))

    @staticmethod
    def half(at, keep, x):
        return pl.ds(pl.multiple_of(at + x * keep, 128), keep)

    def add(self, index, values):
        total = self.grad[index].astype(F32) + values.astype(F32)
        self.grad[index] = total.astype(self.grad.dtype)

    def start_c(self):
        sc, p = self.buffers[0], self.place
        for z, copy in zip(self.lines, self.c, strict=True):
            sc[z] = self.grad[z, :, 1 - p.c, :, self.cols].astype(self.kind)
            copy.start()

    def start_x1(self, pieces=range(4)):
        rc, p = self.buffers[1], self.place
        for k in pieces:
            z = self.lines[k]
            self.c[k].wait()
            away = self.grad[z, :, p.c, :, self.away].astype(F32)
            away += rc[z, :, :, self.local_away].astype(F32)
            self.sx1[z] = away.astype(self.kind)
            self.x1[k].start()
            self.add((z, slice(None), p.c, slice(None), self.part), rc[z, :, :, self.local])

    def start_y(self, pieces=range(4)):
        p = self.place
        held = self.buffers[5 if self.halved else 1]
        for k in pieces:
            z = self.lines[k]
            if self.halved:
                self.x1[k].wait_recv()
            else:
                self.c[k].wait()
            away = self.grad[z, 1 - p.y, p.c, :, self.part].astype(F32)
            away += held[z, 1 - p.y].astype(F32)
            self.sy[z] = away.astype(self.kind)
            self.y[k].start()
            self.add((z, p.y, p.c, slice(None), self.part), held[z, p.y])

    def start_z(self, pieces=range(4)):
        ry, p = self.buffers[2], self.place
        for k in pieces:
            owner = self.lines[k]
            self.y[k].wait_recv()
            if k == 0:
                self.add((owner, p.y, p.c, slice(None), self.part), ry[owner])
                continue
            away = self.grad[owner, p.y, p.c, :, self.part].astype(F32) + ry[owner].astype(F32)
            self.sz[k - 1][...] = away.astype(self.kind)
            self.z[k - 1].start()

    def start_x(self):
        rz, p = self.buffers[3], self.place
        for copy in self.z:
            copy.wait_recv()
        near = self.grad[p.z, p.y, p.c, :, self.part].astype(F32) + rz[0].astype(F32)
        self.sx[...] = (near + (rz[1].astype(F32) + rz[2].astype(F32))).astype(self.kind)
        self.x.start()

    def finish(self, out):
        rx = self.buffers[4]
        self.x.wait_recv()
        if self.halved:
            out[:, self.part] = self.sx[...].astype(F32)
            out[:, self.away] = rx[...].astype(F32)
        else:
            out[:, self.cols] = self.sx[...].astype(F32) + rx[...].astype(F32)

    def close(self):
        for copy in self.z + self.y + [self.x] + (self.x1 if self.halved else []):
            copy.wait_send()


def reduce_leads(halved):
    leads = [((4, 2), False), ((4, 2), False), ((4,), halved), ((3,), halved), ((), halved)]
    return leads + ([((4, 2), True)] if halved else [])


def layer_scratch(row_count, width, hidden_width, shards):
    tile = 256
    seqs = row_count // LENGTH
    pairs = dict(
        active=((tile, hidden_width), BF16),
        slope=((tile, hidden_width), BF16),
        two_t=((width, tile), BF16),
        unit=((tile, width), F32),
        last=((tile, width), F32),
        scale=((tile, 1), F32),
    )
    both = {(name, side): item for name, item in pairs.items() for side in range(2)}
    return both | dict(
        tokens=((row_count, width), BF16),
        middle_grad=((row_count, width), F32),
        normed_t=((width, row_count), BF16),
        qkv=((row_count, 3 * width), BF16),
        attended=((row_count, width), BF16),
        totals=((seqs, width), F32),
        causal=((LENGTH, WIDE), F32),
        advantage=((1, row_count), F32),
        action_row=((1, row_count), jnp.int32),
        two_low=((tile, width), BF16),
        low=((tile, width), BF16),
        low_t=((width, tile), BF16),
        two_in=((tile, width), F32),
        hidden_grad=((tile, hidden_width // 4), BF16),
        local_sem=pltpu.SemaphoreType.DMA((2,)),
    )


def grad_shapes(width, hidden_width, shards):
    split = SPLIT
    part, hidden_part = width // shards, hidden_width // shards
    return dict(
        g_qkv=(split + (part, 3 * width), BF16),
        g_out=(split + (part, width), F32),
        g_up=(split + (part, hidden_width), F32),
        g_down=(split + (width, hidden_part), F32),
        g_actor=((SLOTS, width), F32),
        g_small=((7, 8, width), F32),
        g_up_bias=((8, hidden_width), F32),
        g_positions=((LENGTH, width), F32),
        head_sums=((SLOTS + 8, 128), F32),
    )


def at_step(i, table):
    for step, actions in table.items():

        @pl.when(i == step)
        def _(actions=actions):
            for action in actions:
                action()


def spread_kernel(names, scale, *refs):
    r = Names(names, refs)
    place = Place()
    load = pltpu.make_async_copy(r.tokens_in, r.tokens, r.local_sem.at[0])
    load.start()
    partners = place.partners()
    barrier = pltpu.get_barrier_semaphore()
    for device in partners:
        pl.semaphore_signal(barrier, inc=1, device_id=device, device_id_type=MESH)
    pack_shards(r)
    pl.semaphore_wait(barrier, len(partners))
    width, hidden_width = r.w_out.shape[-1], r.w_up.shape[-1]
    plan = [(r.pack, r.pack_own, 0, 128)]
    plan += [(r.w_qkv, r.qkv_in, k * width, width) for k in range(3)]
    plan += [(r.w_out, r.out_in, 0, width)]
    half = hidden_width // 2
    plan += [(r.w_up, r.up_in, k * half, half, True) for k in range(2)]
    plan += [(r.w_down, r.down_in, k * width // 2, width // 2, True) for k in range(2)]
    gathers = [Gather(r, place, k, *item) for k, item in enumerate(plan)]
    pack, q, k, v, out, up0, up1, down0, down1 = gathers
    pack.start_z()
    q.start_z()
    k.start_z()
    v.start_z()
    pack.start_y()
    q.start_y()
    pack.start_c()
    for group in (out, up0, up1, down0, down1):
        group.start_z()
    frame_values(r)
    k.start_y()
    pack.ready()
    unpack_shards(r)
    v.start_y()
    q.start_c()
    load.wait()
    norm_pass(r)
    k.start_c()
    v.start_c()
    q.ready()
    project_third(r, 0)
    clear(r)
    k.ready()
    project_third(r, 1)
    v.ready()
    project_third(r, 2)

    front(
        r,
        lambda i: at_step(
            i,
            {
                1: [out.start_y],
                3: [up0.start_y, out.start_c],
                5: [up1.start_y, up0.start_x],
                7: [down0.start_y, up1.start_x, up0.start_c],
                9: [down1.start_y, down0.start_x, up1.start_c],
            },
        ),
    )
    out.ready()

    def arrive():
        down1.start_x()
        down0.start_c()
        down1.start_c()
        for group in (up0, up1, down0, down1):
            group.ready()

    middle_part(r, scale, arrive)

    plan = [(r.g_down,), (r.g_up,), (r.g_out,)]
    plan += [(r.g_qkv, k * width) for k in range(3)] + [(r.g_pack,)]
    reduces = [Reduce(r, place, k, *item) for k, item in enumerate(plan)]
    down, up, out, q, k, v, pack = reduces
    down.start_c()
    up.start_c()
    out.start_c()
    attend_back(
        r,
        lambda i: at_step(
            i,
            {
                1: [down.start_y],
                2: [up.start_x1],
                3: [out.start_x1],
                7: [lambda: up.start_y([0])],
                9: [lambda: down.start_z([0, 1]), lambda: up.start_y([1])],
            },
        ),
    )
    qkv_weight_grad(r, 0)
    q.start_c()
    down.start_z([2])
    up.start_y([2])
    qkv_weight_grad(r, 2)
    v.start_c()
    q.start_y()
    down.start_z([3])
    up.start_y([3])
    qkv_weight_grad(r, 1)
    k.start_c()
    v.start_x1()
    k.start_y()

    def stored(i):
        rows = pl.ds(pl.multiple_of(i * 4 * LENGTH, 4 * LENGTH), 4 * LENGTH)
        return pltpu.make_async_copy(
            r.middle_grad.at[rows, :], r.tokens_grad.at[rows, :], r.store_sem.at[i]
        )

    start_back(
        r,
        lambda i: at_step(
            i,
            {
                1: [out.start_y],
                3: [up.start_z],
                4: [v.start_y],
                5: [q.start_z],
                6: [out.start_z],
                8: [down.start_x],
                9: [k.start_z],
            },
        ),
        lambda i: stored(i).start(),
    )
    pack_grads(r)
    pack.start_c()
    v.start_z()
    q.start_x()
    pack.start_y()
    up.start_x()
    out.start_x()
    k.start_x()
    pack.start_z()
    v.start_x()
    down.finish(r.down_out)
    pack.start_x()
    up.finish(r.up_out)
    out.finish(r.out_out)
    for group in (q, k, v):
        group.finish(r.qkv_out)
    for i in range(r.middle_grad.shape[0] // (4 * LENGTH)):
        stored(i).wait()
    for group in gathers + reduces:
        group.close()
    pack.finish(r.pack_out)


def finish_kernel(names, count, *refs):
    r = Names(names, refs)
    step = 4 * LENGTH
    parts = [pl.ds(at, step) for at in range(0, r.tokens.shape[0], step)]
    loads = [
        pltpu.make_async_copy(r.tokens.at[part, :], r.held.at[part, :], r.load_sem.at[k])
        for k, part in enumerate(parts)
    ]
    stores = [
        pltpu.make_async_copy(r.held.at[part, :], r.o_tokens.at[part, :], r.store_sem.at[k])
        for k, part in enumerate(parts)
    ]
    for load in loads:
        load.start()
    r.o_qkv[...] = r.qkv[...]
    r.o_out[...] = r.out[...]
    r.o_up[...] = r.up[...]
    r.o_down[...] = r.down[...].T
    r.o_stats[...] = DECAY_RATE * r.running[...] + (1.0 - DECAY_RATE) * r.percentiles[...]
    part, positions = r.o_positions.shape
    slots = r.o_actor.shape[0]
    features = r.pack[0:part, :]
    r.o_positions[...] = features[:, POSITION_AT : POSITION_AT + positions]
    turned = features.T
    vectors = (r.gain1, r.bias1, r.gain2, r.bias2, r.bias_down, r.gain3, r.bias3)
    for k, ref in enumerate(vectors):
        ref[...] = turned[SMALL_AT + k : SMALL_AT + k + 1, :].reshape(part)
    r.o_actor[...] = turned[SMALL_AT + 7 : SMALL_AT + 7 + slots, :]
    r.o_actor_bias[...] = turned[BIAS_AT : BIAS_AT + 1, :].reshape(part)[0:slots]
    r.o_loss[...] = features[0:1, LOSS_AT : LOSS_AT + 1] * (1.0 / count)
    r.o_up_bias[...] = r.pack[part : part + 1, :].reshape(128)
    for load, store in zip(loads, stores, strict=True):
        load.wait()
        store.start()
    for store in stores:
        store.wait()


def local_kernel(names, scale, *refs):
    r = Names(names, refs)
    load = pltpu.make_async_copy(r.tokens_in, r.tokens, r.local_sem.at[0])
    load.start()
    clear(r)
    frame_values(r)
    load.wait()
    norm_pass(r)
    for third in range(3):
        project_third(r, third)
    front(r, lambda i: None)
    middle_part(r, scale, lambda: None)
    attend_back(r, lambda i: None)
    for third in range(3):
        qkv_weight_grad(r, third)
    start_back(r, lambda i: None, lambda i: None)
    store = pltpu.make_async_copy(r.middle_grad, r.tokens_grad, r.local_sem.at[1])
    store.start()
    store.wait()


def run(kernel, constant, ins, outs, scratch, flops=0, side_effects=False, collective=None):
    vmem = pl.BlockSpec(memory_space=pltpu.VMEM)
    anywhere = pl.BlockSpec(memory_space=pl.ANY)
    in_specs = [anywhere if array.size > LARGE else vmem for array in ins.values()]
    out_specs = [anywhere if math.prod(shape) > LARGE else vmem for shape, _ in outs.values()]
    return pl.pallas_call(
        functools.partial(kernel, (*ins, *outs, *scratch), constant),
        out_shape=[jax.ShapeDtypeStruct(shape, kind) for shape, kind in outs.values()],
        in_specs=in_specs,
        out_specs=out_specs,
        scratch_shapes=[
            item if not isinstance(item, tuple) else pltpu.VMEM(item[0], item[1])
            for item in scratch.values()
        ],
        compiler_params=pltpu.CompilerParams(
            vmem_limit_bytes=VMEM_BYTES, has_side_effects=side_effects, collective_id=collective
        ),
        cost_estimate=pl.CostEstimate(flops=flops, bytes_accessed=1 << 24, transcendentals=0),
    )(*ins.values())


def on_device(
    tokens,
    positions,
    norm_one_gain,
    norm_one_bias,
    qkv_weight,
    out_weight,
    norm_two_gain,
    norm_two_bias,
    up_weight,
    up_bias,
    down_weight,
    down_bias,
    final_gain,
    final_bias,
    actor_weight,
    actor_bias,
    actions,
    action_masks,
    game_ids,
    returns,
    values,
    running,
    percentiles,
):
    row_count, width = tokens.shape
    seq_count = row_count // LENGTH
    hidden_width = up_weight.shape[1]
    slots = actor_weight.shape[1]
    fsdp = lax.axis_size("fsdp")
    device_count = lax.axis_size("dp") * fsdp
    token_total = row_count * device_count
    scale = float(seq_count * device_count) / token_total
    flops = 6 * row_count * width * (4 * width + 2 * hidden_width)
    part, hidden_part = width // fsdp, hidden_width // fsdp

    vectors = dict(
        gain1=norm_one_gain,
        bias1=norm_one_bias,
        gain2=norm_two_gain,
        bias2=norm_two_bias,
        bias_down=down_bias,
        gain3=final_gain,
        bias3=final_bias,
    )
    stats = dict(running=running, percentiles=percentiles)
    frames = stats | dict(
        tokens_in=tokens,
        actor_bias=actor_bias,
        actions=actions,
        masks=action_masks.T,
        game_ids=game_ids,
        returns=returns,
        values=values,
    )
    scratch = layer_scratch(row_count, width, hidden_width, 16)
    grads = grad_shapes(width, hidden_width, 16)
    weight_shapes = dict(
        w_qkv=(SPLIT + (width // 16, 3 * width), BF16),
        w_out=(SPLIT + (width // 16, width), BF16),
        w_up=(SPLIT + (width // 16, hidden_width), BF16),
        w_down=(SPLIT + (hidden_width // 16, width), BF16),
    )

    if fsdp == 16 and lax.axis_size("dp") == 2:
        ins = frames | vectors
        ins |= dict(qkv_in=qkv_weight, out_in=out_weight, up_in=up_weight, down_in=down_weight)
        ins |= dict(up_bias_in=up_bias, positions_in=positions.T, actor_in=actor_weight.T)
        shard_grads = dict(
            qkv_out=((part, 3 * width), F32),
            out_out=((part, width), F32),
            up_out=((part, hidden_width), F32),
            down_out=((width, hidden_part), F32),
        )
        outs = dict(
            tokens_grad=((row_count, width), F32), pack_out=((PACK_GRAD_ROWS, 128), F32)
        )
        scratch |= grads | weight_shapes
        scratch |= dict(
            pack=(SPLIT + (PACK_ROWS, 128), BF16),
            pack_own=((PACK_ROWS, 128), BF16),
            g_pack=(SPLIT + (PACK_GRAD_ROWS, 128), F32),
            positions=((LENGTH, width), F32),
            small=((8, width), F32),
            actor=((SLOTS, width), BF16),
            up_bias=((1, hidden_width), F32),
            gather_send=pltpu.SemaphoreType.DMA((GATHERS, 15)),
            gather_recv=pltpu.SemaphoreType.DMA((GATHERS, 15)),
            reduce_send=pltpu.SemaphoreType.DMA((len(REDUCES), 16)),
            reduce_recv=pltpu.SemaphoreType.DMA((len(REDUCES), 16)),
            store_sem=pltpu.SemaphoreType.DMA((row_count // (4 * LENGTH),)),
        )
        for index, (count, rows, kind, halved) in enumerate(REDUCES):
            for item, (lead, half) in enumerate(reduce_leads(halved)):
                scratch[index, item] = (lead + (rows, count // 2 if half else count), kind)
        tokens_grad, pack, qkv_g, out_g, up_g, down_g = run(
            spread_kernel, scale, ins, outs | shard_grads, scratch, flops, True, 0
        )
        vector = ((part,), F32)
        final = dict(
            o_loss=((1, 1), F32),
            o_stats=(running.shape, F32),
            o_positions=((part, LENGTH), F32),
            o_qkv=shard_grads["qkv_out"],
            o_out=shard_grads["out_out"],
            o_up=shard_grads["up_out"],
            o_down=((hidden_part, width), F32),
            o_up_bias=((hidden_part,), F32),
            o_actor=((slots, part), F32),
            o_actor_bias=((slots,), F32),
            o_tokens=((row_count, width), F32),
        )
        copies = pltpu.SemaphoreType.DMA((row_count // (4 * LENGTH),))
        done = run(
            finish_kernel,
            token_total,
            stats
            | dict(pack=pack, qkv=qkv_g, out=out_g, up=up_g, down=down_g, tokens=tokens_grad),
            final | dict.fromkeys(vectors, vector),
            dict(held=((row_count, width), F32), load_sem=copies, store_sem=copies),
        )
        loss, new_stats, pos_g, qkv_g, out_g, up_g, down_g = done[:7]
        up_bias_g, actor_g, actor_bias_g, tokens_grad = done[7:11]
        gain1, bias1, gain2, bias2, bias_down, gain3, bias3 = done[11:]
        return (
            loss.reshape(()),
            new_stats,
            tokens_grad,
            pos_g.T,
            gain1,
            bias1,
            qkv_g,
            out_g,
            gain2,
            bias2,
            up_g,
            up_bias_g,
            down_g,
            bias_down,
            gain3,
            bias3,
            actor_g.T,
            actor_bias_g,
        )

    def gather(array, axis):
        return lax.all_gather(array, "fsdp", axis=axis, tiled=True)

    packed = gather(
        jnp.concatenate([jnp.stack(list(vectors.values())), actor_weight.T, positions], 0), 1
    )
    fulls = [gather(weight, 0) for weight in (qkv_weight, out_weight, up_weight, down_weight)]
    ins = frames | {
        name: full.reshape(weight_shapes[name][0])
        for name, full in zip(weight_shapes, fulls, strict=True)
    }
    ins |= dict(
        positions=packed[7 + slots :].astype(F32),
        small=jnp.pad(packed[0:7].astype(F32), ((0, 1), (0, 0))),
        actor=jnp.pad(packed[7 : 7 + slots], ((0, SLOTS - slots), (0, 0))),
        up_bias=gather(up_bias, 0).astype(F32).reshape(1, hidden_width),
    )
    outs = dict(tokens_grad=((row_count, width), F32)) | grads
    tokens_grad, *sums = run(local_kernel, scale, ins, outs, scratch, flops)
    sums = Names(grads, sums)

    def scatter(array, axis):
        piece = lax.psum_scatter(array, "fsdp", scatter_dimension=axis, tiled=True)
        return lax.psum(piece.astype(BF16), "dp").astype(F32)

    down_sum = jnp.swapaxes(sums.g_down, 3, 4)
    qkv_part, out_part, up_part, down_part = (
        scatter(merged(grad).astype(F32), 0)
        for grad in (sums.g_qkv, sums.g_out, sums.g_up, down_sum)
    )
    rows = [jnp.sum(sums.g_small, 1), sums.g_actor[:slots], sums.g_positions]
    side = scatter(jnp.concatenate(rows, 0), 1)
    up_bias_part = scatter(jnp.sum(sums.g_up_bias, 0), 0)
    head_total = lax.psum(jnp.sum(sums.head_sums[: SLOTS + 1], 1), ("dp", "fsdp"))
    return (
        head_total[SLOTS] / token_total,
        DECAY_RATE * running + (1.0 - DECAY_RATE) * percentiles,
        tokens_grad,
        side[7 + slots :],
        side[G1],
        side[B1],
        qkv_part,
        out_part,
        side[G2],
        side[B2],
        up_part,
        up_bias_part,
        down_part,
        side[DB],
        side[GL],
        side[BL],
        side[7 : 7 + slots].T,
        head_total[:slots],
    )


def solution(mesh):
    rows, cols, both = P(("dp", "fsdp"), None), P(None, "fsdp"), P(("dp", "fsdp"))
    weight, vector, whole = P("fsdp", None), P("fsdp"), P()
    in_specs = (rows, cols, vector, vector, weight, weight, vector, vector, weight, vector)
    in_specs += (weight, vector, vector, vector, weight, whole, both, rows, both, both, both)
    in_specs += (whole, whole)
    out_specs = (whole, whole, rows, cols, vector, vector, weight, weight, vector, vector)
    out_specs += (weight, vector, weight, vector, vector, vector, weight, whole)
    return jax.shard_map(
        on_device, mesh=mesh, in_specs=in_specs, out_specs=out_specs, check_vma=False
    )
```

```python
import functools
import math
import math

import jax
import jax.numpy as jnp
from jax import lax
from jax.experimental import pallas as pl
from jax.experimental.pallas import tpu as pltpu
from jax.sharding import PartitionSpec as P

HEADS = 8
HEAD = 64
LENGTH = 64
QUAD = 4
WIDE = QUAD * HEAD
MASKED = -1e30
EPSILON = 1e-05
DECAY_RATE = 0.9
ENTROPY_WEIGHT = 0.1
SLOTS = 32
VMEM_BYTES = 63 * 1024 * 1024
BF16 = jnp.bfloat16
F32 = jnp.float32

G1, B1, G2, B2, DB, GL, BL = range(7)
MESH = pl.DeviceIdType.MESH


def dot(left, right, left_dim, right_dim):
    return lax.dot_general(
        left, right, (((left_dim,), (right_dim,)), ((), ())), preferred_element_type=F32
    )


def mean_last(values):
    return jnp.sum(values, -1, keepdims=True) * (1.0 / values.shape[-1])


def normalise(values):
    centred = values - mean_last(values)
    scale = lax.rsqrt(mean_last(centred * centred) + EPSILON)
    return centred * scale, scale


def norm_back(unit, scale, gain, upstream):
    inner = upstream * gain
    return scale * (inner - mean_last(inner) - unit * mean_last(inner * unit))


def fold_rows(values):
    rows, width = values.shape
    return jnp.sum(values.reshape(rows // 8, 8, width), 0)


def gelu_pair(values):
    half = jnp.exp2(values * values * (-0.5 * 1.4426950408889634))
    span = 1.0 + jnp.abs(values) * (0.3275911 * 0.7071067811865476)
    t = 1.0 / span
    poly = t * (
        0.5 * 0.254829592
        + t
        * (
            0.5 * -0.284496736
            + t * (0.5 * 1.421413741 + t * (0.5 * -1.453152027 + t * (0.5 * 1.061405429)))
        )
    )
    tail = poly * half
    cdf = jnp.where(values < 0.0, tail, 1.0 - tail)
    density = half * 0.3989422804014327
    return values * cdf, cdf + values * density


def pair_masks():
    lane = lax.broadcasted_iota(jnp.int32, (LENGTH, 2 * HEAD), 1)
    first = jnp.where(lane < HEAD, 1.0, 0.0)
    return first.astype(BF16), (1.0 - first).astype(BF16)


def spread_heads(rows, masks):
    zero = jnp.zeros((LENGTH, 2 * HEAD), BF16)
    left, right = rows[:, : 2 * HEAD], rows[:, 2 * HEAD :]
    blocks = [jnp.concatenate([left * mask, zero], 1) for mask in masks]
    blocks += [jnp.concatenate([zero, right * mask], 1) for mask in masks]
    return jnp.concatenate(blocks, 0)


def pair_products(left, right):
    lane = lax.broadcasted_iota(jnp.int32, (LENGTH, 2 * HEAD), 1)
    pairs = []
    for at in range(0, WIDE, 2 * HEAD):
        block = dot(left[:, at : at + 2 * HEAD], right[:, at : at + 2 * HEAD], 0, 0)
        pairs.append(jnp.where(lane < HEAD, block[0:HEAD], block[HEAD : 2 * HEAD]))
    return jnp.concatenate(pairs, 1)


def causal_bias():
    key = lax.broadcasted_iota(jnp.int32, (LENGTH, WIDE), 0)
    query = lax.rem(lax.broadcasted_iota(jnp.int32, (LENGTH, WIDE), 1), HEAD)
    return jnp.where(key <= query, 0.0, MASKED)


LOG2E = 1.4426950408889634
SCORE_SCALE = HEAD ** (-0.5) * LOG2E


def chains(r, i):
    width = r.tokens.shape[1]
    found = []
    for s in range(4):
        row = pl.multiple_of((4 * i + s) * LENGTH, LENGTH)
        for half in range(width // WIDE):
            at = half * WIDE
            columns = [slice(k * width + at, k * width + at + WIDE) for k in range(3)]
            found.append((4 * i + s, pl.ds(row, LENGTH), columns))
    return found


def attend_group(r, i):
    masks, bias = pair_masks(), r.causal[...]
    group = chains(r, i)
    loaded = [[r.qkv[rows, part] for part in parts] for _, rows, parts in group]
    scores = [dot(key, spread_heads(query, masks), 1, 1) for query, key, _ in loaded]
    probs, totals = [], []
    for score in scores:
        score = score * SCORE_SCALE + bias
        highest = jnp.max(score, 0, keepdims=True)
        weights = jnp.exp2(score - highest)
        summed = jnp.sum(weights, 0, keepdims=True)
        probs.append((weights * (1.0 / summed)).astype(BF16))
        totals.append(highest + jnp.log(summed) * LOG2E)
    done = [
        pair_products(prob, value).astype(BF16)
        for prob, (_, _, value) in zip(probs, loaded, strict=True)
    ]
    for (seq, rows, (q, _, _)), result, total in zip(group, done, totals, strict=True):
        r.attended[rows, q] = result
        r.totals[pl.ds(seq, 1), q] = total


def attend_back_group(r, i):
    masks, bias = pair_masks(), r.causal[...]
    done = []
    for half in range(2):
        group = chains(r, i)[half::2]
        queries = [spread_heads(r.qkv[rows, q], masks) for _, rows, (q, _, _) in group]
        aboves = [spread_heads(r.attended[rows, q], masks) for _, rows, (q, _, _) in group]
        scores = [
            dot(r.qkv[rows, k], query, 1, 1)
            for (_, rows, (_, k, _)), query in zip(group, queries, strict=True)
        ]
        prob_grads = [
            dot(r.qkv[rows, v], above, 1, 1)
            for (_, rows, (_, _, v)), above in zip(group, aboves, strict=True)
        ]
        probs, score_grads = [], []
        for (seq, _, (q, _, _)), score, pull in zip(group, scores, prob_grads, strict=True):
            prob = jnp.exp2(score * SCORE_SCALE + bias - r.totals[pl.ds(seq, 1), q])
            row_terms = jnp.sum(pull * prob, 0, keepdims=True)
            score_grads.append((prob * (pull - row_terms)).astype(BF16))
            probs.append(prob.astype(BF16))
        value_grads = [dot(prob, above, 1, 0) for prob, above in zip(probs, aboves, strict=True)]
        key_grads = [dot(grad, query, 1, 0) for grad, query in zip(score_grads, queries, strict=True)]
        query_grads = [
            pair_products(grad, r.qkv[rows, k])
            for (_, rows, (_, k, _)), grad in zip(group, score_grads, strict=True)
        ]
        for (_, rows, (q, k, v)), dq, dk, dv in zip(
            group, query_grads, key_grads, value_grads, strict=True
        ):
            done.append((rows, q, (dq * HEAD ** (-0.5)).astype(BF16)))
            done.append((rows, k, (dk * HEAD ** (-0.5)).astype(BF16)))
            done.append((rows, v, dv.astype(BF16)))
    for rows, columns, grad in done:
        r.qkv[rows, columns] = grad


def policy(logits, masks, actions, advantage, scale):
    allowed = masks > 0
    held = jnp.where(allowed, logits, MASKED)
    shifted = held - jnp.max(held, 0, keepdims=True)
    weights = jnp.exp(shifted)
    summed = jnp.sum(weights, 0, keepdims=True)
    log_probs = shifted - jnp.log(summed)
    probs = weights * (1.0 / summed)
    plogp = jnp.where(allowed, probs * log_probs, 0.0)
    entropy = -jnp.sum(plogp, 0, keepdims=True)
    slot = lax.broadcasted_iota(jnp.int32, logits.shape, 0)
    taken = slot == actions
    chosen = jnp.sum(jnp.where(taken, log_probs, 0.0), 0, keepdims=True)
    loss = -advantage * chosen - ENTROPY_WEIGHT * entropy
    pull = advantage * (probs - jnp.where(taken, 1.0, 0.0)) + ENTROPY_WEIGHT * (
        plogp + probs * entropy
    )
    return loss, jnp.where(allowed, pull * scale, 0.0)


STRIP = 32
THIN = 16
LARGE = 1 << 20


class Names:
    def __init__(self, names, refs):
        self.table = dict(zip(names, refs, strict=True))

    def __getattr__(self, name):
        return self.table[name]


SPLIT = (4, 2, 2)
PACK_ROWS = 48
PACK_GRAD_ROWS = 40
POSITION_AT, SMALL_AT, BIAS_AT, LOSS_AT = 0, 64, 96, 97


def merged(block):
    return block.reshape(-1, block.shape[-1])


def strip_rows(row, count):
    return [pl.ds(pl.multiple_of(row + at, STRIP), STRIP) for at in range(0, count, STRIP)]


def load_starts(r, row, count):
    starts = [r.tokens[rows, :].astype(F32) for rows in strip_rows(row, count)]
    frames = [r.positions[at : at + STRIP, :] for at in range(0, LENGTH, STRIP)]
    return [start + frames[k % len(frames)] for k, start in enumerate(starts)]


def norm_pass(r):
    count = r.tokens.shape[0]
    rows = 4 * LENGTH

    def body(i, carry):
        row = pl.multiple_of(i * rows, rows)
        normed = [
            (normalise(start)[0] * r.small[G1 : G1 + 1, :] + r.small[B1 : B1 + 1, :]).astype(BF16)
            for start in load_starts(r, row, rows)
        ]
        normed = jnp.concatenate(normed, 0)
        turned = normed.T
        r.attended[pl.ds(row, rows), :] = normed
        r.normed_t[:, pl.ds(row, rows)] = turned
        return carry

    lax.fori_loop(0, count // rows, body, 0)


def project_third(r, third):
    count, width = r.tokens.shape
    rows = 8 * LENGTH
    columns = slice(third * width, (third + 1) * width)

    def body(i, carry):
        here = pl.ds(pl.multiple_of(i * rows, rows), rows)
        weight = merged(r.w_qkv[:, :, :, :, columns])
        r.qkv[here, columns] = dot(r.attended[here, :], weight, 1, 0).astype(BF16)
        return carry

    lax.fori_loop(0, count // rows, body, 0)


def front(r, pump):
    count = r.tokens.shape[0]

    def body(i, carry):
        pump(i)
        attend_group(r, i)
        return carry

    lax.fori_loop(0, count // (4 * LENGTH), body, 0)


def add_grad(ref, index, values):
    ref[index] += values.reshape(ref[index].shape)


def add_columns(ref, values):
    count = ref.shape[-1]
    for k in range(values.shape[1] // count):
        ref[k // 2, k % 2] += values[:, k * count : (k + 1) * count]


def clear(r):
    for ref in (r.g_out, r.g_up, r.g_down):

        def body(z, carry, ref=ref):
            ref[z] = jnp.zeros(ref.shape[1:], F32)
            return carry

        lax.fori_loop(0, ref.shape[0], body, 0)
    for ref in (r.g_actor, r.g_small, r.g_up_bias, r.g_positions, r.head_sums):
        ref[...] = jnp.zeros_like(ref)


def frame_values(r):
    r.causal[...] = causal_bias()
    fresh = DECAY_RATE * r.running[...] + (1.0 - DECAY_RATE) * r.percentiles[...]
    spread = jnp.maximum(1.0, fresh[1:2, :] - fresh[0:1, :])
    seqs = r.game_ids.shape[0]
    game = r.game_ids[...].reshape(seqs, 1)
    slot = lax.broadcasted_iota(jnp.int32, (seqs, spread.shape[1]), 1)
    column = jnp.sum(jnp.where(slot == game, spread, 0.0), 1, keepdims=True)
    count = 8 * LENGTH
    owner = lax.broadcasted_iota(jnp.int32, (8, count), 0)
    frame = lax.broadcasted_iota(jnp.int32, (8, count), 1)
    for k in range(seqs // 8):
        here = slice(k * count, (k + 1) * count)
        near = jnp.where(frame // LENGTH == owner, column[8 * k : 8 * k + 8], 0.0)
        wide = jnp.sum(near, 0, keepdims=True)
        r.advantage[:, here] = (r.returns[here] - r.values[here]).reshape(1, count) / wide
        r.action_row[:, here] = r.actions[here].reshape(1, count)


class Tile:
    def __init__(self, r, side):
        def pick(name):
            return r.table[name, side]

        self.active, self.slope = pick("active"), pick("slope")
        self.two_t, self.unit, self.last = pick("two_t"), pick("unit"), pick("last")
        self.scale = pick("scale")


def middle_part(r, scale, arrive):
    count, width = r.tokens.shape
    rows = r.low.shape[0]
    shards = r.w_up.shape[0]
    chunk = r.w_up.shape[-1] // shards
    slots = r.masks.shape[0]
    out_weight = r.w_out
    head_bias = jnp.concatenate(
        [r.actor_bias[...].astype(F32).reshape(slots, 1), jnp.zeros((SLOTS - slots, 1), F32)], 0
    )
    everything = slice(None)
    strips = [slice(at, at + STRIP) for at in range(0, rows, STRIP)]

    def gain(k):
        return r.small[k : k + 1, :]

    def tile_rows(i):
        return pl.ds(pl.multiple_of(i * rows, rows), rows)

    def before(t, tokens, attended):
        projected = dot(attended, merged(out_weight[...]), 1, 0)
        for k, strip in enumerate(strips):
            frame = k * STRIP % LENGTH
            start = tokens[k].astype(F32) + r.positions[frame : frame + STRIP, :]
            mid = start + projected[strip]
            unit, spread = normalise(mid)
            r.two_low[strip, :] = (unit * gain(G2) + gain(B2)).astype(BF16)
            t.unit[strip, :] = unit
            t.scale[strip, :] = spread
            t.last[strip, :] = mid + gain(DB)
        t.two_t[...] = r.two_low[...].T

    def columns(j):
        return slice(j * chunk, (j + 1) * chunk)

    def up_weight(j):
        return merged(r.w_up[:, :, :, :, columns(j)])

    def activate(hidden, bias):
        done = [gelu_pair(hidden[at : at + THIN] + bias) for at in range(0, rows, THIN)]
        values = jnp.concatenate([value.astype(BF16) for value, _ in done], 0)
        return values, jnp.concatenate([slope.astype(BF16) for _, slope in done], 0)

    def forward_only(j, t):
        cols = columns(j)
        weight, bias, down = up_weight(j), r.up_bias[:, cols], merged(r.w_down[j])
        active, slope = activate(dot(r.two_low[...], weight, 1, 0), bias)
        t.last[...] += dot(active, down, 1, 0)
        t.active[:, cols], t.slope[:, cols] = active, slope

    def both_ways(j, here, there):
        cols = columns(j)
        bias, total = r.up_bias[:, cols], r.g_up_bias[:, cols]
        if there is not None:
            hidden = dot(r.two_low[...], up_weight(j), 1, 0)
        above = dot(r.low[...], merged(r.w_down[j]), 1, 1)
        for at in range(0, rows, THIN):
            strip = slice(at, at + THIN)
            part = (above[strip] * here.slope[strip, cols].astype(F32)).astype(BF16)
            here.slope[strip, cols] = part
            total += fold_rows(part.astype(F32))
        add_columns(r.g_down.at[j], dot(r.low_t[...], here.active[:, cols], 1, 0))
        add_grad(
            r.g_up,
            (everything, everything, everything, everything, cols),
            dot(here.two_t[...], here.slope[:, cols], 1, 0),
        )
        r.g_up_bias[:, cols] = total
        if there is not None:
            active, slope = activate(hidden, bias)
            there.last[...] += dot(active, merged(r.w_down[j]), 1, 0)
            there.active[:, cols], there.slope[:, cols] = active, slope

    def chunks(step):
        for j in range(shards):
            step(j)

    def last_norm(t):
        spreads = []
        for strip in strips:
            unit, spread = normalise(t.last[strip, :])
            r.low[strip, :] = (unit * gain(GL) + gain(BL)).astype(BF16)
            t.last[strip, :] = unit
            spreads.append(spread)
        return spreads, dot(r.actor[...], r.low[...], 1, 1) + head_bias

    def head(logits, masks, actions, advantage):
        masks = jnp.concatenate([masks, jnp.zeros((SLOTS - slots, rows), jnp.int32)], 0)
        loss, pull = policy(logits, masks, actions, advantage, scale)
        logit_grad = pull.astype(BF16)
        last_in = dot(logit_grad, r.actor[...], 0, 0)
        r.g_actor[...] += dot(logit_grad, r.low[...], 1, 0)
        wide_grad = logit_grad.astype(F32)
        fold = r.head_sums[0:SLOTS, :]
        for at in range(0, rows, 128):
            fold += wide_grad[:, at : at + 128]
        r.head_sums[0:SLOTS, :] = fold
        fold = r.head_sums[SLOTS : SLOTS + 1, :]
        for at in range(0, rows, 128):
            fold += loss[:, at : at + 128]
        r.head_sums[SLOTS : SLOTS + 1, :] = fold
        return last_in

    def last_norm_back(t, spreads, last_in):
        sums = [r.g_small[k] for k in (GL, BL, DB)]
        for strip, spread in zip(strips, spreads, strict=True):
            above, unit = last_in[strip], t.last[strip, :]
            grad = norm_back(unit, spread, gain(GL), above)
            sums[0] += fold_rows(above * unit)
            sums[1] += fold_rows(above)
            sums[2] += fold_rows(grad)
            t.last[strip, :] = grad
            r.low[strip, :] = grad.astype(BF16)
        for k, total in zip((GL, BL, DB), sums, strict=True):
            r.g_small[k] = total
        r.low_t[...] = r.low[...].T

    def two_norm_back(t):
        sums = [r.g_small[k] for k in (G2, B2)]
        for strip in strips:
            above, unit = r.two_in[strip, :], t.unit[strip, :]
            sums[0] += fold_rows(above * unit)
            sums[1] += fold_rows(above)
            grad = t.last[strip, :] + norm_back(unit, t.scale[strip, :], gain(G2), above)
            t.last[strip, :] = grad
            r.hidden_grad[strip, :] = grad.astype(BF16)
        for k, total in zip((G2, B2), sums, strict=True):
            r.g_small[k] = total

    def out_back(i, t, attended):
        low = r.hidden_grad[...]
        add_grad(r.g_out, ..., dot(attended, low, 0, 0))
        r.attended[tile_rows(i), :] = dot(low, merged(out_weight[...]), 1, 1).astype(BF16)
        r.middle_grad[tile_rows(i), :] = t.last[...]

    sides = [Tile(r, 0), Tile(r, 1)]
    tiles = count // rows

    def begin(i):
        row = pl.multiple_of(i * rows, rows)
        return [r.tokens[part, :] for part in strip_rows(row, rows)], r.attended[tile_rows(i), :]

    def step(i, side, first=False, last=False):
        here, there = sides[side], sides[1 - side]
        at = tile_rows(i)
        side_data = r.masks[:, at], r.action_row[:, at], r.advantage[:, at]
        if not first:
            attended = r.attended[tile_rows(i - 1), :]
        if not last:
            ahead = begin(i + 1)
        spreads, logits = last_norm(here)
        if not first:
            two_norm_back(there)
        last_in = head(logits, *side_data)
        if not first:
            out_back(i - 1, there, attended)
        last_norm_back(here, spreads, last_in)
        if not last:
            before(there, *ahead)
        chunks(lambda j: both_ways(j, here, None if last else there))
        r.two_in[...] = dot(here.slope[...], merged(r.w_up[...]), 1, 1)

    before(sides[0], *begin(0))
    arrive()
    chunks(lambda j: forward_only(j, sides[0]))
    step(0, 0, first=True)

    def pair(p, carry):
        step(2 * p + 1, 1)
        step(2 * p + 2, 0)
        return carry

    lax.fori_loop(0, (tiles - 2) // 2, pair, 0)
    step(tiles - 1, 1, last=True)
    two_norm_back(sides[1])
    out_back(tiles - 1, sides[1], r.attended[tile_rows(tiles - 1), :])


def attend_back(r, pump):
    count = r.tokens.shape[0]
    rows = 4 * LENGTH

    def body(i, carry):
        pump(i)
        attend_back_group(r, i)
        return carry

    lax.fori_loop(0, count // rows, body, 0)


def qkv_weight_grad(r, third):
    width = r.tokens.shape[1]
    step = width // 2
    for at in range(third * width, (third + 1) * width, step):
        values = dot(r.normed_t[...], r.qkv[:, at : at + step], 1, 0)
        values = values.astype(BF16).reshape(r.g_qkv.shape[:4] + (step,))
        r.g_qkv[:, :, :, :, at : at + step] = values


def start_back(r, pump, tile_done):
    count = r.tokens.shape[0]
    rows = 4 * LENGTH
    gain = r.small[G1 : G1 + 1, :]

    def body(i, carry):
        pump(i)
        row = pl.multiple_of(i * rows, rows)
        starts = load_starts(r, row, rows)
        one_in = dot(r.qkv[pl.ds(row, rows), :], merged(r.w_qkv[...]), 1, 1)
        sums = [r.g_small[k] for k in (G1, B1)]
        frames = [r.g_positions[at : at + STRIP, :] for at in range(0, LENGTH, STRIP)]
        grads = []
        for k, (start, there) in enumerate(zip(starts, strip_rows(row, rows), strict=True)):
            unit, scale = normalise(start)
            above = one_in[k * STRIP : (k + 1) * STRIP]
            sums[0] += fold_rows(above * unit)
            sums[1] += fold_rows(above)
            grads.append(r.middle_grad[there, :] + norm_back(unit, scale, gain, above))
            frames[k % len(frames)] += grads[k]
        r.g_positions[...] = jnp.concatenate(frames, 0)
        for k, total in zip((G1, B1), sums, strict=True):
            r.g_small[k] = total
        r.attended[pl.ds(row, rows), :] = jnp.concatenate(grads, 0).astype(BF16)
        tile_done(i)
        return carry

    lax.fori_loop(0, count // rows, body, 0)


def pack_shards(r):
    part = r.positions_in.shape[0]
    slots = r.masks.shape[0]
    rows = [
        ref[...].astype(F32).reshape(1, part)
        for ref in (r.gain1, r.bias1, r.gain2, r.bias2, r.bias_down, r.gain3, r.bias3)
    ]
    rows += [r.actor_in[...].astype(F32), jnp.zeros((32 - 7 - slots, part), F32)]
    features = jnp.concatenate(
        [r.positions_in[...].astype(F32), jnp.concatenate(rows, 0).T, jnp.zeros((part, 32), F32)], 1
    )
    bias = r.up_bias_in[...].astype(F32).reshape(1, 128)
    packed = jnp.concatenate([features, bias, jnp.zeros((PACK_ROWS - part - 1, 128), F32)], 0)
    r.pack_own[...] = packed.astype(BF16)


def unpack_shards(r):
    slots = r.masks.shape[0]
    blocks = r.pack[...].astype(F32).reshape(-1, PACK_ROWS, 128)
    part = r.positions_in.shape[0]
    features = merged(blocks[:, :part, :]).T
    r.positions[...] = features[POSITION_AT : POSITION_AT + LENGTH]
    small = features[SMALL_AT : SMALL_AT + 32]
    r.small[...] = small[0:8]
    width = small.shape[1]
    r.actor[...] = jnp.concatenate(
        [small[7 : 7 + slots], jnp.zeros((SLOTS - slots, width), F32)], 0
    ).astype(BF16)
    r.up_bias[...] = jnp.concatenate(
        [blocks[f, part : part + 1, :] for f in range(blocks.shape[0])], 1
    )


def small_rows(r):
    slots = r.masks.shape[0]
    rows = [jnp.sum(r.g_small[k], 0, keepdims=True) for k in range(7)]
    return jnp.concatenate(
        rows + [r.g_actor[0:slots, :], jnp.zeros((32 - 7 - slots, rows[0].shape[1]), F32)], 0
    )


def pack_grads(r):
    width = r.tokens.shape[1]
    part = r.positions_in.shape[0]
    features = jnp.concatenate(
        [r.g_positions[...], small_rows(r), jnp.zeros((128 - SMALL_AT - 32, width), F32)], 0
    ).T
    sums = jnp.sum(r.head_sums[0 : SLOTS + 8, :], 1, keepdims=True)
    lane = lax.broadcasted_iota(jnp.int32, (part, 128), 1)
    bias = jnp.sum(r.g_up_bias[...], 0, keepdims=True)
    shape = r.g_pack.shape
    for f in range(width // part):
        block = features[f * part : (f + 1) * part]
        block = jnp.where(lane == BIAS_AT, sums[0:SLOTS], block)
        block = jnp.where(lane == LOSS_AT, sums[SLOTS : SLOTS + 1], block)
        owner = (f // 4, f // 2 % 2, f % 2)
        rows = [block, bias[:, f * 128 : (f + 1) * 128], jnp.zeros((shape[3] - part - 1, 128), F32)]
        r.g_pack[owner] = jnp.concatenate(rows, 0)


GATHERS = 9
REDUCES = (
    (128, 512, BF16, False),
    (2048, 32, BF16, True),
    (512, 32, BF16, True),
    (512, 32, BF16, False),
    (512, 32, BF16, False),
    (512, 32, BF16, True),
    (128, PACK_GRAD_ROWS, F32, False),
)


class Place:
    def __init__(self):
        self.x = lax.axis_index("dp")
        f = lax.axis_index("fsdp")
        self.z, self.y, self.c = f // 4, f // 2 % 2, f % 2

    def at(self, x=None, z=None, y=None, c=None):
        pick = lambda new, old: old if new is None else new
        f = pick(z, self.z) * 4 + pick(y, self.y) * 2 + pick(c, self.c)
        return (pick(x, self.x), f)

    def z_partner(self, k):
        return (self.z + 1 - 2 * (self.z % 2), (self.z + 2) % 4, 3 - self.z)[k]

    def lines(self):
        return [self.z] + [self.z_partner(k) for k in range(3)]

    def partners(self):
        return [self.at(z=self.z_partner(k)) for k in range(3)] + [
            self.at(y=1 - self.y),
            self.at(c=1 - self.c),
            self.at(x=1 - self.x),
        ]


def remote(r_send, r_recv, index):
    def copy(src, dst, k, device):
        return pltpu.make_async_remote_copy(
            src_ref=src,
            dst_ref=dst,
            send_sem=r_send.at[index, k],
            recv_sem=r_recv.at[index, k],
            device_id=device,
            device_id_type=MESH,
        )

    return copy


class Gather:
    def __init__(self, r, place, index, full, own, at, count, halved=False):
        p = place
        copy = remote(r.gather_send, r.gather_recv, index)
        cols = part = slice(at, at + count)
        if halved:
            part = pl.ds(pl.multiple_of(at + p.x * (count // 2), 128), count // 2)
        self.full, self.own, self.part, self.place, self.halved = full, own, part, place, halved
        mine = full.at[p.z, p.y, p.c, :, part]
        self.z = [copy(own.at[:, part], mine, k, p.at(z=p.z_partner(k))) for k in range(3)]
        self.y, self.x, self.near, self.far, self.swapped = [], [], [], [], []
        sibling = p.at(c=1 - p.c)
        for k, z in enumerate(p.lines()):
            shard = full.at[z, p.y, p.c, :, part]
            self.y.append(copy(shard, shard, 3 + k, p.at(y=1 - p.y)))
            self.near.append(copy(shard, shard, 7 + k, sibling))
            shard = full.at[z, 1 - p.y, p.c, :, part]
            self.far.append(copy(shard, shard, 11 + k, sibling))
            if halved:
                pair = full.at[z, :, p.c, :, part]
                self.x.append(copy(pair, pair, 15 + k, p.at(x=1 - p.x)))
                other = pl.ds(pl.multiple_of(at + (1 - p.x) * (count // 2), 128), count // 2)
                pair = full.at[z, :, p.c, :, other]
                self.swapped.append(copy(pair, pair, 19 + k, sibling))

    def start_z(self):
        for copy in self.z:
            copy.start()
        p = self.place
        self.full[p.z, p.y, p.c, :, self.part] = self.own[:, self.part]
        self.y[0].start()
        self.near[0].start()

    def start_y(self):
        for k, copy in enumerate(self.z):
            copy.wait_recv()
            self.y[k + 1].start()
            self.near[k + 1].start()

    def start_x(self):
        for arrived, copy, far in zip(self.y, self.x, self.far, strict=True):
            arrived.wait_recv()
            copy.start()
            far.start()

    def start_c(self):
        pairs = zip(self.x, self.swapped) if self.halved else zip(self.y, self.far)
        for arrived, copy in pairs:
            arrived.wait_recv()
            copy.start()

    def ready(self):
        for copy in self.near + self.far + self.swapped:
            copy.wait_recv()

    def close(self):
        for copy in self.z + self.y + self.x + self.near + self.far + self.swapped:
            copy.wait_send()


class Reduce:
    def __init__(self, r, place, index, grad, at=0):
        count, _, kind, halved = REDUCES[index]
        self.grad, self.place, self.kind, self.halved = grad, place, kind, halved
        p = place
        copy = remote(r.reduce_send, r.reduce_recv, index)
        self.cols = slice(at, at + count)
        self.buffers = [r.table[index, part] for part in range(len(reduce_leads(halved)))]
        sc, rc, ry, rz, rx = self.buffers[:5]
        keep = count
        self.part = self.cols
        self.lines = p.lines()
        if halved:
            keep = count // 2
            self.part = self.half(at, keep, p.x)
            self.away = self.half(at, keep, 1 - p.x)
            self.local, self.local_away = self.half(0, keep, p.x), self.half(0, keep, 1 - p.x)
            held = self.buffers[5]
            self.sx1 = sc.at[:, :, :, 0:keep]
            self.x1 = [
                copy(self.sx1.at[z], held.at[z], 12 + k, p.at(x=1 - p.x))
                for k, z in enumerate(self.lines)
            ]
        tail = slice(count - keep, count)
        self.sy = sc.at[:, 0, :, tail]
        self.sz = [sc.at[k, 1, :, tail] for k in range(3)]
        self.sx = sc.at[3, 1, :, tail]
        self.c, self.y = [], []
        for k, z in enumerate(self.lines):
            self.c.append(copy(sc.at[z], rc.at[z], k, p.at(c=1 - p.c)))
            self.y.append(copy(self.sy.at[z], ry.at[z], 4 + k, p.at(y=1 - p.y)))
        self.z = [copy(self.sz[k], rz.at[k], 8 + k, p.at(z=p.z_partner(k))) for k in range(3)]
        self.x = copy(self.sx, rx, 11, p.at(x=1 - p.x))

    @staticmethod
    def half(at, keep, x):
        return pl.ds(pl.multiple_of(at + x * keep, 128), keep)

    def add(self, index, values):
        total = self.grad[index].astype(F32) + values.astype(F32)
        self.grad[index] = total.astype(self.grad.dtype)

    def start_c(self):
        sc, p = self.buffers[0], self.place
        for z, copy in zip(self.lines, self.c, strict=True):
            sc[z] = self.grad[z, :, 1 - p.c, :, self.cols].astype(self.kind)
            copy.start()

    def start_x1(self, pieces=range(4)):
        rc, p = self.buffers[1], self.place
        for k in pieces:
            z = self.lines[k]
            self.c[k].wait()
            away = self.grad[z, :, p.c, :, self.away].astype(F32)
            away += rc[z, :, :, self.local_away].astype(F32)
            self.sx1[z] = away.astype(self.kind)
            self.x1[k].start()
            self.add((z, slice(None), p.c, slice(None), self.part), rc[z, :, :, self.local])

    def start_y(self, pieces=range(4)):
        p = self.place
        held = self.buffers[5 if self.halved else 1]
        for k in pieces:
            z = self.lines[k]
            if self.halved:
                self.x1[k].wait_recv()
            else:
                self.c[k].wait()
            away = self.grad[z, 1 - p.y, p.c, :, self.part].astype(F32)
            away += held[z, 1 - p.y].astype(F32)
            self.sy[z] = away.astype(self.kind)
            self.y[k].start()
            self.add((z, p.y, p.c, slice(None), self.part), held[z, p.y])

    def start_z(self, pieces=range(4)):
        ry, p = self.buffers[2], self.place
        for k in pieces:
            owner = self.lines[k]
            self.y[k].wait_recv()
            if k == 0:
                self.add((owner, p.y, p.c, slice(None), self.part), ry[owner])
                continue
            away = self.grad[owner, p.y, p.c, :, self.part].astype(F32) + ry[owner].astype(F32)
            self.sz[k - 1][...] = away.astype(self.kind)
            self.z[k - 1].start()

    def start_x(self):
        rz, p = self.buffers[3], self.place
        for copy in self.z:
            copy.wait_recv()
        near = self.grad[p.z, p.y, p.c, :, self.part].astype(F32) + rz[0].astype(F32)
        self.sx[...] = (near + (rz[1].astype(F32) + rz[2].astype(F32))).astype(self.kind)
        self.x.start()

    def finish(self, out):
        rx = self.buffers[4]
        self.x.wait_recv()
        if self.halved:
            out[:, self.part] = self.sx[...].astype(F32)
            out[:, self.away] = rx[...].astype(F32)
        else:
            out[:, self.cols] = self.sx[...].astype(F32) + rx[...].astype(F32)

    def close(self):
        for copy in self.z + self.y + [self.x] + (self.x1 if self.halved else []):
            copy.wait_send()


def reduce_leads(halved):
    leads = [((4, 2), False), ((4, 2), False), ((4,), halved), ((3,), halved), ((), halved)]
    return leads + ([((4, 2), True)] if halved else [])


def layer_scratch(row_count, width, hidden_width, shards):
    tile = 256
    seqs = row_count // LENGTH
    pairs = dict(
        active=((tile, hidden_width), BF16),
        slope=((tile, hidden_width), BF16),
        two_t=((width, tile), BF16),
        unit=((tile, width), F32),
        last=((tile, width), F32),
        scale=((tile, 1), F32),
    )
    both = {(name, side): item for name, item in pairs.items() for side in range(2)}
    return both | dict(
        tokens=((row_count, width), BF16),
        middle_grad=((row_count, width), F32),
        normed_t=((width, row_count), BF16),
        qkv=((row_count, 3 * width), BF16),
        attended=((row_count, width), BF16),
        totals=((seqs, width), F32),
        causal=((LENGTH, WIDE), F32),
        advantage=((1, row_count), F32),
        action_row=((1, row_count), jnp.int32),
        two_low=((tile, width), BF16),
        low=((tile, width), BF16),
        low_t=((width, tile), BF16),
        two_in=((tile, width), F32),
        hidden_grad=((tile, hidden_width // 4), BF16),
        local_sem=pltpu.SemaphoreType.DMA((2,)),
    )


def grad_shapes(width, hidden_width, shards):
    split = SPLIT
    part, hidden_part = width // shards, hidden_width // shards
    return dict(
        g_qkv=(split + (part, 3 * width), BF16),
        g_out=(split + (part, width), F32),
        g_up=(split + (part, hidden_width), F32),
        g_down=(split + (width, hidden_part), F32),
        g_actor=((SLOTS, width), F32),
        g_small=((7, 8, width), F32),
        g_up_bias=((8, hidden_width), F32),
        g_positions=((LENGTH, width), F32),
        head_sums=((SLOTS + 8, 128), F32),
    )


def at_step(i, table):
    for step, actions in table.items():

        @pl.when(i == step)
        def _(actions=actions):
            for action in actions:
                action()


def spread_kernel(names, scale, *refs):
    r = Names(names, refs)
    place = Place()
    load = pltpu.make_async_copy(r.tokens_in, r.tokens, r.local_sem.at[0])
    load.start()
    partners = place.partners()
    barrier = pltpu.get_barrier_semaphore()
    for device in partners:
        pl.semaphore_signal(barrier, inc=1, device_id=device, device_id_type=MESH)
    pack_shards(r)
    pl.semaphore_wait(barrier, len(partners))
    width, hidden_width = r.w_out.shape[-1], r.w_up.shape[-1]
    plan = [(r.pack, r.pack_own, 0, 128)]
    plan += [(r.w_qkv, r.qkv_in, k * width, width) for k in range(3)]
    plan += [(r.w_out, r.out_in, 0, width)]
    half = hidden_width // 2
    plan += [(r.w_up, r.up_in, k * half, half, True) for k in range(2)]
    plan += [(r.w_down, r.down_in, k * width // 2, width // 2, True) for k in range(2)]
    gathers = [Gather(r, place, k, *item) for k, item in enumerate(plan)]
    pack, q, k, v, out, up0, up1, down0, down1 = gathers
    pack.start_z()
    q.start_z()
    k.start_z()
    v.start_z()
    pack.start_y()
    q.start_y()
    pack.start_c()
    for group in (out, up0, up1, down0, down1):
        group.start_z()
    frame_values(r)
    k.start_y()
    pack.ready()
    unpack_shards(r)
    v.start_y()
    q.start_c()
    load.wait()
    norm_pass(r)
    k.start_c()
    v.start_c()
    q.ready()
    project_third(r, 0)
    clear(r)
    k.ready()
    project_third(r, 1)
    v.ready()
    project_third(r, 2)

    front(
        r,
        lambda i: at_step(
            i,
            {
                1: [out.start_y],
                3: [up0.start_y, out.start_c],
                5: [up1.start_y, up0.start_x],
                7: [down0.start_y, up1.start_x, up0.start_c],
                9: [down1.start_y, down0.start_x, up1.start_c],
            },
        ),
    )
    out.ready()

    def arrive():
        down1.start_x()
        down0.start_c()
        down1.start_c()
        for group in (up0, up1, down0, down1):
            group.ready()

    middle_part(r, scale, arrive)

    plan = [(r.g_down,), (r.g_up,), (r.g_out,)]
    plan += [(r.g_qkv, k * width) for k in range(3)] + [(r.g_pack,)]
    reduces = [Reduce(r, place, k, *item) for k, item in enumerate(plan)]
    down, up, out, q, k, v, pack = reduces
    down.start_c()
    up.start_c()
    out.start_c()
    attend_back(
        r,
        lambda i: at_step(
            i,
            {
                1: [down.start_y],
                2: [up.start_x1],
                3: [out.start_x1],
                7: [lambda: up.start_y([0])],
                9: [lambda: down.start_z([0, 1]), lambda: up.start_y([1])],
            },
        ),
    )
    qkv_weight_grad(r, 0)
    q.start_c()
    down.start_z([2])
    up.start_y([2])
    qkv_weight_grad(r, 2)
    v.start_c()
    q.start_y()
    down.start_z([3])
    up.start_y([3])
    qkv_weight_grad(r, 1)
    k.start_c()
    v.start_x1()
    k.start_y()

    def stored(i):
        rows = pl.ds(pl.multiple_of(i * 4 * LENGTH, 4 * LENGTH), 4 * LENGTH)
        return pltpu.make_async_copy(
            r.attended.at[rows, :], r.tokens_grad.at[rows, :], r.store_sem.at[i]
        )

    start_back(
        r,
        lambda i: at_step(
            i,
            {
                1: [out.start_y],
                3: [up.start_z],
                4: [v.start_y],
                5: [q.start_z],
                6: [out.start_z],
                8: [down.start_x],
                9: [k.start_z],
            },
        ),
        lambda i: stored(i).start(),
    )
    pack_grads(r)
    pack.start_c()
    v.start_z()
    q.start_x()
    pack.start_y()
    up.start_x()
    out.start_x()
    k.start_x()
    pack.start_z()
    v.start_x()
    down.finish(r.down_out)
    pack.start_x()
    up.finish(r.up_out)
    out.finish(r.out_out)
    for group in (q, k, v):
        group.finish(r.qkv_out)
    for i in range(r.middle_grad.shape[0] // (4 * LENGTH)):
        stored(i).wait()
    for group in gathers + reduces:
        group.close()
    pack.finish(r.pack_out)


def finish_kernel(names, count, *refs):
    r = Names(names, refs)
    step = 4 * LENGTH
    parts = [pl.ds(at, step) for at in range(0, r.tokens.shape[0], step)]
    loads = [
        pltpu.make_async_copy(r.tokens.at[part, :], r.held.at[part, :], r.load_sem.at[k])
        for k, part in enumerate(parts)
    ]
    stores = [
        pltpu.make_async_copy(r.wide.at[part, :], r.o_tokens.at[part, :], r.store_sem.at[k])
        for k, part in enumerate(parts)
    ]
    for load in loads:
        load.start()
    r.o_qkv[...] = r.qkv[...]
    r.o_out[...] = r.out[...]
    r.o_up[...] = r.up[...]
    r.o_down[...] = r.down[...].T
    r.o_stats[...] = DECAY_RATE * r.running[...] + (1.0 - DECAY_RATE) * r.percentiles[...]
    part, positions = r.o_positions.shape
    slots = r.o_actor.shape[0]
    features = r.pack[0:part, :]
    r.o_positions[...] = features[:, POSITION_AT : POSITION_AT + positions]
    turned = features.T
    vectors = (r.gain1, r.bias1, r.gain2, r.bias2, r.bias_down, r.gain3, r.bias3)
    for k, ref in enumerate(vectors):
        ref[...] = turned[SMALL_AT + k : SMALL_AT + k + 1, :].reshape(part)
    r.o_actor[...] = turned[SMALL_AT + 7 : SMALL_AT + 7 + slots, :]
    r.o_actor_bias[...] = turned[BIAS_AT : BIAS_AT + 1, :].reshape(part)[0:slots]
    r.o_loss[...] = features[0:1, LOSS_AT : LOSS_AT + 1] * (1.0 / count)
    r.o_up_bias[...] = r.pack[part : part + 1, :].reshape(128)
    for part, load, store in zip(parts, loads, stores, strict=True):
        load.wait()
        r.wide[part, :] = r.held[part, :].astype(F32)
        store.start()
    for store in stores:
        store.wait()


def local_kernel(names, scale, *refs):
    r = Names(names, refs)
    load = pltpu.make_async_copy(r.tokens_in, r.tokens, r.local_sem.at[0])
    load.start()
    clear(r)
    frame_values(r)
    load.wait()
    norm_pass(r)
    for third in range(3):
        project_third(r, third)
    front(r, lambda i: None)
    middle_part(r, scale, lambda: None)
    attend_back(r, lambda i: None)
    for third in range(3):
        qkv_weight_grad(r, third)
    start_back(r, lambda i: None, lambda i: None)
    store = pltpu.make_async_copy(r.attended, r.tokens_grad, r.local_sem.at[1])
    store.start()
    store.wait()


def run(kernel, constant, ins, outs, scratch, flops=0, side_effects=False, collective=None):
    vmem = pl.BlockSpec(memory_space=pltpu.VMEM)
    anywhere = pl.BlockSpec(memory_space=pl.ANY)
    in_specs = [anywhere if array.size > LARGE else vmem for array in ins.values()]
    out_specs = [anywhere if math.prod(shape) > LARGE else vmem for shape, _ in outs.values()]
    return pl.pallas_call(
        functools.partial(kernel, (*ins, *outs, *scratch), constant),
        out_shape=[jax.ShapeDtypeStruct(shape, kind) for shape, kind in outs.values()],
        in_specs=in_specs,
        out_specs=out_specs,
        scratch_shapes=[
            item if not isinstance(item, tuple) else pltpu.VMEM(item[0], item[1])
            for item in scratch.values()
        ],
        compiler_params=pltpu.CompilerParams(
            vmem_limit_bytes=VMEM_BYTES, has_side_effects=side_effects, collective_id=collective
        ),
        cost_estimate=pl.CostEstimate(flops=flops, bytes_accessed=1 << 24, transcendentals=0),
    )(*ins.values())


def on_device(
    tokens,
    positions,
    norm_one_gain,
    norm_one_bias,
    qkv_weight,
    out_weight,
    norm_two_gain,
    norm_two_bias,
    up_weight,
    up_bias,
    down_weight,
    down_bias,
    final_gain,
    final_bias,
    actor_weight,
    actor_bias,
    actions,
    action_masks,
    game_ids,
    returns,
    values,
    running,
    percentiles,
):
    row_count, width = tokens.shape
    seq_count = row_count // LENGTH
    hidden_width = up_weight.shape[1]
    slots = actor_weight.shape[1]
    fsdp = lax.axis_size("fsdp")
    device_count = lax.axis_size("dp") * fsdp
    token_total = row_count * device_count
    scale = float(seq_count * device_count) / token_total
    flops = 6 * row_count * width * (4 * width + 2 * hidden_width)
    part, hidden_part = width // fsdp, hidden_width // fsdp

    vectors = dict(
        gain1=norm_one_gain,
        bias1=norm_one_bias,
        gain2=norm_two_gain,
        bias2=norm_two_bias,
        bias_down=down_bias,
        gain3=final_gain,
        bias3=final_bias,
    )
    stats = dict(running=running, percentiles=percentiles)
    frames = stats | dict(
        tokens_in=tokens,
        actor_bias=actor_bias,
        actions=actions,
        masks=action_masks.T,
        game_ids=game_ids,
        returns=returns,
        values=values,
    )
    scratch = layer_scratch(row_count, width, hidden_width, 16)
    grads = grad_shapes(width, hidden_width, 16)
    weight_shapes = dict(
        w_qkv=(SPLIT + (width // 16, 3 * width), BF16),
        w_out=(SPLIT + (width // 16, width), BF16),
        w_up=(SPLIT + (width // 16, hidden_width), BF16),
        w_down=(SPLIT + (hidden_width // 16, width), BF16),
    )

    if fsdp == 16 and lax.axis_size("dp") == 2:
        ins = frames | vectors
        ins |= dict(qkv_in=qkv_weight, out_in=out_weight, up_in=up_weight, down_in=down_weight)
        ins |= dict(up_bias_in=up_bias, positions_in=positions.T, actor_in=actor_weight.T)
        shard_grads = dict(
            qkv_out=((part, 3 * width), F32),
            out_out=((part, width), F32),
            up_out=((part, hidden_width), F32),
            down_out=((width, hidden_part), F32),
        )
        outs = dict(
            tokens_grad=((row_count, width), BF16), pack_out=((PACK_GRAD_ROWS, 128), F32)
        )
        scratch |= grads | weight_shapes
        scratch |= dict(
            pack=(SPLIT + (PACK_ROWS, 128), BF16),
            pack_own=((PACK_ROWS, 128), BF16),
            g_pack=(SPLIT + (PACK_GRAD_ROWS, 128), F32),
            positions=((LENGTH, width), F32),
            small=((8, width), F32),
            actor=((SLOTS, width), BF16),
            up_bias=((1, hidden_width), F32),
            gather_send=pltpu.SemaphoreType.DMA((GATHERS, 23)),
            gather_recv=pltpu.SemaphoreType.DMA((GATHERS, 23)),
            reduce_send=pltpu.SemaphoreType.DMA((len(REDUCES), 16)),
            reduce_recv=pltpu.SemaphoreType.DMA((len(REDUCES), 16)),
            store_sem=pltpu.SemaphoreType.DMA((row_count // (4 * LENGTH),)),
        )
        for index, (count, rows, kind, halved) in enumerate(REDUCES):
            for item, (lead, half) in enumerate(reduce_leads(halved)):
                scratch[index, item] = (lead + (rows, count // 2 if half else count), kind)
        tokens_grad, pack, qkv_g, out_g, up_g, down_g = run(
            spread_kernel, scale, ins, outs | shard_grads, scratch, flops, True, 0
        )
        vector = ((part,), F32)
        final = dict(
            o_loss=((1, 1), F32),
            o_stats=(running.shape, F32),
            o_positions=((part, LENGTH), F32),
            o_qkv=shard_grads["qkv_out"],
            o_out=shard_grads["out_out"],
            o_up=shard_grads["up_out"],
            o_down=((hidden_part, width), F32),
            o_up_bias=((hidden_part,), F32),
            o_actor=((slots, part), F32),
            o_actor_bias=((slots,), F32),
            o_tokens=((row_count, width), F32),
        )
        copies = pltpu.SemaphoreType.DMA((row_count // (4 * LENGTH),))
        done = run(
            finish_kernel,
            token_total,
            stats
            | dict(pack=pack, qkv=qkv_g, out=out_g, up=up_g, down=down_g, tokens=tokens_grad),
            final | dict.fromkeys(vectors, vector),
            dict(
                held=((row_count, width), BF16),
                wide=((row_count, width), F32),
                load_sem=copies,
                store_sem=copies,
            ),
        )
        loss, new_stats, pos_g, qkv_g, out_g, up_g, down_g = done[:7]
        up_bias_g, actor_g, actor_bias_g, tokens_grad = done[7:11]
        gain1, bias1, gain2, bias2, bias_down, gain3, bias3 = done[11:]
        return (
            loss.reshape(()),
            new_stats,
            tokens_grad,
            pos_g.T,
            gain1,
            bias1,
            qkv_g,
            out_g,
            gain2,
            bias2,
            up_g,
            up_bias_g,
            down_g,
            bias_down,
            gain3,
            bias3,
            actor_g.T,
            actor_bias_g,
        )

    def gather(array, axis):
        return lax.all_gather(array, "fsdp", axis=axis, tiled=True)

    packed = gather(
        jnp.concatenate([jnp.stack(list(vectors.values())), actor_weight.T, positions], 0), 1
    )
    fulls = [gather(weight, 0) for weight in (qkv_weight, out_weight, up_weight, down_weight)]
    ins = frames | {
        name: full.reshape(weight_shapes[name][0])
        for name, full in zip(weight_shapes, fulls, strict=True)
    }
    ins |= dict(
        positions=packed[7 + slots :].astype(F32),
        small=jnp.pad(packed[0:7].astype(F32), ((0, 1), (0, 0))),
        actor=jnp.pad(packed[7 : 7 + slots], ((0, SLOTS - slots), (0, 0))),
        up_bias=gather(up_bias, 0).astype(F32).reshape(1, hidden_width),
    )
    outs = dict(tokens_grad=((row_count, width), BF16)) | grads
    tokens_grad, *sums = run(local_kernel, scale, ins, outs, scratch, flops)
    sums = Names(grads, sums)

    def scatter(array, axis):
        piece = lax.psum_scatter(array, "fsdp", scatter_dimension=axis, tiled=True)
        return lax.psum(piece.astype(BF16), "dp").astype(F32)

    down_sum = jnp.swapaxes(sums.g_down, 3, 4)
    qkv_part, out_part, up_part, down_part = (
        scatter(merged(grad).astype(F32), 0)
        for grad in (sums.g_qkv, sums.g_out, sums.g_up, down_sum)
    )
    rows = [jnp.sum(sums.g_small, 1), sums.g_actor[:slots], sums.g_positions]
    side = scatter(jnp.concatenate(rows, 0), 1)
    up_bias_part = scatter(jnp.sum(sums.g_up_bias, 0), 0)
    head_total = lax.psum(jnp.sum(sums.head_sums[: SLOTS + 1], 1), ("dp", "fsdp"))
    return (
        head_total[SLOTS] / token_total,
        DECAY_RATE * running + (1.0 - DECAY_RATE) * percentiles,
        tokens_grad.astype(F32),
        side[7 + slots :],
        side[G1],
        side[B1],
        qkv_part,
        out_part,
        side[G2],
        side[B2],
        up_part,
        up_bias_part,
        down_part,
        side[DB],
        side[GL],
        side[BL],
        side[7 : 7 + slots].T,
        head_total[:slots],
    )


def solution(mesh):
    rows, cols, both = P(("dp", "fsdp"), None), P(None, "fsdp"), P(("dp", "fsdp"))
    weight, vector, whole = P("fsdp", None), P("fsdp"), P()
    in_specs = (rows, cols, vector, vector, weight, weight, vector, vector, weight, vector)
    in_specs += (weight, vector, vector, vector, weight, whole, both, rows, both, both, both)
    in_specs += (whole, whole)
    out_specs = (whole, whole, rows, cols, vector, vector, weight, weight, vector, vector)
    out_specs += (weight, vector, weight, vector, vector, vector, weight, whole)
    return jax.shard_map(
        on_device, mesh=mesh, in_specs=in_specs, out_specs=out_specs, check_vma=False
    )
```
